512 devices in a mesh: sample: 16 (over z_hi, y, core), context: 32 (over z_lo, x).
Axes of the slice: x: 4, y: 4, z: 16 (z_hi: 2, z_lo: 8; z = z_hi * 8 + z_lo), core: 2. Of those that a mesh axis runs over, the one named last changes fastest.
Arguments:
- hidden_in: bfloat16 [3, 32, 16, 4608], P(None, 'context', 'sample'), may hold values from -6 to 6
- pre_gain: bfloat16 [4608], replicated, may hold values from 0.099609375 to 1.8984375
- post_gain: bfloat16 [4608], replicated, may hold values from 0.099609375 to 1.8984375
- w_query: bfloat16 [4608, 4096], P('context', 'sample'), may hold values from -0.09375 to 0.09375
- key_projection_weight: bfloat16 [4608, 2048], P('context', 'sample'), may hold values from -0.09375 to 0.09375
- value_projection_weight: bfloat16 [4608, 2048], P('context', 'sample'), may hold values from -0.09375 to 0.09375
- w_out: bfloat16 [4096, 4608], P('sample'), may hold values from -0.09375 to 0.09375
- prompt_rotated_keys: bfloat16 [32768, 2048], P('context', 'sample'), may hold values from -18 to 18
- prompt_value_rows: bfloat16 [32768, 2048], P('context', 'sample'), may hold values from -6 to 6
- suffix_key_cache: bfloat16 [32, 16, 128, 2048], P('context', None, None, 'sample'), may hold values from -18 to 18
- suffix_value_cache: bfloat16 [32, 16, 128, 2048], P('context', None, None, 'sample'), may hold values from -6 to 6
- parents: int32 [3, 32, 16], P(None, 'context'), may hold values from 0 to 15
- lengths: int32 [32], replicated, may hold values from 1 to 125, as said below
Outputs:
- hidden_out: float32 [3, 32, 16, 4608], P(None, 'context', 'sample')
- keys_out: bfloat16 [32, 16, 128, 2048], P('context', None, None, 'sample')
- values_out: bfloat16 [32, 16, 128, 2048], P('context', None, None, 'sample')
The draws below stay inside these ranges and needn't reach their ends.
Inputs may be any that keep to these rules, and one draw needn't show every extreme that they name: `lengths`: some request has exactly 125 valid slots. parents[t] refer to the beams as reordered by the earlier steps.
All inputs are finite; a program needn't handle non-finite values.
Results may differ from the reference program's by a relative error of at most 0.012.
Values may be sent and summed in bfloat16 or wider, within the bound.
A program may use at most 64 MiB of HBM per device.

```python
import jax
import jax.numpy as jnp
from jax import lax

MODEL_WIDTH = 4608
QUERY_HEADS = 32
KEY_VALUE_HEADS = 16
HEAD_SIZE = 128
SUFFIX_SLOTS = 128
STEPS = 3
REQUEST_COUNT = 32
BEAM_WIDTH = 16
PROMPT_LENGTH = 32768


def draw_lengths(key, part):
    key = jax.random.fold_in(key, 11)
    lower_key, upper_key = jax.random.split(key)
    drawn = jax.random.randint(lower_key, (REQUEST_COUNT,), 1, SUFFIX_SLOTS - STEPS + 1)
    chosen = jax.random.randint(upper_key, (), 0, REQUEST_COUNT)
    return jnp.where(jnp.arange(REQUEST_COUNT) == chosen, SUFFIX_SLOTS - STEPS, drawn).astype(jnp.int32)


def with_ends(array, stream_key, least, largest):
    extent = array.shape
    index_at = [jax.random.randint(jax.random.fold_in(stream_key, axis), (), 0, extent[axis]) for axis in range(len(extent))]
    array = array.at[tuple(index_at)].set(least)
    longest = extent.index(max(extent))
    index_at[longest] = (index_at[longest] + 1) % extent[longest]
    return array.at[tuple(index_at)].set(largest)


def steps_of(own_key, dims, shards, low, top_value):
    loudness = 1.0
    for position, shards_of in shards:
        steps = jax.random.uniform(jax.random.fold_in(jax.random.fold_in(own_key, 6), position), (shards_of,), jnp.float32, low / len(shards), top_value / len(shards))
        loudness = loudness * jnp.repeat(jnp.exp(steps), dims[position] // shards_of).reshape((-1,) + (1,) * (len(dims) - 1 - position))
    return loudness


def gaussian(own_key, shape, spread, limit, shards=(), kind=jnp.bfloat16):
    array = jax.random.normal(own_key, shape, jnp.float32) * spread
    if len(shards) > 0:
        array = steps_of(own_key, shape, shards, -0.22, 0.18) * array
    return jnp.clip(array, min=-limit, max=limit).astype(kind)


def setup_inputs(seed: int = 0) -> dict:
    keys = jax.random.split(jax.random.key(seed), 14)
    hidden_in = gaussian(keys[0], (STEPS, REQUEST_COUNT, BEAM_WIDTH, MODEL_WIDTH), 1.0, 6.0, ((1, 32), (2, 16)))
    pre_gain = jnp.clip(1.0 + 0.18 * jax.random.normal(keys[1], (MODEL_WIDTH,), jnp.float32), 0.099609375, 1.8984375).astype(jnp.bfloat16)
    post_gain = jnp.clip(1.0 + 0.18 * jax.random.normal(keys[2], (MODEL_WIDTH,), jnp.float32), 0.099609375, 1.8984375).astype(jnp.bfloat16)
    w_query = gaussian(keys[3], (MODEL_WIDTH, QUERY_HEADS * HEAD_SIZE), MODEL_WIDTH ** -0.5, 0.09375, ((0, 32), (1, 16)))
    key_projection_weight = gaussian(keys[4], (MODEL_WIDTH, KEY_VALUE_HEADS * HEAD_SIZE), MODEL_WIDTH ** -0.5, 0.09375, ((0, 32), (1, 16)))
    value_projection_weight = gaussian(keys[5], (MODEL_WIDTH, KEY_VALUE_HEADS * HEAD_SIZE), MODEL_WIDTH ** -0.5, 0.09375, ((0, 32), (1, 16)))
    w_out = gaussian(keys[6], (QUERY_HEADS * HEAD_SIZE, MODEL_WIDTH), (QUERY_HEADS * HEAD_SIZE) ** -0.5, 0.09375, ((0, 16),))
    prompt_rotated_keys = gaussian(keys[7], (PROMPT_LENGTH, KEY_VALUE_HEADS * HEAD_SIZE), 3.0, 18.0, ((0, 32), (1, 16)))
    prompt_value_rows = gaussian(keys[8], (PROMPT_LENGTH, KEY_VALUE_HEADS * HEAD_SIZE), 1.0, 6.0, ((0, 32), (1, 16)))
    suffix_key_cache = gaussian(keys[9], (REQUEST_COUNT, BEAM_WIDTH, SUFFIX_SLOTS, KEY_VALUE_HEADS * HEAD_SIZE), 3.0, 18.0, ((0, 32), (3, 16)))
    suffix_value_cache = gaussian(keys[10], (REQUEST_COUNT, BEAM_WIDTH, SUFFIX_SLOTS, KEY_VALUE_HEADS * HEAD_SIZE), 1.0, 6.0, ((0, 32), (3, 16)))
    parents = with_ends(jax.random.randint(keys[11], (STEPS, REQUEST_COUNT, BEAM_WIDTH), 0, BEAM_WIDTH), jax.random.fold_in(keys[11], 1), 0, BEAM_WIDTH - 1).astype(jnp.int32)
    lengths = draw_lengths(jax.random.fold_in(keys[13], 71), 0)
    return {"hidden_in": hidden_in, "pre_gain": pre_gain, "post_gain": post_gain, "w_query": w_query, "key_projection_weight": key_projection_weight, "value_projection_weight": value_projection_weight, "w_out": w_out, "prompt_rotated_keys": prompt_rotated_keys, "prompt_value_rows": prompt_value_rows, "suffix_key_cache": suffix_key_cache, "suffix_value_cache": suffix_value_cache, "parents": parents, "lengths": lengths}


epsilon = 1e-06
query_scale = 144.0 ** (-0.5)
rope_base = 10000.0
logit_cap = 50.0

def apply_pair_rotation(vectors, decode_position):
    half_dim = vectors.shape[-1] // 2
    frequency = rope_base ** (-2.0 * jnp.arange(half_dim, dtype=jnp.float32) / vectors.shape[-1])
    angles = decode_position.astype(jnp.float32)[..., None, None] * frequency
    cosine = jnp.cos(angles)
    sine = jnp.sin(angles)
    lower_half = vectors[..., :half_dim]
    upper_half = vectors[..., half_dim:]
    return jnp.concatenate([lower_half * cosine - upper_half * sine, upper_half * cosine + lower_half * sine], axis=-1)

def soft_cap(scores):
    return logit_cap * jnp.tanh(scores / logit_cap)

def reference(hidden_in, pre_gain, post_gain, w_query, key_projection_weight, value_projection_weight, w_out, prompt_rotated_keys, prompt_value_rows, suffix_key_cache, suffix_value_cache, parents, lengths):
    query_group_width = QUERY_HEADS // KEY_VALUE_HEADS
    keys_cache = suffix_key_cache
    values_cache = suffix_value_cache
    slot_index = jnp.arange(SUFFIX_SLOTS, dtype=jnp.int32)
    per_head_keys = jnp.moveaxis(prompt_rotated_keys.reshape(PROMPT_LENGTH, KEY_VALUE_HEADS, HEAD_SIZE), 1, 0)
    per_head_values = jnp.moveaxis(prompt_value_rows.reshape(PROMPT_LENGTH, KEY_VALUE_HEADS, HEAD_SIZE), 1, 0)
    results = []
    for step_index in range(STEPS):
        rows_float = hidden_in[step_index].astype(jnp.float32)
        mean_square = lax.optimization_barrier(jnp.mean(rows_float * rows_float, axis=-1, keepdims=True))
        normed = (rows_float * lax.rsqrt(mean_square + epsilon) * pre_gain.astype(jnp.float32)).astype(jnp.bfloat16)
        flattened_rows = normed.reshape(REQUEST_COUNT * BEAM_WIDTH, MODEL_WIDTH)
        query_raw = jnp.dot(flattened_rows, w_query, preferred_element_type=jnp.float32).reshape(REQUEST_COUNT, BEAM_WIDTH, QUERY_HEADS, HEAD_SIZE)
        unrotated_key = jnp.dot(flattened_rows, key_projection_weight, preferred_element_type=jnp.float32).reshape(REQUEST_COUNT, BEAM_WIDTH, KEY_VALUE_HEADS, HEAD_SIZE)
        projected_value = jnp.dot(flattened_rows, value_projection_weight, preferred_element_type=jnp.float32).reshape(REQUEST_COUNT, BEAM_WIDTH, KEY_VALUE_HEADS * HEAD_SIZE)
        decode_position = (PROMPT_LENGTH + lengths + step_index)[:, None]
        query_rows = (apply_pair_rotation(query_raw, decode_position) * query_scale).astype(jnp.bfloat16)
        fresh_rotated_keys = apply_pair_rotation(unrotated_key, decode_position).astype(jnp.bfloat16).reshape(REQUEST_COUNT, BEAM_WIDTH, KEY_VALUE_HEADS * HEAD_SIZE)
        new_values = projected_value.astype(jnp.bfloat16)
        ancestors = parents[step_index][:, :, None, None]
        keys_cache = jnp.take_along_axis(keys_cache, ancestors, axis=1)
        values_cache = jnp.take_along_axis(values_cache, ancestors, axis=1)
        write_slot = lengths + step_index
        at_slot = (slot_index[None, :] == write_slot[:, None])[:, None, :, None]
        keys_cache = jnp.where(at_slot, fresh_rotated_keys[:, :, None, :], keys_cache)
        values_cache = jnp.where(at_slot, new_values[:, :, None, :], values_cache)
        grouped_queries = query_rows.reshape(REQUEST_COUNT, BEAM_WIDTH, KEY_VALUE_HEADS, query_group_width, HEAD_SIZE)
        head_queries = jnp.moveaxis(grouped_queries, 2, 0)

        def per_head(operands):
            head_query, head_key, head_value = operands
            scores = jnp.einsum('rbeh,ph->rbep', head_query.astype(jnp.float32), head_key.astype(jnp.float32))
            weights = jnp.exp(soft_cap(scores))
            rounded = lax.optimization_barrier(weights.astype(jnp.bfloat16)).astype(jnp.float32)
            weighted = jnp.einsum('rbep,ph->rbeh', rounded, head_value.astype(jnp.float32))
            return (weighted, lax.optimization_barrier(jnp.sum(weights, axis=-1)))
        prefix_weighted, prefix_totals = lax.map(per_head, (head_queries, per_head_keys, per_head_values))
        prefix_weighted = jnp.moveaxis(prefix_weighted, 0, 2)
        prefix_totals = jnp.moveaxis(prefix_totals, 0, 2)
        suffix_cache_shape = (REQUEST_COUNT, BEAM_WIDTH, SUFFIX_SLOTS, KEY_VALUE_HEADS, HEAD_SIZE)
        suffix_scores = jnp.einsum('rbgeh,rbjgh->rbgej', grouped_queries.astype(jnp.float32), keys_cache.reshape(suffix_cache_shape).astype(jnp.float32))
        visible = (slot_index[None, :] <= write_slot[:, None])[:, None, None, None, :]
        suffix_weights = jnp.where(visible, jnp.exp(soft_cap(suffix_scores)), 0.0)
        suffix_rounded = lax.optimization_barrier(suffix_weights.astype(jnp.bfloat16)).astype(jnp.float32)
        suffix_weighted = jnp.einsum('rbgej,rbjgh->rbgeh', suffix_rounded, values_cache.reshape(suffix_cache_shape).astype(jnp.float32))
        suffix_totals = lax.optimization_barrier(jnp.sum(suffix_weights, axis=-1))
        attended = ((prefix_weighted + suffix_weighted) / (prefix_totals + suffix_totals)[..., None]).astype(jnp.bfloat16)
        branch = jnp.dot(attended.reshape(REQUEST_COUNT * BEAM_WIDTH, QUERY_HEADS * HEAD_SIZE), w_out, preferred_element_type=jnp.float32)
        branch_square = lax.optimization_barrier(jnp.mean(branch * branch, axis=-1, keepdims=True))
        scaled = branch * lax.rsqrt(branch_square + epsilon) * post_gain.astype(jnp.float32)
        results.append(rows_float + scaled.reshape(REQUEST_COUNT, BEAM_WIDTH, MODEL_WIDTH))
    return (jnp.stack(results), keys_cache, values_cache)
```

```python
import functools

import jax
import jax.numpy as jnp
import numpy as np
from jax import lax
from jax.experimental import pallas as pl
from jax.experimental.pallas import tpu as pltpu
from jax.sharding import PartitionSpec as P

HEAD = 128
STEPS = 3
XN = 4
POS_TILE = 512

epsilon = 1e-06
query_scale = 144.0 ** (-0.5)
rope_base = 10000.0
logit_cap = 50.0
MESH = pl.DeviceIdType.MESH
F32 = jnp.float32
BF16 = jnp.bfloat16


def weights_of(scores):
    return jnp.exp(logit_cap * jnp.tanh(scores * (1.0 / logit_cap)))


def dot_t(a, b):
    return lax.dot_general(a, b, (((1,), (1,)), ((), ())), preferred_element_type=F32)


def dot(a, b):
    return jnp.dot(a, b, preferred_element_type=F32)


def kernel(
    dims, prompt_total,
    tiles, hid, gain, cos_rows, sin_rows, perm, wq, wk, wv, wout, pk, pv, kc, vc, par, lens,
    out_h, out_k, out_v,
    a1, a1f, xb, wf, wp, yf, sred, rred, g, gf, qa, kall, vall, acc, psend, precv,
    woutv, kcv, vcv, ancv, freshv, freshk, br, csend, crecv, s1, ysend, yrecv, zsend, zrecv,
    as_, ar, ws, wr, ks, kr, xs, xr, ys, yr, cs, cr, rs, rr, gs, gr, qs, qr, ps, pr,
    bcs, bcr, bys, byr, bzs, bzr, ls,
):
    ZH, YN, KN, ZL = dims
    ZN = ZH * ZL
    YK = YN * KN
    BEAMS = ZH * YK
    ROWS = STEPS * BEAMS
    s = lax.axis_index("sample")
    c = lax.axis_index("context")
    zh = lax.div(s, YK)
    y = lax.div(lax.rem(s, YK), KN)
    k = lax.rem(s, KN)
    zl = lax.div(c, XN)
    x = lax.rem(c, XN)
    z = zh * ZL + zl
    width = hid.shape[1]

    def at(zh_=None, y_=None, k_=None, zl_=None, x_=None):
        zh_ = zh if zh_ is None else zh_
        y_ = y if y_ is None else y_
        k_ = k if k_ is None else k_
        zl_ = zl if zl_ is None else zl_
        x_ = x if x_ is None else x_
        return {"sample": zh_ * YK + y_ * KN + k_, "context": zl_ * XN + x_}

    def rc(src, dst, ssem, rsem, where):
        return pltpu.make_async_remote_copy(
            src_ref=src, dst_ref=dst, send_sem=ssem, recv_sem=rsem,
            device_id=where, device_id_type=MESH,
        )

    def z_at(o):
        zz = lax.rem(z + o, ZN)
        return at(zh_=lax.div(zz, ZL), zl_=lax.rem(zz, ZL)), lax.rem(zz, ZL)

    peers = [z_at(o)[0] for o in range(1, ZN)]
    peers += [at(x_=lax.rem(x + o, XN)) for o in range(1, XN)]
    peers += [at(y_=lax.rem(y + o, YN)) for o in range(1, YN)]
    if KN > 1:
        peers += [at(k_=1 - k)]
    barrier = pltpu.get_barrier_semaphore()
    for peer in peers:
        pl.semaphore_signal(barrier, inc=1, device_id=peer, device_id_type=MESH)
    pl.semaphore_wait(barrier, len(peers))

    a_copies = []
    for o in range(1, ZN):
        where, zl_to = z_at(o)
        cp = rc(tiles.at[zl_to], a1.at[z], as_.at[o], ar.at[o], where)
        cp.start()
        a_copies.append(cp)

    half = wq.shape[1] // 2
    w_src = [wq.at[:, pl.ds(0, half)], wq.at[:, pl.ds(half, half)], wk, wv]

    def w_copy(to):
        return rc(w_src[to], wf.at[x], ws.at[to], wr.at[x], at(x_=to))

    def w_local(to):
        return pltpu.make_async_copy(w_src[to], wf.at[x], ls.at[0])

    for to in range(XN):
        @pl.when(x != to)
        def _():
            w_copy(to).start()

        @pl.when(x == to)
        def _():
            w_local(to).start()

    loc = [
        pltpu.make_async_copy(wout, woutv, ls.at[1]),
        pltpu.make_async_copy(kc, kcv, ls.at[2]),
        pltpu.make_async_copy(vc, vcv, ls.at[3]),
        pltpu.make_async_copy(pk, kall.at[x], ls.at[4]),
        pltpu.make_async_copy(pv, vall.at[x], ls.at[5]),
    ]
    for cp in loc:
        cp.start()

    a1[z] = tiles[zl]
    for cp in a_copies:
        cp.wait_recv()

    TJ = a1.shape[1]
    J = xb.shape[2] // 128
    for i in range(ZN):
        a1f[pl.ds(i * TJ, TJ), :] = a1[i].astype(F32)
    b_own = (x * YN + y) * KN + k
    for t in range(STEPS):
        for j in range(J):
            xb[b_own, pl.ds(t * ZN, ZN), pl.ds(j * 128, 128)] = a1f[
                pl.ds(t * J + j, ZN, stride=TJ), :
            ].astype(BF16)

    def blk(x_, y_, k_):
        return xb.at[(x_ * YN + y_) * KN + k_]

    sends = []

    def push(cp):
        cp.start()
        sends.append(cp)
        return cp

    x_copies = {}
    for o in (1, 3, 2):
        x_copies[o] = push(rc(blk(x, y, k), blk(x, y, k), xs.at[o], xr.at[o], at(x_=lax.rem(x + o, XN))))
    y_copies = {}
    c_copies = {}

    def from_x(ox):
        xo = lax.rem(x + XN - ox, XN)
        for oy in range(1, YN):
            y_copies[ox, oy] = push(
                rc(blk(xo, y, k), blk(xo, y, k), ys.at[ox, oy], yr.at[ox, oy], at(y_=lax.rem(y + oy, YN)))
            )
        to_core(ox, 0)

    def to_core(ox, oy):
        if KN == 1:
            return
        xo = lax.rem(x + XN - ox, XN)
        yo = lax.rem(y + YN - oy, YN)
        c_copies[ox, oy] = push(
            rc(blk(xo, yo, k), blk(xo, yo, k), cs.at[ox, oy], cr.at[ox, oy], at(k_=1 - k))
        )

    from_x(0)
    X_ORDER = (1, 3, 2)
    for ox in X_ORDER:
        x_copies[ox].wait_recv()
        from_x(ox)

    kv_copies = []
    for o in range(1, XN):
        to = at(x_=lax.rem(x + o, XN))
        kv_copies.append(push(rc(pk, kall.at[x], ks.at[0, o], kr.at[0, o], to)))
        kv_copies.append(push(rc(pv, vall.at[x], ks.at[1, o], kr.at[1, o], to)))

    for to in range(XN):
        @pl.when(x != to)
        def _():
            rc(w_src[to], wf.at[to], ws.at[to], wr.at[to], at(x_=to)).wait_recv()

        @pl.when(x == to)
        def _():
            w_local(to).wait()

    depth = XN * wf.shape[1]
    wp[pl.ds(0, depth), :] = wf[...].reshape(depth, HEAD)
    if wp.shape[0] > depth:
        wp[pl.ds(depth, wp.shape[0] - depth), :] = jnp.zeros((wp.shape[0] - depth, HEAD), BF16)

    GR = YK * STEPS * ZN
    r_copies = {}
    for ox in (0,) + X_ORDER:
        xo = lax.rem(x + XN - ox, XN)
        for oy in range(1, YN):
            y_copies[ox, oy].wait_recv()
            to_core(ox, oy)
        for oy in range(YN):
            if KN > 1:
                c_copies[ox, oy].wait_recv()
        xg = xb[pl.ds(xo * YK, YK)].reshape(GR, xb.shape[2])
        yf[...] = dot(xg, wp[...])
        for o in range(ZL):
            zo = lax.rem(zl + o, ZL)
            for t in range(STEPS):
                piece = jnp.concatenate(
                    [
                        yf[pl.ds(t * ZN + h * ZL + zo, YK, stride=STEPS * ZN), :]
                        for h in range(ZH)
                    ],
                    axis=0,
                )
                sred[ox, o, pl.ds(t * BEAMS, BEAMS), :] = piece.astype(BF16)
            if o > 0:
                r_copies[ox, o] = push(
                    rc(sred.at[ox, o], rred.at[ox, o], rs.at[ox, o], rr.at[ox, o], at(zl_=zo))
                )

    scale = jnp.where(x < 2, query_scale, 1.0).astype(F32)
    g_copies = {}
    for ox in (0,) + X_ORDER:
        xo = lax.rem(x + XN - ox, XN)
        total = sred[ox, 0].astype(F32)
        for o in range(1, ZL):
            r_copies[ox, o].wait_recv()
            total = total + rred[ox, o].astype(F32)
        for t in range(STEPS):
            part = total[t * BEAMS : (t + 1) * BEAMS]
            cosine = cos_rows[pl.ds(xo * STEPS + t, 1), :]
            sine = sin_rows[pl.ds(xo * STEPS + t, 1), :]
            turned = part * cosine + pltpu.roll(part, HEAD // 2, 1) * sine
            gf[ox, pl.ds(t * BEAMS, BEAMS), :] = (turned * scale).astype(BF16)
        if ox == 0:
            g[x] = gf[0]
        else:
            g_copies[ox] = push(rc(gf.at[ox], g.at[x], gs.at[ox], gr.at[ox], at(x_=xo)))
    for ox in X_ORDER:
        g_copies[ox].wait_recv()

    q_copies = []
    for o in range(1, ZL):
        q_copies.append(
            push(rc(g.at[pl.ds(0, 2)], qa.at[zl], qs.at[o], qr.at[o], at(zl_=lax.rem(zl + o, ZL))))
        )
    qa[zl] = g[0:2]

    length = lens[c]
    for cp in loc[1:3]:
        cp.wait()
    p0 = [par[0, b] for b in range(BEAMS)]
    p1 = [par[1, b] for b in range(BEAMS)]
    p2 = [par[2, b] for b in range(BEAMS)]
    first_of = [par[0, p1[b]] for b in range(BEAMS)]
    mid_of = [par[1, p2[b]] for b in range(BEAMS)]
    last_of = [par[0, mid_of[b]] for b in range(BEAMS)]
    never = jnp.int32(-1)
    for b in range(BEAMS):
        own = jnp.int32(b)
        chains = (
            (p0[b], own, never, never),
            (first_of[b], p1[b], own + BEAMS, never),
            (last_of[b], mid_of[b], p2[b] + BEAMS, own + 2 * BEAMS),
        )
        for t in range(STEPS):
            row = t * BEAMS + b
            ancv[pl.ds(row, 1), :] = jnp.full((1, 128), chains[t][0], jnp.int32)
            for u in range(STEPS):
                freshv[u, pl.ds(row, 1), :] = jnp.full((1, 128), chains[t][1 + u], jnp.int32)
    my_q = g[0:2].reshape(2 * ROWS, HEAD)
    SLOTS = kcv.shape[1]
    anc = ancv[:, :SLOTS]
    anc2 = jnp.concatenate([anc, anc], axis=0)
    slot = lax.broadcasted_iota(jnp.int32, (2 * ROWS, SLOTS), 1)
    lane = lax.broadcasted_iota(jnp.int32, (ROWS, ROWS), 1)
    seen = (lane == freshv[0, :, :ROWS]) | (lane == freshv[1, :, :ROWS]) | (lane == freshv[2, :, :ROWS])
    seen2 = jnp.concatenate([seen.astype(F32)] * 2, axis=0)
    fresh_w = weights_of(dot_t(my_q, g[2])) * seen2
    suf_w = dot(fresh_w.astype(BF16), g[3])
    suf_t = jnp.sum(fresh_w, axis=1, keepdims=True)
    for b in range(BEAMS):
        cached = weights_of(dot_t(my_q, kcv[b]))
        cached = jnp.where((anc2 == b) & (slot < length), cached, 0.0)
        suf_w = suf_w + dot(cached.astype(BF16), vcv[b])
        suf_t = suf_t + jnp.sum(cached, axis=1, keepdims=True)

    for src, cache, dst in ((2, kcv, out_k), (3, vcv, out_v)):
        freshk[...] = g[src].astype(F32)
        slots = lax.broadcasted_iota(jnp.int32, (SLOTS, HEAD), 0)
        for b in range(BEAMS):
            rows = [
                freshk[pl.ds(mid_of[b], 1), :],
                freshk[pl.ds(p2[b] + BEAMS, 1), :],
                freshk[pl.ds(b + 2 * BEAMS, 1), :],
            ]
            block = cache[last_of[b]].astype(F32)
            for u in range(STEPS):
                block = jnp.where(slots == length + u, rows[u], block)
            dst[b] = block.astype(BF16)

    for cp in loc[3:5]:
        cp.wait()
    for cp in kv_copies:
        cp.wait_recv()
    for cp in q_copies:
        cp.wait_recv()
    acc[...] = jnp.zeros_like(acc)
    per = kall.shape[1] // POS_TILE if kall.shape[1] >= POS_TILE else 1
    tile = kall.shape[1] // per

    def attend(i, carry):
        xi = lax.div(i, per)
        at_row = pl.multiple_of(lax.rem(i, per) * tile, tile)
        keys = kall[xi, pl.ds(at_row, tile), :]
        values = vall[xi, pl.ds(at_row, tile), :]
        queries = qa[...].reshape(ZL * 2 * ROWS, HEAD)
        w = weights_of(dot_t(queries, keys)).astype(BF16)
        wide = jnp.concatenate([values, jnp.ones((tile, HEAD), BF16)], axis=1)
        acc[...] += dot(w, wide)
        return carry

    lax.fori_loop(0, XN * per, attend, 0)

    QR = 2 * ROWS
    eye = lax.broadcasted_iota(jnp.int32, (QR, 128), 0) == lax.broadcasted_iota(jnp.int32, (QR, 128), 1)
    upper = lax.broadcasted_iota(jnp.int32, (16, 128), 0) < 8
    p_copies = []
    for o in range(ZL):
        zo = lax.rem(zl + o, ZL)
        at_row = pl.multiple_of(zo * QR, 8)
        psend[o, pl.ds(0, QR), :] = acc[pl.ds(at_row, QR), pl.ds(0, HEAD)].astype(BF16)
        totals = acc[pl.ds(at_row, QR), pl.ds(HEAD, HEAD)]
        line = jnp.sum(jnp.where(eye, totals, 0.0), axis=0, keepdims=True)
        coarse = line.astype(BF16).astype(F32)
        psend[o, pl.ds(QR, 16), :] = jnp.where(upper, coarse, line - coarse).astype(BF16)
        if o > 0:
            p_copies.append(push(rc(psend.at[o], precv.at[o], ps.at[o], pr.at[o], at(zl_=zo))))
    both = psend[0].astype(F32)
    for o in range(1, ZL):
        p_copies[o - 1].wait_recv()
        both = both + precv[o].astype(F32)
    line = both[QR : QR + 1] + both[QR + 8 : QR + 9]
    column = jnp.sum(jnp.where(eye, line, 0.0), axis=1, keepdims=True)
    attended = ((both[:QR] + suf_w) / (column + suf_t)).astype(BF16)
    heads = jnp.concatenate([attended[:ROWS], attended[ROWS:]], axis=1)

    loc[0].wait()
    ordered = dot(perm[...], heads).astype(BF16)
    GRP = 4 * ZH
    HALF = YN * GRP
    WC = width // 9 if width % 1152 == 0 and width > 1152 else width
    for i in range(width // WC):
        cols = pl.ds(i * WC, WC)
        res = dot(ordered, woutv[:, cols])
        for kk in range(KN):
            br[kk, :, cols] = res[kk * HALF : (kk + 1) * HALF]
    mine = br[k]
    if KN > 1:
        csend[...] = br[1 - k].astype(BF16)
        cp = push(rc(csend, crecv, bcs, bcr, at(k_=1 - k)))
        cp.wait_recv()
        mine = mine + crecv[...].astype(F32)
    for yy in range(YN):
        s1[yy] = mine[yy * GRP : (yy + 1) * GRP]
    hw = width // 2
    by_copies = []
    for o in range(1, YN):
        yo = lax.rem(y + o, YN)
        v = s1[yo]
        ysend[o] = jnp.concatenate([v[:, :hw], v[:, hw:]], axis=0).astype(BF16)
        by_copies.append(push(rc(ysend.at[o], yrecv.at[o], bys.at[o], byr.at[o], at(y_=yo))))
    total = s1[y]
    for o in range(1, YN):
        by_copies[o - 1].wait_recv()
        v = yrecv[o].astype(F32)
        total = total + jnp.concatenate([v[:GRP], v[GRP:]], axis=1)
    branch = total[0:4]
    if ZH > 1:
        qw = width // 4
        first = zh == 0
        other = jnp.where(first, total[4:8], total[0:4])
        zsend[...] = jnp.concatenate(
            [other[:, i * qw : (i + 1) * qw] for i in range(4)], axis=0
        ).astype(BF16)
        cp = push(rc(zsend, zrecv, bzs, bzr, at(zh_=1 - zh)))
        cp.wait_recv()
        v = zrecv[...].astype(F32)
        branch = jnp.where(first, total[0:4], total[4:8]) + jnp.concatenate(
            [v[i * 4 : (i + 1) * 4] for i in range(4)], axis=1
        )
    branch = branch[0:STEPS]
    square = jnp.mean(branch * branch, axis=-1, keepdims=True)
    scaled = branch * lax.rsqrt(square + epsilon) * gain[...].astype(F32)
    out_h[...] = hid[...].astype(F32) + scaled

    for cp in a_copies + sends:
        cp.wait_send()
    for to in range(XN):
        @pl.when(x != to)
        def _():
            w_copy(to).wait_send()


def order_matrix(dims):
    ZH, YN, KN, ZL = dims
    beams = ZH * YN * KN
    m = np.zeros((KN * YN * ZH * 4, STEPS * beams), np.float32)
    for kk in range(KN):
        for yy in range(YN):
            for hh in range(ZH):
                for t in range(STEPS):
                    m[((kk * YN + yy) * ZH + hh) * 4 + t, t * beams + (hh * YN + yy) * KN + kk] = 1.0
    return m


def body(
    dims,
    hidden_in,
    pre_gain,
    post_gain,
    w_query,
    key_projection_weight,
    value_projection_weight,
    w_out,
    prompt_rotated_keys,
    prompt_value_rows,
    suffix_key_cache,
    suffix_value_cache,
    parents,
    lengths,
):
    ZH, YN, KN, ZL = dims
    ZN = ZH * ZL
    YK = YN * KN
    beams = ZH * YK
    rows = STEPS * beams
    width = hidden_in.shape[3]
    slots = suffix_key_cache.shape[2]
    positions = prompt_rotated_keys.shape[0]
    prompt_total = positions * ZL * XN
    depth = width // ZL
    J = -(-depth // 128)
    TJ = -(-(STEPS * J) // 16) * 16
    hid = hidden_in.reshape(STEPS, width)
    rows_float = hid.astype(F32)
    mean_square = jnp.mean(rows_float * rows_float, axis=-1, keepdims=True)
    normed = (rows_float * lax.rsqrt(mean_square + epsilon) * pre_gain.astype(F32)).astype(BF16)
    tiles = jnp.pad(normed.reshape(STEPS, ZL, depth), ((0, 0), (0, 0), (0, J * 128 - depth)))
    tiles = tiles.reshape(STEPS, ZL, J, 128).transpose(1, 0, 2, 3).reshape(ZL, STEPS * J, 128)
    tiles = jnp.pad(tiles, ((0, 0), (0, TJ - STEPS * J), (0, 0)))

    at_context = lax.axis_index("context")
    own = lax.dynamic_slice_in_dim(lengths, at_context // XN * XN, XN)
    place = (prompt_total + own[:, None] + jnp.arange(STEPS, dtype=jnp.int32)[None, :]).reshape(-1, 1)
    frequency = rope_base ** (-2.0 * jnp.arange(HEAD // 2, dtype=F32) / HEAD)
    angles = place.astype(F32) * frequency
    is_value = at_context % XN == 3
    cosine = jnp.where(is_value, 1.0, jnp.cos(angles))
    sine = jnp.where(is_value, 0.0, jnp.sin(angles))
    cos_rows = jnp.concatenate([cosine, cosine], axis=1)
    sin_rows = jnp.concatenate([-sine, sine], axis=1)

    perm = jnp.asarray(order_matrix(dims), BF16)
    hbm = pl.BlockSpec(memory_space=pl.ANY)
    vmem = pl.BlockSpec(memory_space=pltpu.VMEM)
    smem = pl.BlockSpec(memory_space=pltpu.SMEM)
    wrows = w_query.shape[0]
    grp = 4 * ZH
    half = YN * grp
    V = pltpu.VMEM
    D = pltpu.SemaphoreType.DMA
    scratch = [
        V((ZN, TJ, 128), BF16),
        V((ZN * TJ, 128), F32),
        V((XN * YK, STEPS * ZN, J * 128), BF16),
        V((XN, wrows, HEAD), BF16),
        V((J * 128, HEAD), BF16),
        V((YK * STEPS * ZN, HEAD), F32),
        V((XN, ZL, rows, HEAD), BF16),
        V((XN, ZL, rows, HEAD), BF16),
        V((XN, rows, HEAD), BF16),
        V((XN, rows, HEAD), BF16),
        V((ZL, 2, rows, HEAD), BF16),
        V((XN, positions, HEAD), BF16),
        V((XN, positions, HEAD), BF16),
        V((ZL * 2 * rows, 2 * HEAD), F32),
        V((ZL, 2 * rows + 16, HEAD), BF16),
        V((ZL, 2 * rows + 16, HEAD), BF16),
        V(w_out.shape, BF16),
        V((beams, slots, HEAD), BF16),
        V((beams, slots, HEAD), BF16),
        V((rows, 128), jnp.int32),
        V((STEPS, rows, 128), jnp.int32),
        V((rows, HEAD), F32),
        V((KN, half, width), F32),
        V((half, width), BF16),
        V((half, width), BF16),
        V((YN, grp, width), F32),
        V((YN, 2 * grp, width // 2), BF16),
        V((YN, 2 * grp, width // 2), BF16),
        V((16, width // 4), BF16),
        V((16, width // 4), BF16),
        D((ZN,)), D((ZN,)), D((XN,)), D((XN,)), D((2, XN)), D((2, XN)), D((XN,)), D((XN,)),
        D((XN, YN)), D((XN, YN)), D((XN, YN)), D((XN, YN)), D((XN, ZL)), D((XN, ZL)),
        D((XN,)), D((XN,)), D((ZL,)), D((ZL,)), D((ZL,)), D((ZL,)),
        D, D, D((YN,)), D((YN,)), D, D, D((8,)),
    ]
    hidden_out, keys_out, values_out = pl.pallas_call(
        functools.partial(kernel, dims, prompt_total),
        out_shape=(
            jax.ShapeDtypeStruct((STEPS, width), F32),
            jax.ShapeDtypeStruct((beams, slots, HEAD), BF16),
            jax.ShapeDtypeStruct((beams, slots, HEAD), BF16),
        ),
        in_specs=[vmem] * 6 + [hbm] * 8 + [smem] * 2,
        out_specs=(vmem, vmem, vmem),
        scratch_shapes=scratch,
        compiler_params=pltpu.CompilerParams(
            collective_id=0, has_side_effects=True, vmem_limit_bytes=48 * 1024 * 1024
        ),
    )(
        tiles,
        hid,
        post_gain.reshape(1, width),
        cos_rows,
        sin_rows,
        perm,
        w_query,
        key_projection_weight,
        value_projection_weight,
        w_out,
        prompt_rotated_keys,
        prompt_value_rows,
        suffix_key_cache.reshape(beams, slots, HEAD),
        suffix_value_cache.reshape(beams, slots, HEAD),
        parents.reshape(STEPS, beams),
        lengths,
    )
    return (
        hidden_out.reshape(STEPS, 1, 1, width),
        keys_out.reshape(1, beams, slots, HEAD),
        values_out.reshape(1, beams, slots, HEAD),
    )


def solution(mesh, dims=(2, 4, 2, 8)):
    placed = (
        P(None, "context", "sample", None),
        P(),
        P(),
        P("context", "sample"),
        P("context", "sample"),
        P("context", "sample"),
        P("sample", None),
        P("context", "sample"),
        P("context", "sample"),
        P("context", None, None, "sample"),
        P("context", None, None, "sample"),
        P(None, "context", None),
        P(),
    )
    return jax.shard_map(
        functools.partial(body, dims),
        mesh=mesh,
        in_specs=placed,
        out_specs=(
            P(None, "context", "sample", None),
            P("context", None, None, "sample"),
            P("context", None, None, "sample"),
        ),
        check_vma=False,
    )
```

```python
import functools

import jax
import jax.numpy as jnp
import numpy as np
from jax import lax
from jax.experimental import pallas as pl
from jax.experimental.pallas import tpu as pltpu
from jax.sharding import PartitionSpec as P

HEAD = 128
STEPS = 3
XN = 4
POS_TILE = 512

epsilon = 1e-06
query_scale = 144.0 ** (-0.5)
rope_base = 10000.0
logit_cap = 50.0
TURN = 2 * np.pi
TURN_A = 6.28125
TURN_B = float(np.float32(np.round((TURN - TURN_A) * 2.0**20) / 2.0**20))
TURN_C = float(TURN - TURN_A - TURN_B)
MESH = pl.DeviceIdType.MESH
F32 = jnp.float32
BF16 = jnp.bfloat16


def weights_of(scores):
    return jnp.exp(logit_cap * jnp.tanh(scores * (1.0 / logit_cap)))


def dot_t(a, b):
    return lax.dot_general(a, b, (((1,), (1,)), ((), ())), preferred_element_type=F32)


def dot(a, b):
    return jnp.dot(a, b, preferred_element_type=F32)


def kernel(
    dims, prompt_total,
    hid, pre_gain, post_gain, freq, perm, wq, wk, wv, wout, pk, pv, kc, vc, par, lens,
    out_h, out_k, out_v,
    tiles, tilesf, cos_rows, sin_rows, a1, a1f, xb, wf, wp, yf, sred, rred, g, gf, qa, kall, vall, acc, psend, precv,
    woutv, kcv, vcv, ancv, freshv, freshk, br, csend, crecv, s1, ysend, yrecv, zsend, zrecv,
    as_, ar, ws, wr, ks, kr, xs, xr, ys, yr, cs, cr, rs, rr, gs, gr, qs, qr, ps, pr,
    bcs, bcr, bys, byr, bzs, bzr, ls,
):
    ZH, YN, KN, ZL = dims
    ZN = ZH * ZL
    YK = YN * KN
    BEAMS = ZH * YK
    ROWS = STEPS * BEAMS
    s = lax.axis_index("sample")
    c = lax.axis_index("context")
    zh = lax.div(s, YK)
    y = lax.div(lax.rem(s, YK), KN)
    k = lax.rem(s, KN)
    zl = lax.div(c, XN)
    x = lax.rem(c, XN)
    z = zh * ZL + zl
    width = hid.shape[1]

    def at(zh_=None, y_=None, k_=None, zl_=None, x_=None):
        zh_ = zh if zh_ is None else zh_
        y_ = y if y_ is None else y_
        k_ = k if k_ is None else k_
        zl_ = zl if zl_ is None else zl_
        x_ = x if x_ is None else x_
        return {"sample": zh_ * YK + y_ * KN + k_, "context": zl_ * XN + x_}

    def rc(src, dst, ssem, rsem, where):
        return pltpu.make_async_remote_copy(
            src_ref=src, dst_ref=dst, send_sem=ssem, recv_sem=rsem,
            device_id=where, device_id_type=MESH,
        )

    def z_at(o):
        zz = lax.rem(z + o, ZN)
        return at(zh_=lax.div(zz, ZL), zl_=lax.rem(zz, ZL)), lax.rem(zz, ZL)

    peers = [z_at(o)[0] for o in range(1, ZN)]
    peers += [at(x_=lax.rem(x + o, XN)) for o in range(1, XN)]
    peers += [at(y_=lax.rem(y + o, YN)) for o in range(1, YN)]
    if KN > 1:
        peers += [at(k_=1 - k)]
    barrier = pltpu.get_barrier_semaphore()
    for peer in peers:
        pl.semaphore_signal(barrier, inc=1, device_id=peer, device_id_type=MESH)

    part_width = width // ZL
    J = xb.shape[2] // 128
    TJ = a1.shape[1]
    hid_f = hid[...].astype(F32)
    gain_row = pre_gain[...].reshape(1, width).astype(F32)
    pieces = []
    for t in range(STEPS):
        row = hid_f[t : t + 1]
        mean_square = jnp.mean(row * row, axis=-1, keepdims=True)
        pieces.append(row * lax.rsqrt(mean_square + epsilon) * gain_row)
    rows3 = jnp.concatenate(pieces, axis=0)
    lane1 = lax.broadcasted_iota(jnp.int32, (STEPS, 128), 1)
    tilesf[...] = jnp.zeros_like(tilesf)
    for part in range(ZL):
        for j in range(J):
            start = part * part_width + j * 128
            got = min(128, (part + 1) * part_width - start)
            base = min(start, width - 128)
            shift = start - base
            seg = rows3[:, base : base + 128]
            if shift:
                seg = pltpu.roll(seg, 128 - shift, 1)
            if got < 128:
                seg = jnp.where(lane1 < got, seg, 0.0)
            tilesf[part, pl.ds(j * STEPS, STEPS), :] = seg
    tiles[...] = tilesf[...].astype(BF16)
    pl.semaphore_wait(barrier, len(peers))

    a_copies = []
    for o in range(1, ZN):
        where, zl_to = z_at(o)
        cp = rc(tiles.at[zl_to], a1.at[z], as_.at[o], ar.at[o], where)
        cp.start()
        a_copies.append(cp)

    half = wq.shape[1] // 2
    w_src = [wq.at[:, pl.ds(0, half)], wq.at[:, pl.ds(half, half)], wk, wv]

    def w_copy(to):
        return rc(w_src[to], wf.at[x], ws.at[to], wr.at[x], at(x_=to))

    def w_local(to):
        return pltpu.make_async_copy(w_src[to], wf.at[x], ls.at[0])

    for to in range(XN):
        @pl.when(x != to)
        def _():
            w_copy(to).start()

        @pl.when(x == to)
        def _():
            w_local(to).start()

    loc = [
        pltpu.make_async_copy(wout, woutv, ls.at[1]),
        pltpu.make_async_copy(kc, kcv, ls.at[2]),
        pltpu.make_async_copy(vc, vcv, ls.at[3]),
        pltpu.make_async_copy(pk, kall.at[x], ls.at[4]),
        pltpu.make_async_copy(pv, vall.at[x], ls.at[5]),
    ]
    for cp in loc:
        cp.start()

    a1[z] = tiles[zl]
    for cp in a_copies:
        cp.wait_recv()

    for i in range(ZN):
        a1f[pl.ds(i * TJ, TJ), :] = a1[i].astype(F32)
    b_own = (x * YN + y) * KN + k
    for t in range(STEPS):
        for j in range(J):
            xb[b_own, pl.ds(t * ZN, ZN), pl.ds(j * 128, 128)] = a1f[
                pl.ds(j * STEPS + t, ZN, stride=TJ), :
            ].astype(BF16)

    def blk(x_, y_, k_):
        return xb.at[(x_ * YN + y_) * KN + k_]

    sends = []

    def push(cp):
        cp.start()
        sends.append(cp)
        return cp

    x_copies = {}
    for o in (1, 3, 2):
        x_copies[o] = push(rc(blk(x, y, k), blk(x, y, k), xs.at[o], xr.at[o], at(x_=lax.rem(x + o, XN))))
    y_copies = {}
    c_copies = {}

    def from_x(ox):
        xo = lax.rem(x + XN - ox, XN)
        for oy in range(1, YN):
            y_copies[ox, oy] = push(
                rc(blk(xo, y, k), blk(xo, y, k), ys.at[ox, oy], yr.at[ox, oy], at(y_=lax.rem(y + oy, YN)))
            )
        to_core(ox, 0)

    def to_core(ox, oy):
        if KN == 1:
            return
        xo = lax.rem(x + XN - ox, XN)
        yo = lax.rem(y + YN - oy, YN)
        c_copies[ox, oy] = push(
            rc(blk(xo, yo, k), blk(xo, yo, k), cs.at[ox, oy], cr.at[ox, oy], at(k_=1 - k))
        )

    from_x(0)
    X_ORDER = (1, 3, 2)
    for ox in X_ORDER:
        x_copies[ox].wait_recv()
        from_x(ox)

    kv_copies = []
    for o in range(1, XN):
        to = at(x_=lax.rem(x + o, XN))
        kv_copies.append(push(rc(pk, kall.at[x], ks.at[0, o], kr.at[0, o], to)))
        kv_copies.append(push(rc(pv, vall.at[x], ks.at[1, o], kr.at[1, o], to)))

    for to in range(XN):
        @pl.when(x != to)
        def _():
            rc(w_src[to], wf.at[to], ws.at[to], wr.at[to], at(x_=to)).wait_recv()

        @pl.when(x == to)
        def _():
            w_local(to).wait()

    depth = XN * wf.shape[1]
    wp[pl.ds(0, depth), :] = wf[...].reshape(depth, HEAD)
    if wp.shape[0] > depth:
        wp[pl.ds(depth, wp.shape[0] - depth), :] = jnp.zeros((wp.shape[0] - depth, HEAD), BF16)

    GR = YK * STEPS * ZN
    r_copies = {}
    for ox in (0,) + X_ORDER:
        xo = lax.rem(x + XN - ox, XN)
        for oy in range(1, YN):
            y_copies[ox, oy].wait_recv()
            to_core(ox, oy)
        for oy in range(YN):
            if KN > 1:
                c_copies[ox, oy].wait_recv()
        xg = xb[pl.ds(xo * YK, YK)].reshape(GR, xb.shape[2])
        yf[...] = dot(xg, wp[...])
        for o in range(ZL):
            zo = lax.rem(zl + o, ZL)
            for t in range(STEPS):
                piece = jnp.concatenate(
                    [
                        yf[pl.ds(t * ZN + h * ZL + zo, YK, stride=STEPS * ZN), :]
                        for h in range(ZH)
                    ],
                    axis=0,
                )
                sred[ox, o, pl.ds(t * BEAMS, BEAMS), :] = piece.astype(BF16)
            if o > 0:
                r_copies[ox, o] = push(
                    rc(sred.at[ox, o], rred.at[ox, o], rs.at[ox, o], rr.at[ox, o], at(zl_=zo))
                )

    at_row = lax.broadcasted_iota(jnp.int32, (16, 128), 0)
    place = jnp.zeros((16, 128), jnp.int32)
    for i in range(XN):
        for t in range(STEPS):
            place = jnp.where(at_row == i * STEPS + t, lens[zl * XN + i] + (prompt_total + t), place)
    angles = place.astype(F32) * freq[...]
    turns = jnp.round(angles * (1.0 / TURN))
    angles = ((angles - turns * TURN_A) - turns * TURN_B) - turns * TURN_C
    lower = lax.broadcasted_iota(jnp.int32, (16, 128), 1) < HEAD // 2
    sines = jnp.sin(angles)
    plain = x == 3
    cos_rows[...] = jnp.where(plain, 1.0, jnp.cos(angles))
    sin_rows[...] = jnp.where(plain, 0.0, jnp.where(lower, -sines, sines))

    scale = jnp.where(x < 2, query_scale, 1.0).astype(F32)
    g_copies = {}
    for ox in (0,) + X_ORDER:
        xo = lax.rem(x + XN - ox, XN)
        total = sred[ox, 0].astype(F32)
        for o in range(1, ZL):
            r_copies[ox, o].wait_recv()
            total = total + rred[ox, o].astype(F32)
        for t in range(STEPS):
            part = total[t * BEAMS : (t + 1) * BEAMS]
            cosine = cos_rows[pl.ds(xo * STEPS + t, 1), :]
            sine = sin_rows[pl.ds(xo * STEPS + t, 1), :]
            turned = part * cosine + pltpu.roll(part, HEAD // 2, 1) * sine
            gf[ox, pl.ds(t * BEAMS, BEAMS), :] = (turned * scale).astype(BF16)
        if ox == 0:
            g[x] = gf[0]
        else:
            g_copies[ox] = push(rc(gf.at[ox], g.at[x], gs.at[ox], gr.at[ox], at(x_=xo)))
    for ox in X_ORDER:
        g_copies[ox].wait_recv()

    q_copies = []
    for o in range(1, ZL):
        q_copies.append(
            push(rc(g.at[pl.ds(0, 2)], qa.at[zl], qs.at[o], qr.at[o], at(zl_=lax.rem(zl + o, ZL))))
        )
    qa[zl] = g[0:2]

    length = lens[c]
    for cp in loc[1:3]:
        cp.wait()
    p0 = [par[0, 0, b] for b in range(BEAMS)]
    p1 = [par[1, 0, b] for b in range(BEAMS)]
    p2 = [par[2, 0, b] for b in range(BEAMS)]
    first_of = [par[0, 0, p1[b]] for b in range(BEAMS)]
    mid_of = [par[1, 0, p2[b]] for b in range(BEAMS)]
    last_of = [par[0, 0, mid_of[b]] for b in range(BEAMS)]
    never = jnp.int32(-1)
    for b in range(BEAMS):
        own = jnp.int32(b)
        chains = (
            (p0[b], own, never, never),
            (first_of[b], p1[b], own + BEAMS, never),
            (last_of[b], mid_of[b], p2[b] + BEAMS, own + 2 * BEAMS),
        )
        for t in range(STEPS):
            row = t * BEAMS + b
            ancv[pl.ds(row, 1), :] = jnp.full((1, 128), chains[t][0], jnp.int32)
            for u in range(STEPS):
                freshv[u, pl.ds(row, 1), :] = jnp.full((1, 128), chains[t][1 + u], jnp.int32)
    my_q = g[0:2].reshape(2 * ROWS, HEAD)
    SLOTS = kcv.shape[1]
    anc = ancv[:, :SLOTS]
    anc2 = jnp.concatenate([anc, anc], axis=0)
    slot = lax.broadcasted_iota(jnp.int32, (2 * ROWS, SLOTS), 1)
    lane = lax.broadcasted_iota(jnp.int32, (ROWS, ROWS), 1)
    seen = (lane == freshv[0, :, :ROWS]) | (lane == freshv[1, :, :ROWS]) | (lane == freshv[2, :, :ROWS])
    seen2 = jnp.concatenate([seen.astype(F32)] * 2, axis=0)
    fresh_w = weights_of(dot_t(my_q, g[2])) * seen2
    suf_w = dot(fresh_w.astype(BF16), g[3])
    suf_t = jnp.sum(fresh_w, axis=1, keepdims=True)
    for b in range(BEAMS):
        cached = weights_of(dot_t(my_q, kcv[b]))
        cached = jnp.where((anc2 == b) & (slot < length), cached, 0.0)
        suf_w = suf_w + dot(cached.astype(BF16), vcv[b])
        suf_t = suf_t + jnp.sum(cached, axis=1, keepdims=True)

    for src, cache, dst in ((2, kcv, out_k), (3, vcv, out_v)):
        freshk[...] = g[src].astype(F32)
        slots = lax.broadcasted_iota(jnp.int32, (SLOTS, HEAD), 0)
        for b in range(BEAMS):
            rows = [
                freshk[pl.ds(mid_of[b], 1), :],
                freshk[pl.ds(p2[b] + BEAMS, 1), :],
                freshk[pl.ds(b + 2 * BEAMS, 1), :],
            ]
            block = cache[last_of[b]].astype(F32)
            for u in range(STEPS):
                block = jnp.where(slots == length + u, rows[u], block)
            dst[b] = block.astype(BF16)

    for cp in loc[3:5]:
        cp.wait()
    for cp in kv_copies:
        cp.wait_recv()
    for cp in q_copies:
        cp.wait_recv()
    acc[...] = jnp.zeros_like(acc)
    per = kall.shape[1] // POS_TILE if kall.shape[1] >= POS_TILE else 1
    tile = kall.shape[1] // per

    def attend(i, carry):
        xi = lax.div(i, per)
        at_row = pl.multiple_of(lax.rem(i, per) * tile, tile)
        keys = kall[xi, pl.ds(at_row, tile), :]
        values = vall[xi, pl.ds(at_row, tile), :]
        queries = qa[...].reshape(ZL * 2 * ROWS, HEAD)
        w = weights_of(dot_t(queries, keys)).astype(BF16)
        wide = jnp.concatenate([values, jnp.ones((tile, HEAD), BF16)], axis=1)
        acc[...] += dot(w, wide)
        return carry

    lax.fori_loop(0, XN * per, attend, 0)

    QR = 2 * ROWS
    eye = lax.broadcasted_iota(jnp.int32, (QR, 128), 0) == lax.broadcasted_iota(jnp.int32, (QR, 128), 1)
    upper = lax.broadcasted_iota(jnp.int32, (16, 128), 0) < 8
    p_copies = []
    for o in range(ZL):
        zo = lax.rem(zl + o, ZL)
        at_row = pl.multiple_of(zo * QR, 8)
        psend[o, pl.ds(0, QR), :] = acc[pl.ds(at_row, QR), pl.ds(0, HEAD)].astype(BF16)
        totals = acc[pl.ds(at_row, QR), pl.ds(HEAD, HEAD)]
        line = jnp.sum(jnp.where(eye, totals, 0.0), axis=0, keepdims=True)
        coarse = line.astype(BF16).astype(F32)
        psend[o, pl.ds(QR, 16), :] = jnp.where(upper, coarse, line - coarse).astype(BF16)
        if o > 0:
            p_copies.append(push(rc(psend.at[o], precv.at[o], ps.at[o], pr.at[o], at(zl_=zo))))
    both = psend[0].astype(F32)
    for o in range(1, ZL):
        p_copies[o - 1].wait_recv()
        both = both + precv[o].astype(F32)
    line = both[QR : QR + 1] + both[QR + 8 : QR + 9]
    column = jnp.sum(jnp.where(eye, line, 0.0), axis=1, keepdims=True)
    attended = ((both[:QR] + suf_w) / (column + suf_t)).astype(BF16)
    heads = jnp.concatenate([attended[:ROWS], attended[ROWS:]], axis=1)

    loc[0].wait()
    ordered = dot(perm[...], heads).astype(BF16)
    GRP = 4 * ZH
    HALF = YN * GRP
    WC = width // 9 if width % 1152 == 0 and width > 1152 else width
    for i in range(width // WC):
        cols = pl.ds(i * WC, WC)
        res = dot(ordered, woutv[:, cols])
        for kk in range(KN):
            br[kk, :, cols] = res[kk * HALF : (kk + 1) * HALF]
    mine = br[k]
    if KN > 1:
        csend[...] = br[1 - k].astype(BF16)
        cp = push(rc(csend, crecv, bcs, bcr, at(k_=1 - k)))
        cp.wait_recv()
        mine = mine + crecv[...].astype(F32)
    for yy in range(YN):
        s1[yy] = mine[yy * GRP : (yy + 1) * GRP]
    hw = width // 2
    by_copies = []
    for o in range(1, YN):
        yo = lax.rem(y + o, YN)
        v = s1[yo]
        ysend[o] = jnp.concatenate([v[:, :hw], v[:, hw:]], axis=0).astype(BF16)
        by_copies.append(push(rc(ysend.at[o], yrecv.at[o], bys.at[o], byr.at[o], at(y_=yo))))
    total = s1[y]
    for o in range(1, YN):
        by_copies[o - 1].wait_recv()
        v = yrecv[o].astype(F32)
        total = total + jnp.concatenate([v[:GRP], v[GRP:]], axis=1)
    branch = total[0:4]
    if ZH > 1:
        qw = width // 4
        first = zh == 0
        other = jnp.where(first, total[4:8], total[0:4])
        zsend[...] = jnp.concatenate(
            [other[:, i * qw : (i + 1) * qw] for i in range(4)], axis=0
        ).astype(BF16)
        cp = push(rc(zsend, zrecv, bzs, bzr, at(zh_=1 - zh)))
        cp.wait_recv()
        v = zrecv[...].astype(F32)
        branch = jnp.where(first, total[0:4], total[4:8]) + jnp.concatenate(
            [v[i * 4 : (i + 1) * 4] for i in range(4)], axis=1
        )
    branch = branch[0:STEPS]
    square = jnp.mean(branch * branch, axis=-1, keepdims=True)
    scaled = branch * lax.rsqrt(square + epsilon) * post_gain[...].reshape(1, width).astype(F32)
    for t in range(STEPS):
        out_h[t, 0] = hid[t : t + 1].astype(F32) + scaled[t : t + 1]

    for cp in a_copies + sends:
        cp.wait_send()
    for to in range(XN):
        @pl.when(x != to)
        def _():
            w_copy(to).wait_send()


def order_matrix(dims):
    ZH, YN, KN, ZL = dims
    beams = ZH * YN * KN
    m = np.zeros((KN * YN * ZH * 4, STEPS * beams), np.float32)
    for kk in range(KN):
        for yy in range(YN):
            for hh in range(ZH):
                for t in range(STEPS):
                    m[((kk * YN + yy) * ZH + hh) * 4 + t, t * beams + (hh * YN + yy) * KN + kk] = 1.0
    return m


def body(
    dims,
    hidden_in,
    pre_gain,
    post_gain,
    w_query,
    key_projection_weight,
    value_projection_weight,
    w_out,
    prompt_rotated_keys,
    prompt_value_rows,
    suffix_key_cache,
    suffix_value_cache,
    parents,
    lengths,
):
    ZH, YN, KN, ZL = dims
    ZN = ZH * ZL
    YK = YN * KN
    beams = ZH * YK
    rows = STEPS * beams
    width = hidden_in.shape[3]
    slots = suffix_key_cache.shape[2]
    positions = prompt_rotated_keys.shape[0]
    prompt_total = positions * ZL * XN
    depth = width // ZL
    J = -(-depth // 128)
    TJ = -(-(STEPS * J) // 16) * 16
    frequency = 1.0 / rope_base ** (np.arange(HEAD // 2) * 2.0 / HEAD)
    freq = jnp.asarray(np.concatenate([frequency, frequency])[None], F32)

    perm = jnp.asarray(order_matrix(dims), BF16)
    hbm = pl.BlockSpec(memory_space=pltpu.HBM)
    vmem = pl.BlockSpec(memory_space=pltpu.VMEM)
    smem = pl.BlockSpec(memory_space=pltpu.SMEM)
    wrows = w_query.shape[0]
    grp = 4 * ZH
    half = YN * grp
    V = pltpu.VMEM
    D = pltpu.SemaphoreType.DMA
    scratch = [
        V((ZL, TJ, 128), BF16),
        V((ZL, TJ, 128), F32),
        V((16, 128), F32),
        V((16, 128), F32),
        V((ZN, TJ, 128), BF16),
        V((ZN * TJ, 128), F32),
        V((XN * YK, STEPS * ZN, J * 128), BF16),
        V((XN, wrows, HEAD), BF16),
        V((J * 128, HEAD), BF16),
        V((YK * STEPS * ZN, HEAD), F32),
        V((XN, ZL, rows, HEAD), BF16),
        V((XN, ZL, rows, HEAD), BF16),
        V((XN, rows, HEAD), BF16),
        V((XN, rows, HEAD), BF16),
        V((ZL, 2, rows, HEAD), BF16),
        V((XN, positions, HEAD), BF16),
        V((XN, positions, HEAD), BF16),
        V((ZL * 2 * rows, 2 * HEAD), F32),
        V((ZL, 2 * rows + 16, HEAD), BF16),
        V((ZL, 2 * rows + 16, HEAD), BF16),
        V(w_out.shape, BF16),
        V((beams, slots, HEAD), BF16),
        V((beams, slots, HEAD), BF16),
        V((rows, 128), jnp.int32),
        V((STEPS, rows, 128), jnp.int32),
        V((rows, HEAD), F32),
        V((KN, half, width), F32),
        V((half, width), BF16),
        V((half, width), BF16),
        V((YN, grp, width), F32),
        V((YN, 2 * grp, width // 2), BF16),
        V((YN, 2 * grp, width // 2), BF16),
        V((16, width // 4), BF16),
        V((16, width // 4), BF16),
        D((ZN,)), D((ZN,)), D((XN,)), D((XN,)), D((2, XN)), D((2, XN)), D((XN,)), D((XN,)),
        D((XN, YN)), D((XN, YN)), D((XN, YN)), D((XN, YN)), D((XN, ZL)), D((XN, ZL)),
        D((XN,)), D((XN,)), D((ZL,)), D((ZL,)), D((ZL,)), D((ZL,)),
        D, D, D((YN,)), D((YN,)), D, D, D((8,)),
    ]
    hidden_out, keys_out, values_out = pl.pallas_call(
        functools.partial(kernel, dims, prompt_total),
        out_shape=(
            jax.ShapeDtypeStruct((STEPS, 1, 1, width), F32),
            jax.ShapeDtypeStruct((beams, slots, HEAD), BF16),
            jax.ShapeDtypeStruct((beams, slots, HEAD), BF16),
        ),
        in_specs=[vmem] * 5 + [hbm] * 8 + [smem] * 2,
        out_specs=(vmem, vmem, vmem),
        scratch_shapes=scratch,
        compiler_params=pltpu.CompilerParams(
            collective_id=0, has_side_effects=True, vmem_limit_bytes=63 * 1024 * 1024
        ),
    )(
        hidden_in.reshape(STEPS, width),
        pre_gain,
        post_gain,
        freq,
        perm,
        w_query,
        key_projection_weight,
        value_projection_weight,
        w_out,
        prompt_rotated_keys,
        prompt_value_rows,
        suffix_key_cache.reshape(beams, slots, HEAD),
        suffix_value_cache.reshape(beams, slots, HEAD),
        parents,
        lengths,
    )
    return (
        hidden_out,
        keys_out.reshape(1, beams, slots, HEAD),
        values_out.reshape(1, beams, slots, HEAD),
    )


def solution(mesh, dims=(2, 4, 2, 8)):
    placed = (
        P(None, "context", "sample", None),
        P(),
        P(),
        P("context", "sample"),
        P("context", "sample"),
        P("context", "sample"),
        P("sample", None),
        P("context", "sample"),
        P("context", "sample"),
        P("context", None, None, "sample"),
        P("context", None, None, "sample"),
        P(None, "context", None),
        P(),
    )
    return jax.shard_map(
        functools.partial(body, dims),
        mesh=mesh,
        in_specs=placed,
        out_specs=(
            P(None, "context", "sample", None),
            P("context", None, None, "sample"),
            P("context", None, None, "sample"),
        ),
        check_vma=False,
    )
```

```python
import functools

import jax
import jax.numpy as jnp
import numpy as np
from jax import lax
from jax.experimental import pallas as pl
from jax.experimental.pallas import tpu as pltpu
from jax.sharding import PartitionSpec as P

HEAD = 128
STEPS = 3
XN = 4
BLOCK = 16
CHUNKS = 3
POS_TILE = 512

epsilon = 1e-06
query_scale = 144.0 ** (-0.5)
rope_base = 10000.0
logit_cap = 50.0
TURN = 2 * np.pi
TURN_A = 6.28125
TURN_B = float(np.float32(np.round((TURN - TURN_A) * 2.0**20) / 2.0**20))
TURN_C = float(TURN - TURN_A - TURN_B)
MESH = pl.DeviceIdType.MESH
F32 = jnp.float32
BF16 = jnp.bfloat16
AROUND = (1, 3, 2)


def weights_of(scores):
    return jnp.exp(logit_cap * jnp.tanh(scores * (1.0 / logit_cap)))


def dot_t(a, b):
    return lax.dot_general(a, b, (((1,), (1,)), ((), ())), preferred_element_type=F32)


def dot(a, b):
    return jnp.dot(a, b, preferred_element_type=F32)


def iota(shape, axis):
    return lax.broadcasted_iota(jnp.int32, shape, axis)


def kernel(
    dims, prompt_total,
    hid, pre_gain, post_gain, freq, perm, wq, wk, wv, wout, pk, pv, kc, vc, par, lens,
    out_h, out_f,
    tiles, tilesf, cos_rows, sin_rows, a1, a1f, xb, wz, yf, sred, rred, g, gf, qa, kall, vall, acc,
    psend, precv, both, osend, orecv, woutv, kcv, vcv, ancv, freshv, br, csend, crecv, s1, ysend,
    yrecv, zsend, zrecv,
    as_, ar, ws, wr, wzs, wzr, ks, kr, pxs, pxr, pys, pyr, rys, ryr, rxs, rxr, cs, cr, rs, rr, gs,
    gr, qs, qr, ps, pr, os_, or_, bcs, bcr, bys, byr, bzs, bzr, ls,
):
    ZH, YN, KN, ZL = dims
    ZN = ZH * ZL
    PN = ZL // 2
    GN = 2 * ZH
    YK = YN * KN
    BEAMS = ZH * YK
    ROWS = STEPS * BEAMS
    s = lax.axis_index("sample")
    c = lax.axis_index("context")
    zh = lax.div(s, YK)
    y = lax.div(lax.rem(s, YK), KN)
    k = lax.rem(s, KN)
    zl = lax.div(c, XN)
    x = lax.rem(c, XN)
    z = zh * ZL + zl
    q = lax.div(zl, PN)
    p = lax.rem(zl, PN)
    width = hid.shape[1]

    def at(zh_=None, y_=None, k_=None, zl_=None, x_=None):
        zh_ = zh if zh_ is None else zh_
        y_ = y if y_ is None else y_
        k_ = k if k_ is None else k_
        zl_ = zl if zl_ is None else zl_
        x_ = x if x_ is None else x_
        return {"sample": zh_ * YK + y_ * KN + k_, "context": zl_ * XN + x_}

    def rc(src, dst, ssem, rsem, where):
        return pltpu.make_async_remote_copy(
            src_ref=src, dst_ref=dst, send_sem=ssem, recv_sem=rsem,
            device_id=where, device_id_type=MESH,
        )

    sends = []

    def push(cp):
        cp.start()
        sends.append(cp)
        return cp

    def x_of(o):
        return lax.rem(x + o + XN, XN)

    def y_of(o):
        return lax.rem(y + o + YN, YN)

    def p_of(o):
        return lax.rem(p + o + PN, PN)

    def half_at(m):
        zz = lax.rem(z + PN * m, ZN)
        zl_ = lax.rem(zz, ZL)
        return at(zh_=lax.div(zz, ZL), zl_=zl_), lax.div(zl_, PN)

    across = at(zl_=(1 - q) * PN + p)

    peers = [half_at(m)[0] for m in range(1, GN)]
    peers += [at(zl_=q * PN + p_of(o)) for o in range(1, PN)]
    peers += [at(x_=x_of(o)) for o in range(1, XN)]
    peers += [at(y_=y_of(o)) for o in range(1, YN)]
    if KN > 1:
        peers += [at(k_=1 - k)]
    if ZH == 1:
        assert GN == 2
    barrier = pltpu.get_barrier_semaphore()
    for peer in peers:
        pl.semaphore_signal(barrier, inc=1, device_id=peer, device_id_type=MESH)

    loc = [
        pltpu.make_async_copy(wout, woutv, ls.at[1]),
        pltpu.make_async_copy(kc, kcv, ls.at[2]),
        pltpu.make_async_copy(vc, vcv, ls.at[3]),
        pltpu.make_async_copy(pk, kall.at[x], ls.at[4]),
        pltpu.make_async_copy(pv, vall.at[x], ls.at[5]),
    ]
    for cp in loc:
        cp.start()

    J = width // 256
    TJ = a1.shape[1]
    hid_f = hid[...].astype(F32)
    mean_square = jnp.mean(hid_f * hid_f, axis=-1, keepdims=True)
    normed = hid_f * lax.rsqrt(mean_square + epsilon) * pre_gain[...].reshape(1, width).astype(F32)
    for part in range(2):
        for j in range(J):
            start = (part * J + j) * 128
            tilesf[part, pl.ds(j * STEPS, STEPS), :] = normed[:, start : start + 128]
        if TJ > J * STEPS:
            tilesf[part, pl.ds(J * STEPS, TJ - J * STEPS), :] = jnp.zeros((TJ - J * STEPS, 128), F32)
    tiles[...] = tilesf[...].astype(BF16)
    pl.semaphore_wait(barrier, len(peers))

    mine = lax.div(z, PN)
    a_copies = []
    for m in (2, 1, 3):
        if m < GN:
            where, q_to = half_at(m)
            a_copies.append(push(rc(tiles.at[q_to], a1.at[mine], as_.at[m], ar.at[m], where)))

    half = wq.shape[1] // 2
    w_src = [wq.at[:, pl.ds(0, half)], wq.at[:, pl.ds(half, half)], wk, wv]

    def w_copy(to):
        return rc(w_src[to], wz.at[p, x], ws.at[to], wr.at[x], at(x_=to))

    def w_local(to):
        return pltpu.make_async_copy(w_src[to], wz.at[p, x], ls.at[0])

    for to in range(XN):
        @pl.when(x != to)
        def _():
            w_copy(to).start()

        @pl.when(x == to)
        def _():
            w_local(to).start()

    kv_copies = []

    def send_prompt(which, o):
        src, dst = ((pk, kall), (pv, vall))[which]
        kv_copies.append(push(rc(src, dst.at[x], ks.at[which, o], kr.at[which, o], at(x_=x_of(o)))))

    a1[mine] = tiles[q]
    for to in range(XN):
        @pl.when(x != to)
        def _():
            rc(w_src[to], wz.at[p, to], ws.at[to], wr.at[to], at(x_=to)).wait_recv()

        @pl.when(x == to)
        def _():
            w_local(to).wait()
    wz_copies = []
    for o in range(1, PN):
        wz_copies.append(
            push(rc(wz.at[p], wz.at[p], wzs.at[o], wzr.at[o], at(zl_=q * PN + p_of(o))))
        )
    send_prompt(0, 1)
    send_prompt(0, 3)
    for cp in a_copies:
        cp.wait_recv()

    for i in range(GN):
        a1f[pl.ds(i * TJ, TJ), :] = a1[i].astype(F32)
    own = (x * YN + y) * KN + k
    rest = jnp.zeros((BLOCK - STEPS * GN, 128), F32)
    for j in range(J):
        lines = [a1f[pl.ds(j * STEPS + t, GN, stride=TJ), :] for t in range(STEPS)]
        xb[own, :, pl.ds(j * 128, 128)] = jnp.concatenate(lines + [rest], axis=0).astype(BF16)

    cols = xb.shape[2] // 2

    def blk(ox, oy):
        return (x_of(-ox) * YN + y_of(-oy)) * KN + k

    def first(b):
        return xb.at[b, :, pl.ds(0, cols)]

    def second(b):
        return xb.at[b, :, pl.ds(cols, cols)]

    px, py, ry, rx, cc = {}, {}, {}, {}, {}

    def forward_y(ox):
        b = blk(ox, 0)
        for o in AROUND[: YN - 1]:
            py[ox, o] = push(rc(first(b), first(b), pys.at[ox, o], pyr.at[ox, o], at(y_=y_of(o))))

    def forward_x(oy):
        b = blk(0, oy)
        for o in AROUND:
            rx[oy, o] = push(rc(second(b), second(b), rxs.at[oy, o], rxr.at[oy, o], at(x_=x_of(o))))

    def to_core(ox, oy):
        if KN > 1:
            b = xb.at[blk(ox, oy)]
            cc[ox, oy] = push(rc(b, b, cs.at[ox, oy], cr.at[ox, oy], at(k_=1 - k)))

    y_around = [o for o in AROUND if o < YN]
    for o in AROUND:
        b = blk(0, 0)
        px[o] = push(rc(first(b), first(b), pxs.at[o], pxr.at[o], at(x_=x_of(o))))
        if o < YN:
            ry[o] = push(rc(second(b), second(b), rys.at[o], ryr.at[o], at(y_=y_of(o))))
    if YN > 1:
        for o in y_around:
            b = blk(0, 0)
            py[0, o] = push(rc(first(b), first(b), pys.at[0, o], pyr.at[0, o], at(y_=y_of(o))))
    forward_x(0)
    to_core(0, 0)
    for o in AROUND:
        px[o].wait_recv()
        for o2 in y_around:
            b = blk(o, 0)
            py[o, o2] = push(rc(first(b), first(b), pys.at[o, o2], pyr.at[o, o2], at(y_=y_of(o2))))
        if o < YN:
            ry[o].wait_recv()
            forward_x(o)

    def gather(ox):
        for oy in [0] + y_around:
            if oy > 0:
                py[ox, oy].wait_recv()
            if ox > 0:
                rx[oy, ox].wait_recv()
            if ox > 0 or oy > 0:
                to_core(ox, oy)

    r_copies = {}

    def project(ox):
        for oy in [0] + y_around:
            if KN > 1:
                cc[ox, oy].wait_recv()
        rows = xb[pl.ds(x_of(-ox) * YK, YK)].reshape(YK * BLOCK, xb.shape[2])
        yf[...] = dot(rows, wz[...].reshape(xb.shape[2], HEAD))
        for h in range(2):
            for t in range(STEPS):
                piece = [
                    yf[pl.ds(t * GN + i * 2 + h, YK, stride=BLOCK), :] for i in range(ZH)
                ]
                sred[ox, h, pl.ds(t * BEAMS, BEAMS), :] = jnp.concatenate(piece, axis=0).astype(BF16)
        r_copies[ox] = push(rc(sred.at[ox], rred.at[ox], rs.at[ox], rr.at[ox], across))

    gather(0)
    for cp in wz_copies:
        cp.wait_recv()
    project(0)
    gather(1)
    gather(3)
    project(1)
    gather(2)
    project(3)
    project(2)
    for which, o in ((0, 2), (1, 1), (1, 3), (1, 2)):
        send_prompt(which, o)

    NT = 2 * XN * STEPS
    at_row = iota((NT, 128), 0)
    place = jnp.zeros((NT, 128), jnp.int32)
    for h in range(2):
        for i in range(XN):
            for t in range(STEPS):
                here = lens[(h * PN + p) * XN + i] + (prompt_total + t)
                place = jnp.where(at_row == (h * XN + i) * STEPS + t, here, place)
    angles = place.astype(F32) * freq[...]
    turns = jnp.round(angles * (1.0 / TURN))
    angles = ((angles - turns * TURN_A) - turns * TURN_B) - turns * TURN_C
    lower = iota((NT, 128), 1) < HEAD // 2
    sines = jnp.sin(angles)
    plain = x == 3
    cos_rows[...] = jnp.where(plain, 1.0, jnp.cos(angles))
    sin_rows[...] = jnp.where(plain, 0.0, jnp.where(lower, -sines, sines))

    scale = jnp.where(x < 2, query_scale, 1.0).astype(F32)
    g_copies = {}
    for ox in (0,) + AROUND:
        xo = x_of(-ox)
        r_copies[ox].wait_recv()
        for h in range(2):
            total = sred[ox, h].astype(F32) + rred[ox, h].astype(F32)
            for t in range(STEPS):
                part = total[t * BEAMS : (t + 1) * BEAMS]
                row = pl.ds((h * XN + xo) * STEPS + t, 1)
                turned = part * cos_rows[row, :] + pltpu.roll(part, HEAD // 2, 1) * sin_rows[row, :]
                gf[ox, h, pl.ds(t * BEAMS, BEAMS), :] = (turned * scale).astype(BF16)
        if ox == 0:
            for h in range(2):
                g[h, x] = gf[0, h]
        else:
            g_copies[ox] = push(rc(gf.at[ox], g.at[:, x], gs.at[ox], gr.at[ox], at(x_=xo)))
    for ox in AROUND:
        g_copies[ox].wait_recv()

    q_copies = {}
    for o in range(1, PN):
        q_copies[o] = push(
            rc(g.at[:, pl.ds(0, 2)], qa.at[p], qs.at[o], qr.at[o], at(zl_=q * PN + p_of(o)))
        )
    for h in range(2):
        qa[p, h] = g[h, 0:2]

    for cp in loc[3:5]:
        cp.wait()
    for cp in kv_copies:
        cp.wait_recv()
    per = kall.shape[1] // POS_TILE if kall.shape[1] >= POS_TILE else 1
    tile = kall.shape[1] // per
    QR = 2 * ROWS
    eye = iota((QR, 128), 0) == iota((QR, 128), 1)
    upper = iota((16, 128), 0) < 8

    def with_totals(line):
        coarse = line.astype(BF16).astype(F32)
        return jnp.where(upper, coarse, line - coarse).astype(BF16)

    p_copies = {}
    for o in [0] + [o for o in AROUND if o < PN]:
        if o > 0:
            q_copies[o].wait_recv()
        there = p_of(-o)
        acc[...] = jnp.zeros_like(acc)

        def attend(i, carry):
            xi = lax.div(i, per)
            at_pos = pl.multiple_of(lax.rem(i, per) * tile, tile)
            keys = kall[xi, pl.ds(at_pos, tile), :]
            values = vall[xi, pl.ds(at_pos, tile), :]
            w = weights_of(dot_t(qa[there].reshape(2 * QR, HEAD), keys)).astype(BF16)
            acc[...] += dot(w, jnp.concatenate([values, jnp.ones((tile, HEAD), BF16)], axis=1))
            return carry

        lax.fori_loop(0, XN * per, attend, 0)
        for h in range(2):
            psend[o, h, pl.ds(0, QR), :] = acc[pl.ds(h * QR, QR), pl.ds(0, HEAD)].astype(BF16)
            totals = acc[pl.ds(h * QR, QR), pl.ds(HEAD, HEAD)]
            line = jnp.sum(jnp.where(eye, totals, 0.0), axis=0, keepdims=True)
            psend[o, h, pl.ds(QR, 16), :] = with_totals(line)
        if o > 0:
            p_copies[o] = push(
                rc(psend.at[o], precv.at[o], ps.at[o], pr.at[o], at(zl_=q * PN + there))
            )

    length = lens[c]
    for cp in loc[1:3]:
        cp.wait()
    never = jnp.int32(-1)
    for b in range(BEAMS):
        one = par[1, 0, b]
        two = par[2, 0, b]
        mid = par[1, 0, two]
        me = jnp.int32(b)
        chains = (
            (par[0, 0, b], me, never, never),
            (par[0, 0, one], one, me + BEAMS, never),
            (par[0, 0, mid], mid, two + BEAMS, me + 2 * BEAMS),
        )
        for t in range(STEPS):
            row = t * BEAMS + b
            ancv[pl.ds(row, 1), :] = jnp.full((1, 128), chains[t][0], jnp.int32)
            for u in range(STEPS):
                freshv[u, pl.ds(row, 1), :] = jnp.full((1, 128), chains[t][1 + u], jnp.int32)
    my_q = g[q, 0:2].reshape(QR, HEAD)
    SLOTS = kcv.shape[1]
    anc = ancv[:, :SLOTS]
    anc2 = jnp.concatenate([anc, anc], axis=0)
    in_use = iota((QR, SLOTS), 1) < length
    lane = iota((ROWS, ROWS), 1)
    seen = (lane == freshv[0, :, :ROWS]) | (lane == freshv[1, :, :ROWS]) | (lane == freshv[2, :, :ROWS])
    seen2 = jnp.concatenate([seen.astype(F32)] * 2, axis=0)
    fresh_w = weights_of(dot_t(my_q, g[q, 2])) * seen2
    suf_w = dot(fresh_w.astype(BF16), g[q, 3])
    suf_t = jnp.sum(fresh_w, axis=1, keepdims=True)
    for b in range(BEAMS):
        cached = weights_of(dot_t(my_q, kcv[b]))
        cached = jnp.where((anc2 == b) & in_use, cached, 0.0)
        suf_w = suf_w + dot(cached.astype(BF16), vcv[b])
        suf_t = suf_t + jnp.sum(cached, axis=1, keepdims=True)
    out_f[...] = g[q, 2:4]

    for h in range(2):
        both[h] = psend[0, h].astype(F32)
    for o in range(1, PN):
        p_copies[o].wait_recv()
        for h in range(2):
            both[h] += precv[o, h].astype(F32)
    theirs = both[1 - q]
    osend[pl.ds(0, QR), :] = theirs[:QR].astype(BF16)
    osend[pl.ds(QR, 16), :] = with_totals(theirs[QR : QR + 1] + theirs[QR + 8 : QR + 9])
    o_copy = push(rc(osend, orecv, os_, or_, across))
    ours = both[q]
    o_copy.wait_recv()
    ours = ours + orecv[...].astype(F32)
    line = ours[QR : QR + 1] + ours[QR + 8 : QR + 9]
    column = jnp.sum(jnp.where(eye, line, 0.0), axis=1, keepdims=True)
    attended = ((ours[:QR] + suf_w) / (column + suf_t)).astype(BF16)
    heads = jnp.concatenate([attended[:ROWS], attended[ROWS:]], axis=1)

    loc[0].wait()
    ordered = dot(perm[...], heads).astype(BF16)
    GRP = 4 * ZH
    HALF = YN * GRP
    wide = width // CHUNKS
    bc_copies = []
    for i in range(CHUNKS):
        for n in range(3):
            part = wide // 3
            at_col = pl.ds(i * wide + n * part, part)
            res = dot(ordered, woutv[:, at_col])
            for kk in range(KN):
                br[kk, i, :, pl.ds(n * part, part)] = res[kk * HALF : (kk + 1) * HALF]
        if KN > 1:
            csend[i] = br[1 - k, i].astype(BF16)
            bc_copies.append(push(rc(csend.at[i], crecv.at[i], bcs.at[i], bcr.at[i], at(k_=1 - k))))
    by_copies = {}
    for i in range(CHUNKS):
        total = br[k, i]
        if KN > 1:
            bc_copies[i].wait_recv()
            total = total + crecv[i].astype(F32)
        for yy in range(YN):
            s1[i, yy] = total[yy * GRP : (yy + 1) * GRP]
        for o in y_around:
            v = s1[i, y_of(o)]
            ysend[i, o] = jnp.concatenate([v[:, : wide // 2], v[:, wide // 2 :]], axis=0).astype(BF16)
            by_copies[i, o] = push(
                rc(ysend.at[i, o], yrecv.at[i, o], bys.at[i, o], byr.at[i, o], at(y_=y_of(o)))
            )
    bz_copies = []
    kept = []
    is_first = zh == 0
    quarter = wide // 4
    for i in range(CHUNKS):
        total = s1[i, y]
        for o in y_around:
            by_copies[i, o].wait_recv()
            v = yrecv[i, o].astype(F32)
            total = total + jnp.concatenate([v[:GRP], v[GRP:]], axis=1)
        if ZH > 1:
            other = jnp.where(is_first, total[4:8], total[0:4])
            zsend[i] = jnp.concatenate(
                [other[:, n * quarter : (n + 1) * quarter] for n in range(4)], axis=0
            ).astype(BF16)
            bz_copies.append(push(rc(zsend.at[i], zrecv.at[i], bzs.at[i], bzr.at[i], at(zh_=1 - zh))))
            kept.append(jnp.where(is_first, total[0:4], total[4:8]))
        else:
            kept.append(total[0:4])
    if ZH > 1:
        for i in range(CHUNKS):
            bz_copies[i].wait_recv()
            v = zrecv[i].astype(F32)
            kept[i] = kept[i] + jnp.concatenate([v[n * 4 : (n + 1) * 4] for n in range(4)], axis=1)
    square = sum(jnp.sum(v * v, axis=-1, keepdims=True) for v in kept) * (1.0 / width)
    factor = lax.rsqrt(square + epsilon)
    branch = jnp.concatenate(kept, axis=1) * factor
    out_h[...] = hid[...].astype(F32) + branch[:STEPS] * post_gain[...].reshape(1, width).astype(F32)

    for cp in sends:
        cp.wait_send()
    for to in range(XN):
        @pl.when(x != to)
        def _():
            w_copy(to).wait_send()


def cache_kernel(hid, fresh, kc, vc, par, lens, out_h, out_k, out_v, old, new, rows, ins, outs):
    beams, slots = kc.shape[0], kc.shape[1]
    length = lens[lax.axis_index("context")]
    loads = [pltpu.make_async_copy(src, old.at[i], ins.at[i]) for i, src in enumerate((kc, vc))]
    for cp in loads:
        cp.start()
    for t in range(STEPS):
        out_h[t, 0] = hid[t : t + 1]
    window = min(32, slots)
    start = pl.multiple_of(jnp.minimum(lax.div(length, 16) * 16, slots - window), 16)
    at_slot = iota((window, HEAD), 0) + start
    group = max(beams // 4, 1)
    stores = []
    for i, dst in enumerate((out_k, out_v)):
        rows[...] = fresh[i].astype(F32)
        loads[i].wait()
        for b in range(beams):
            two = par[2, 0, b]
            mid = par[1, 0, two]
            new[i, b] = old[i, par[0, 0, mid]]
            block = new[i, b, pl.ds(start, window), :].astype(F32)
            for u, row in enumerate((mid, two + beams, b + 2 * beams)):
                block = jnp.where(at_slot == length + u, rows[pl.ds(row, 1), :], block)
            new[i, b, pl.ds(start, window), :] = block.astype(BF16)
            if (b + 1) % group == 0:
                span = pl.ds(b + 1 - group, group)
                cp = pltpu.make_async_copy(new.at[i, span], dst.at[span], outs.at[i, b // group])
                cp.start()
                stores.append(cp)
    for cp in stores:
        cp.wait()


def order_matrix(dims):
    ZH, YN, KN, ZL = dims
    beams = ZH * YN * KN
    m = np.zeros((KN * YN * ZH * 4, STEPS * beams), np.float32)
    for kk in range(KN):
        for yy in range(YN):
            for hh in range(ZH):
                for t in range(STEPS):
                    m[((kk * YN + yy) * ZH + hh) * 4 + t, t * beams + (hh * YN + yy) * KN + kk] = 1.0
    return m


def body(
    dims,
    hidden_in,
    pre_gain,
    post_gain,
    w_query,
    key_projection_weight,
    value_projection_weight,
    w_out,
    prompt_rotated_keys,
    prompt_value_rows,
    suffix_key_cache,
    suffix_value_cache,
    parents,
    lengths,
):
    ZH, YN, KN, ZL = dims
    PN = ZL // 2
    GN = 2 * ZH
    YK = YN * KN
    beams = ZH * YK
    rows = STEPS * beams
    width = hidden_in.shape[3]
    slots = suffix_key_cache.shape[2]
    positions = prompt_rotated_keys.shape[0]
    prompt_total = positions * ZL * XN
    J = width // 256
    TJ = -(-(STEPS * J) // 16) * 16
    frequency = 1.0 / rope_base ** (np.arange(HEAD // 2) * 2.0 / HEAD)
    freq = jnp.asarray(np.concatenate([frequency, frequency])[None], F32)
    perm = jnp.asarray(order_matrix(dims), BF16)
    hbm = pl.BlockSpec(memory_space=pltpu.HBM)
    vmem = pl.BlockSpec(memory_space=pltpu.VMEM)
    smem = pl.BlockSpec(memory_space=pltpu.SMEM)
    wrows = w_query.shape[0]
    grp = 4 * ZH
    half = YN * grp
    wide = width // CHUNKS
    V = pltpu.VMEM
    D = pltpu.SemaphoreType.DMA
    scratch = [
        V((2, TJ, 128), BF16),
        V((2, TJ, 128), F32),
        V((2 * XN * STEPS, 128), F32),
        V((2 * XN * STEPS, 128), F32),
        V((GN, TJ, 128), BF16),
        V((GN * TJ, 128), F32),
        V((XN * YK, BLOCK, width // 2), BF16),
        V((PN, XN, wrows, HEAD), BF16),
        V((YK * BLOCK, HEAD), F32),
        V((XN, 2, rows, HEAD), BF16),
        V((XN, 2, rows, HEAD), BF16),
        V((2, XN, rows, HEAD), BF16),
        V((XN, 2, rows, HEAD), BF16),
        V((PN, 2, 2, rows, HEAD), BF16),
        V((XN, positions, HEAD), BF16),
        V((XN, positions, HEAD), BF16),
        V((4 * rows, 2 * HEAD), F32),
        V((PN, 2, 2 * rows + 16, HEAD), BF16),
        V((PN, 2, 2 * rows + 16, HEAD), BF16),
        V((2, 2 * rows + 16, HEAD), F32),
        V((2 * rows + 16, HEAD), BF16),
        V((2 * rows + 16, HEAD), BF16),
        V(w_out.shape, BF16),
        V((beams, slots, HEAD), BF16),
        V((beams, slots, HEAD), BF16),
        V((rows, 128), jnp.int32),
        V((STEPS, rows, 128), jnp.int32),
        V((KN, CHUNKS, half, wide), F32),
        V((CHUNKS, half, wide), BF16),
        V((CHUNKS, half, wide), BF16),
        V((CHUNKS, YN, grp, wide), F32),
        V((CHUNKS, YN, 2 * grp, wide // 2), BF16),
        V((CHUNKS, YN, 2 * grp, wide // 2), BF16),
        V((CHUNKS, 16, wide // 4), BF16),
        V((CHUNKS, 16, wide // 4), BF16),
        D((4,)), D((4,)), D((XN,)), D((XN,)), D((PN,)), D((PN,)), D((2, XN)), D((2, XN)),
        D((XN,)), D((XN,)), D((XN, 4)), D((XN, 4)), D((4,)), D((4,)), D((4, XN)), D((4, XN)),
        D((XN, 4)), D((XN, 4)), D((XN,)), D((XN,)), D((XN,)), D((XN,)), D((PN,)), D((PN,)),
        D((PN,)), D((PN,)), D, D, D((CHUNKS,)), D((CHUNKS,)), D((CHUNKS, 4)), D((CHUNKS, 4)),
        D((CHUNKS,)), D((CHUNKS,)), D((8,)),
    ]
    keys_in = suffix_key_cache.reshape(beams, slots, HEAD)
    values_in = suffix_value_cache.reshape(beams, slots, HEAD)
    hidden, fresh = pl.pallas_call(
        functools.partial(kernel, dims, prompt_total),
        out_shape=(
            jax.ShapeDtypeStruct((STEPS, width), F32),
            jax.ShapeDtypeStruct((2, rows, HEAD), BF16),
        ),
        in_specs=[vmem] * 5 + [hbm] * 8 + [smem] * 2,
        out_specs=(vmem, vmem),
        scratch_shapes=scratch,
        compiler_params=pltpu.CompilerParams(
            collective_id=0, has_side_effects=True, vmem_limit_bytes=63 * 1024 * 1024
        ),
    )(
        hidden_in.reshape(STEPS, width),
        pre_gain,
        post_gain,
        freq,
        perm,
        w_query,
        key_projection_weight,
        value_projection_weight,
        w_out,
        prompt_rotated_keys,
        prompt_value_rows,
        keys_in,
        values_in,
        parents,
        lengths,
    )
    hidden_out, keys_out, values_out = pl.pallas_call(
        cache_kernel,
        out_shape=(
            jax.ShapeDtypeStruct((STEPS, 1, 1, width), F32),
            jax.ShapeDtypeStruct((beams, slots, HEAD), BF16),
            jax.ShapeDtypeStruct((beams, slots, HEAD), BF16),
        ),
        in_specs=[vmem] * 2 + [hbm] * 2 + [smem] * 2,
        out_specs=(vmem, hbm, hbm),
        scratch_shapes=[
            V((2, beams, slots, HEAD), BF16),
            V((2, beams, slots, HEAD), BF16),
            V((rows, HEAD), F32),
            D((2,)),
            D((2, 4)),
        ],
        compiler_params=pltpu.CompilerParams(vmem_limit_bytes=63 * 1024 * 1024),
    )(hidden, fresh, keys_in, values_in, parents, lengths)
    return (
        hidden_out,
        keys_out.reshape(1, beams, slots, HEAD),
        values_out.reshape(1, beams, slots, HEAD),
    )


def solution(mesh, dims=(2, 4, 2, 8)):
    placed = (
        P(None, "context", "sample", None),
        P(),
        P(),
        P("context", "sample"),
        P("context", "sample"),
        P("context", "sample"),
        P("sample", None),
        P("context", "sample"),
        P("context", "sample"),
        P("context", None, None, "sample"),
        P("context", None, None, "sample"),
        P(None, "context", None),
        P(),
    )
    return jax.shard_map(
        functools.partial(body, dims),
        mesh=mesh,
        in_specs=placed,
        out_specs=(
            P(None, "context", "sample", None),
            P("context", None, None, "sample"),
            P("context", None, None, "sample"),
        ),
        check_vma=False,
    )
```

```python
import functools

import jax
import jax.numpy as jnp
import numpy as np
from jax import lax
from jax.experimental import pallas as pl
from jax.experimental.pallas import tpu as pltpu
from jax.sharding import PartitionSpec as P

HEAD = 128
STEPS = 3
XN = 4
BLOCK = 16
CHUNKS = 3

epsilon = 1e-06
query_scale = 144.0 ** (-0.5)
rope_base = 10000.0
logit_cap = 50.0
TURN = 2 * np.pi
TURN_A = 6.28125
TURN_B = float(np.float32(np.round((TURN - TURN_A) * 2.0**20) / 2.0**20))
TURN_C = float(TURN - TURN_A - TURN_B)
MESH = pl.DeviceIdType.MESH
F32 = jnp.float32
BF16 = jnp.bfloat16
AROUND = (1, 3, 2)


def weights_of(scores):
    return jnp.exp(logit_cap * jnp.tanh(scores * (1.0 / logit_cap)))


def dot_t(a, b):
    return lax.dot_general(a, b, (((1,), (1,)), ((), ())), preferred_element_type=F32)


def dot(a, b):
    return jnp.dot(a, b, preferred_element_type=F32)


def iota(shape, axis):
    return lax.broadcasted_iota(jnp.int32, shape, axis)


def kernel(
    dims, prompt_total,
    hid, pre_gain, post_gain, freq, perm, wq, wk, wv, wout, pk, pv, kc, vc, par, lens,
    out_h, out_f,
    tiles, tilesf, cos_rows, sin_rows, a1, a1f, xb, wz, yf, sred, rred, g, gf, qa, kall, vall, acc,
    psend, precv, both, osend, orecv, woutv, kcv, vcv, ancv, freshv, br, csend, crecv, s1, ysend,
    yrecv, zsend, zrecv,
    as_, ar, ws, wr, wzs, wzr, ks, kr, pxs, pxr, pys, pyr, rys, ryr, rxs, rxr, cs, cr, rs, rr, gs,
    gr, qs, qr, ps, pr, os_, or_, bcs, bcr, bys, byr, bzs, bzr, ls,
):
    ZH, YN, KN, ZL = dims
    ZN = ZH * ZL
    PN = ZL // 2
    GN = 2 * ZH
    YK = YN * KN
    BEAMS = ZH * YK
    ROWS = STEPS * BEAMS
    s = lax.axis_index("sample")
    c = lax.axis_index("context")
    zh = lax.div(s, YK)
    y = lax.div(lax.rem(s, YK), KN)
    k = lax.rem(s, KN)
    zl = lax.div(c, XN)
    x = lax.rem(c, XN)
    z = zh * ZL + zl
    q = lax.div(zl, PN)
    p = lax.rem(zl, PN)
    width = hid.shape[1]

    def at(zh_=None, y_=None, k_=None, zl_=None, x_=None):
        zh_ = zh if zh_ is None else zh_
        y_ = y if y_ is None else y_
        k_ = k if k_ is None else k_
        zl_ = zl if zl_ is None else zl_
        x_ = x if x_ is None else x_
        return {"sample": zh_ * YK + y_ * KN + k_, "context": zl_ * XN + x_}

    def rc(src, dst, ssem, rsem, where):
        return pltpu.make_async_remote_copy(
            src_ref=src, dst_ref=dst, send_sem=ssem, recv_sem=rsem,
            device_id=where, device_id_type=MESH,
        )

    sends = []

    def push(cp):
        cp.start()
        sends.append(cp)
        return cp

    def x_of(o):
        return lax.rem(x + o + XN, XN)

    def y_of(o):
        return lax.rem(y + o + YN, YN)

    def p_of(o):
        return lax.rem(p + o + PN, PN)

    def half_at(m):
        zz = lax.rem(z + PN * m, ZN)
        zl_ = lax.rem(zz, ZL)
        return at(zh_=lax.div(zz, ZL), zl_=zl_), lax.div(zl_, PN)

    across = at(zl_=(1 - q) * PN + p)

    peers = [half_at(m)[0] for m in range(1, GN)]
    peers += [at(zl_=q * PN + p_of(o)) for o in range(1, PN)]
    peers += [at(x_=x_of(o)) for o in range(1, XN)]
    peers += [at(y_=y_of(o)) for o in range(1, YN)]
    if KN > 1:
        peers += [at(k_=1 - k)]
    if ZH == 1:
        assert GN == 2
    barrier = pltpu.get_barrier_semaphore()
    for peer in peers:
        pl.semaphore_signal(barrier, inc=1, device_id=peer, device_id_type=MESH)

    loc = [
        pltpu.make_async_copy(wout, woutv, ls.at[1]),
        pltpu.make_async_copy(kc, kcv, ls.at[2]),
        pltpu.make_async_copy(vc, vcv, ls.at[3]),
        pltpu.make_async_copy(pk, kall.at[x], ls.at[4]),
        pltpu.make_async_copy(pv, vall.at[x], ls.at[5]),
    ]
    for cp in loc:
        cp.start()

    J = width // 256
    TJ = a1.shape[1]
    hid_f = hid[...].astype(F32)
    mean_square = jnp.mean(hid_f * hid_f, axis=-1, keepdims=True)
    normed = hid_f * lax.rsqrt(mean_square + epsilon) * pre_gain[...].reshape(1, width).astype(F32)
    for part in range(2):
        for j in range(J):
            start = (part * J + j) * 128
            tilesf[part, pl.ds(j * STEPS, STEPS), :] = normed[:, start : start + 128]
        if TJ > J * STEPS:
            tilesf[part, pl.ds(J * STEPS, TJ - J * STEPS), :] = jnp.zeros((TJ - J * STEPS, 128), F32)
    tiles[...] = tilesf[...].astype(BF16)
    pl.semaphore_wait(barrier, len(peers))

    mine = lax.div(z, PN)
    a_copies = []
    for m in (2, 1, 3):
        if m < GN:
            where, q_to = half_at(m)
            a_copies.append(push(rc(tiles.at[q_to], a1.at[mine], as_.at[m], ar.at[m], where)))

    half = wq.shape[1] // 2
    w_src = [wq.at[:, pl.ds(0, half)], wq.at[:, pl.ds(half, half)], wk, wv]

    def w_copy(to):
        return rc(w_src[to], wz.at[p, x], ws.at[to], wr.at[x], at(x_=to))

    def w_local(to):
        return pltpu.make_async_copy(w_src[to], wz.at[p, x], ls.at[0])

    for to in range(XN):
        @pl.when(x != to)
        def _():
            w_copy(to).start()

        @pl.when(x == to)
        def _():
            w_local(to).start()

    kv_copies = {}
    positions = kall.shape[1]

    def send_prompt(which, o, start=0, count=positions):
        src, dst = ((pk, kall), (pv, vall))[which]
        span = pl.ds(start, count)
        sem = 0 if start == 0 else 1
        cp = rc(
            src.at[span], dst.at[x, span], ks.at[which, o, sem], kr.at[which, o, sem], at(x_=x_of(o))
        )
        kv_copies.setdefault(o, []).append(push(cp))

    for o in (1, 3):
        send_prompt(0, o)
    for o in (1, 3):
        send_prompt(1, o, 0, positions // 2)

    a1[mine] = tiles[q]
    for to in range(XN):
        @pl.when(x != to)
        def _():
            rc(w_src[to], wz.at[p, to], ws.at[to], wr.at[to], at(x_=to)).wait_recv()

        @pl.when(x == to)
        def _():
            w_local(to).wait()
    wz_copies = []
    for o in range(1, PN):
        wz_copies.append(
            push(rc(wz.at[p], wz.at[p], wzs.at[o], wzr.at[o], at(zl_=q * PN + p_of(o))))
        )
    for cp in a_copies:
        cp.wait_recv()

    for i in range(GN):
        a1f[pl.ds(i * TJ, TJ), :] = a1[i].astype(F32)
    own = (x * YN + y) * KN + k
    rest = jnp.zeros((BLOCK - STEPS * GN, 128), F32)
    for j in range(J):
        lines = [a1f[pl.ds(j * STEPS + t, GN, stride=TJ), :] for t in range(STEPS)]
        xb[own, :, pl.ds(j * 128, 128)] = jnp.concatenate(lines + [rest], axis=0).astype(BF16)

    cols = xb.shape[2] // 2

    def blk(ox, oy):
        return (x_of(-ox) * YN + y_of(-oy)) * KN + k

    def first(b):
        return xb.at[b, :, pl.ds(0, cols)]

    def second(b):
        return xb.at[b, :, pl.ds(cols, cols)]

    px, py, ry, rx, cc = {}, {}, {}, {}, {}

    def forward_y(ox):
        b = blk(ox, 0)
        for o in AROUND[: YN - 1]:
            py[ox, o] = push(rc(first(b), first(b), pys.at[ox, o], pyr.at[ox, o], at(y_=y_of(o))))

    def forward_x(oy):
        b = blk(0, oy)
        for o in AROUND:
            rx[oy, o] = push(rc(second(b), second(b), rxs.at[oy, o], rxr.at[oy, o], at(x_=x_of(o))))

    def to_core(ox, oy):
        if KN > 1:
            b = xb.at[blk(ox, oy)]
            cc[ox, oy] = push(rc(b, b, cs.at[ox, oy], cr.at[ox, oy], at(k_=1 - k)))

    y_around = [o for o in AROUND if o < YN]
    for o in AROUND:
        b = blk(0, 0)
        px[o] = push(rc(first(b), first(b), pxs.at[o], pxr.at[o], at(x_=x_of(o))))
        if o < YN:
            ry[o] = push(rc(second(b), second(b), rys.at[o], ryr.at[o], at(y_=y_of(o))))
    if YN > 1:
        for o in y_around:
            b = blk(0, 0)
            py[0, o] = push(rc(first(b), first(b), pys.at[0, o], pyr.at[0, o], at(y_=y_of(o))))
    forward_x(0)
    to_core(0, 0)
    for o in AROUND:
        px[o].wait_recv()
        for o2 in y_around:
            b = blk(o, 0)
            py[o, o2] = push(rc(first(b), first(b), pys.at[o, o2], pyr.at[o, o2], at(y_=y_of(o2))))
        if o < YN:
            ry[o].wait_recv()
            forward_x(o)

    def gather(ox):
        for oy in [0] + y_around:
            if oy > 0:
                py[ox, oy].wait_recv()
            if ox > 0:
                rx[oy, ox].wait_recv()
            if ox > 0 or oy > 0:
                to_core(ox, oy)

    r_copies = {}

    def project(ox):
        for oy in [0] + y_around:
            if KN > 1:
                cc[ox, oy].wait_recv()
        rows = xb[pl.ds(x_of(-ox) * YK, YK)].reshape(YK * BLOCK, xb.shape[2])
        yf[...] = dot(rows, wz[...].reshape(xb.shape[2], HEAD))
        for h in range(2):
            for t in range(STEPS):
                piece = [
                    yf[pl.ds(t * GN + i * 2 + h, YK, stride=BLOCK), :] for i in range(ZH)
                ]
                sred[ox, h, pl.ds(t * BEAMS, BEAMS), :] = jnp.concatenate(piece, axis=0).astype(BF16)
        r_copies[ox] = push(rc(sred.at[ox], rred.at[ox], rs.at[ox], rr.at[ox], across))

    for o in (1, 3):
        send_prompt(1, o, positions // 2, positions // 2)
    send_prompt(0, 2)
    send_prompt(1, 2)

    gather(0)
    for cp in wz_copies:
        cp.wait_recv()
    project(0)
    gather(1)
    gather(3)
    project(1)
    gather(2)
    project(3)
    project(2)

    NT = 2 * XN * STEPS
    at_row = iota((NT, 128), 0)
    place = jnp.zeros((NT, 128), jnp.int32)
    for h in range(2):
        for i in range(XN):
            for t in range(STEPS):
                here = lens[(h * PN + p) * XN + i] + (prompt_total + t)
                place = jnp.where(at_row == (h * XN + i) * STEPS + t, here, place)
    angles = place.astype(F32) * freq[...]
    turns = jnp.round(angles * (1.0 / TURN))
    angles = ((angles - turns * TURN_A) - turns * TURN_B) - turns * TURN_C
    lower = iota((NT, 128), 1) < HEAD // 2
    sines = jnp.sin(angles)
    plain = x == 3
    cos_rows[...] = jnp.where(plain, 1.0, jnp.cos(angles))
    sin_rows[...] = jnp.where(plain, 0.0, jnp.where(lower, -sines, sines))

    scale = jnp.where(x < 2, query_scale, 1.0).astype(F32)
    g_copies = {}
    for ox in (0,) + AROUND:
        xo = x_of(-ox)
        r_copies[ox].wait_recv()
        for h in range(2):
            total = sred[ox, h].astype(F32) + rred[ox, h].astype(F32)
            for t in range(STEPS):
                part = total[t * BEAMS : (t + 1) * BEAMS]
                row = pl.ds((h * XN + xo) * STEPS + t, 1)
                turned = part * cos_rows[row, :] + pltpu.roll(part, HEAD // 2, 1) * sin_rows[row, :]
                gf[ox, h, pl.ds(t * BEAMS, BEAMS), :] = (turned * scale).astype(BF16)
        if ox == 0:
            for h in range(2):
                g[h, x] = gf[0, h]
        else:
            g_copies[ox] = push(rc(gf.at[ox], g.at[:, x], gs.at[ox], gr.at[ox], at(x_=xo)))
    for ox in AROUND:
        g_copies[ox].wait_recv()

    q_copies = {}
    for o in range(1, PN):
        q_copies[o] = push(
            rc(g.at[:, pl.ds(0, 2)], qa.at[p], qs.at[o], qr.at[o], at(zl_=q * PN + p_of(o)))
        )
    for h in range(2):
        qa[p, h] = g[h, 0:2]

    for cp in loc[3:5]:
        cp.wait()
    QR = 2 * ROWS
    eye = iota((QR, 128), 0) == iota((QR, 128), 1)
    upper = iota((16, 128), 0) < 8

    def with_totals(line):
        coarse = line.astype(BF16).astype(F32)
        return jnp.where(upper, coarse, line - coarse).astype(BF16)

    p_copies = {}
    for o in [0] + [o for o in AROUND if o < PN]:
        if o > 0:
            q_copies[o].wait_recv()
        there = p_of(-o)
        queries = qa[there].reshape(2 * QR, HEAD)
        for ox in (0,) + AROUND:
            if o == 0 and ox > 0:
                for cp in kv_copies[ox]:
                    cp.wait_recv()
            xo = x_of(-ox)
            w = weights_of(dot_t(queries, kall[xo])).astype(BF16)
            part = dot(w, jnp.concatenate([vall[xo], jnp.ones((positions, HEAD), BF16)], axis=1))
            if ox == 0:
                acc[...] = part
            else:
                acc[...] += part
        for h in range(2):
            psend[o, h, pl.ds(0, QR), :] = acc[pl.ds(h * QR, QR), pl.ds(0, HEAD)].astype(BF16)
            totals = acc[pl.ds(h * QR, QR), pl.ds(HEAD, HEAD)]
            line = jnp.sum(jnp.where(eye, totals, 0.0), axis=0, keepdims=True)
            psend[o, h, pl.ds(QR, 16), :] = with_totals(line)
        if o > 0:
            p_copies[o] = push(
                rc(psend.at[o], precv.at[o], ps.at[o], pr.at[o], at(zl_=q * PN + there))
            )

    length = lens[c]
    for cp in loc[1:3]:
        cp.wait()
    never = jnp.int32(-1)
    for b in range(BEAMS):
        one = par[1, 0, b]
        two = par[2, 0, b]
        mid = par[1, 0, two]
        me = jnp.int32(b)
        chains = (
            (par[0, 0, b], me, never, never),
            (par[0, 0, one], one, me + BEAMS, never),
            (par[0, 0, mid], mid, two + BEAMS, me + 2 * BEAMS),
        )
        for t in range(STEPS):
            row = t * BEAMS + b
            ancv[pl.ds(row, 1), :] = jnp.full((1, 128), chains[t][0], jnp.int32)
            for u in range(STEPS):
                freshv[u, pl.ds(row, 1), :] = jnp.full((1, 128), chains[t][1 + u], jnp.int32)
    my_q = g[q, 0:2].reshape(QR, HEAD)
    SLOTS = kcv.shape[1]
    anc = ancv[:, :SLOTS]
    anc2 = jnp.concatenate([anc, anc], axis=0)
    in_use = iota((QR, SLOTS), 1) < length
    lane = iota((ROWS, ROWS), 1)
    seen = (lane == freshv[0, :, :ROWS]) | (lane == freshv[1, :, :ROWS]) | (lane == freshv[2, :, :ROWS])
    seen2 = jnp.concatenate([seen.astype(F32)] * 2, axis=0)
    fresh_w = weights_of(dot_t(my_q, g[q, 2])) * seen2
    suf_w = dot(fresh_w.astype(BF16), g[q, 3])
    suf_t = jnp.sum(fresh_w, axis=1, keepdims=True)
    for b in range(BEAMS):
        cached = weights_of(dot_t(my_q, kcv[b]))
        cached = jnp.where((anc2 == b) & in_use, cached, 0.0)
        suf_w = suf_w + dot(cached.astype(BF16), vcv[b])
        suf_t = suf_t + jnp.sum(cached, axis=1, keepdims=True)
    out_f[...] = g[q, 2:4]

    for h in range(2):
        both[h] = psend[0, h].astype(F32)
    for o in range(1, PN):
        p_copies[o].wait_recv()
        for h in range(2):
            both[h] += precv[o, h].astype(F32)
    theirs = both[1 - q]
    osend[pl.ds(0, QR), :] = theirs[:QR].astype(BF16)
    osend[pl.ds(QR, 16), :] = with_totals(theirs[QR : QR + 1] + theirs[QR + 8 : QR + 9])
    o_copy = push(rc(osend, orecv, os_, or_, across))
    ours = both[q]
    o_copy.wait_recv()
    ours = ours + orecv[...].astype(F32)
    line = ours[QR : QR + 1] + ours[QR + 8 : QR + 9]
    column = jnp.sum(jnp.where(eye, line, 0.0), axis=1, keepdims=True)
    attended = ((ours[:QR] + suf_w) / (column + suf_t)).astype(BF16)
    heads = jnp.concatenate([attended[:ROWS], attended[ROWS:]], axis=1)

    loc[0].wait()
    ordered = dot(perm[...], heads).astype(BF16)
    GRP = 4 * ZH
    HALF = YN * GRP
    wide = width // CHUNKS
    bc_copies = []
    for i in range(CHUNKS):
        for n in range(3):
            part = wide // 3
            at_col = pl.ds(i * wide + n * part, part)
            res = dot(ordered, woutv[:, at_col])
            for kk in range(KN):
                br[kk, i, :, pl.ds(n * part, part)] = res[kk * HALF : (kk + 1) * HALF]
        if KN > 1:
            csend[i] = br[1 - k, i].astype(BF16)
            bc_copies.append(push(rc(csend.at[i], crecv.at[i], bcs.at[i], bcr.at[i], at(k_=1 - k))))
    by_copies = {}
    for i in range(CHUNKS):
        total = br[k, i]
        if KN > 1:
            bc_copies[i].wait_recv()
            total = total + crecv[i].astype(F32)
        for yy in range(YN):
            s1[i, yy] = total[yy * GRP : (yy + 1) * GRP]
        for o in y_around:
            v = s1[i, y_of(o)]
            ysend[i, o] = jnp.concatenate([v[:, : wide // 2], v[:, wide // 2 :]], axis=0).astype(BF16)
            by_copies[i, o] = push(
                rc(ysend.at[i, o], yrecv.at[i, o], bys.at[i, o], byr.at[i, o], at(y_=y_of(o)))
            )
    bz_copies = []
    kept = []
    is_first = zh == 0
    quarter = wide // 4
    for i in range(CHUNKS):
        total = s1[i, y]
        for o in y_around:
            by_copies[i, o].wait_recv()
            v = yrecv[i, o].astype(F32)
            total = total + jnp.concatenate([v[:GRP], v[GRP:]], axis=1)
        if ZH > 1:
            other = jnp.where(is_first, total[4:8], total[0:4])
            zsend[i] = jnp.concatenate(
                [other[:, n * quarter : (n + 1) * quarter] for n in range(4)], axis=0
            ).astype(BF16)
            bz_copies.append(push(rc(zsend.at[i], zrecv.at[i], bzs.at[i], bzr.at[i], at(zh_=1 - zh))))
            kept.append(jnp.where(is_first, total[0:4], total[4:8]))
        else:
            kept.append(total[0:4])
    if ZH > 1:
        for i in range(CHUNKS):
            bz_copies[i].wait_recv()
            v = zrecv[i].astype(F32)
            kept[i] = kept[i] + jnp.concatenate([v[n * 4 : (n + 1) * 4] for n in range(4)], axis=1)
    square = sum(jnp.sum(v * v, axis=-1, keepdims=True) for v in kept) * (1.0 / width)
    factor = lax.rsqrt(square + epsilon)
    branch = jnp.concatenate(kept, axis=1) * factor
    out_h[...] = hid[...].astype(F32) + branch[:STEPS] * post_gain[...].reshape(1, width).astype(F32)

    for cp in sends:
        cp.wait_send()
    for to in range(XN):
        @pl.when(x != to)
        def _():
            w_copy(to).wait_send()


def cache_kernel(hid, fresh, kc, vc, par, lens, out_h, out_k, out_v, old, new, rows, ins, outs):
    beams, slots = kc.shape[0], kc.shape[1]
    length = lens[lax.axis_index("context")]
    loads = [pltpu.make_async_copy(src, old.at[i], ins.at[i]) for i, src in enumerate((kc, vc))]
    for cp in loads:
        cp.start()
    for t in range(STEPS):
        out_h[t, 0] = hid[t : t + 1]
    window = min(32, slots)
    start = pl.multiple_of(jnp.minimum(lax.div(length, 16) * 16, slots - window), 16)
    at_slot = iota((window, HEAD), 0) + start
    group = max(beams // 4, 1)
    stores = []
    for i, dst in enumerate((out_k, out_v)):
        rows[...] = fresh[i].astype(F32)
        loads[i].wait()
        for b in range(beams):
            two = par[2, 0, b]
            mid = par[1, 0, two]
            new[i, b] = old[i, par[0, 0, mid]]
            block = new[i, b, pl.ds(start, window), :].astype(F32)
            for u, row in enumerate((mid, two + beams, b + 2 * beams)):
                block = jnp.where(at_slot == length + u, rows[pl.ds(row, 1), :], block)
            new[i, b, pl.ds(start, window), :] = block.astype(BF16)
            if (b + 1) % group == 0:
                span = pl.ds(b + 1 - group, group)
                cp = pltpu.make_async_copy(new.at[i, span], dst.at[span], outs.at[i, b // group])
                cp.start()
                stores.append(cp)
    for cp in stores:
        cp.wait()


def order_matrix(dims):
    ZH, YN, KN, ZL = dims
    beams = ZH * YN * KN
    m = np.zeros((KN * YN * ZH * 4, STEPS * beams), np.float32)
    for kk in range(KN):
        for yy in range(YN):
            for hh in range(ZH):
                for t in range(STEPS):
                    m[((kk * YN + yy) * ZH + hh) * 4 + t, t * beams + (hh * YN + yy) * KN + kk] = 1.0
    return m


def body(
    dims,
    hidden_in,
    pre_gain,
    post_gain,
    w_query,
    key_projection_weight,
    value_projection_weight,
    w_out,
    prompt_rotated_keys,
    prompt_value_rows,
    suffix_key_cache,
    suffix_value_cache,
    parents,
    lengths,
):
    ZH, YN, KN, ZL = dims
    PN = ZL // 2
    GN = 2 * ZH
    YK = YN * KN
    beams = ZH * YK
    rows = STEPS * beams
    width = hidden_in.shape[3]
    slots = suffix_key_cache.shape[2]
    positions = prompt_rotated_keys.shape[0]
    prompt_total = positions * ZL * XN
    J = width // 256
    TJ = -(-(STEPS * J) // 16) * 16
    frequency = 1.0 / rope_base ** (np.arange(HEAD // 2) * 2.0 / HEAD)
    freq = jnp.asarray(np.concatenate([frequency, frequency])[None], F32)
    perm = jnp.asarray(order_matrix(dims), BF16)
    hbm = pl.BlockSpec(memory_space=pltpu.HBM)
    vmem = pl.BlockSpec(memory_space=pltpu.VMEM)
    smem = pl.BlockSpec(memory_space=pltpu.SMEM)
    wrows = w_query.shape[0]
    grp = 4 * ZH
    half = YN * grp
    wide = width // CHUNKS
    V = pltpu.VMEM
    D = pltpu.SemaphoreType.DMA
    scratch = [
        V((2, TJ, 128), BF16),
        V((2, TJ, 128), F32),
        V((2 * XN * STEPS, 128), F32),
        V((2 * XN * STEPS, 128), F32),
        V((GN, TJ, 128), BF16),
        V((GN * TJ, 128), F32),
        V((XN * YK, BLOCK, width // 2), BF16),
        V((PN, XN, wrows, HEAD), BF16),
        V((YK * BLOCK, HEAD), F32),
        V((XN, 2, rows, HEAD), BF16),
        V((XN, 2, rows, HEAD), BF16),
        V((2, XN, rows, HEAD), BF16),
        V((XN, 2, rows, HEAD), BF16),
        V((PN, 2, 2, rows, HEAD), BF16),
        V((XN, positions, HEAD), BF16),
        V((XN, positions, HEAD), BF16),
        V((4 * rows, 2 * HEAD), F32),
        V((PN, 2, 2 * rows + 16, HEAD), BF16),
        V((PN, 2, 2 * rows + 16, HEAD), BF16),
        V((2, 2 * rows + 16, HEAD), F32),
        V((2 * rows + 16, HEAD), BF16),
        V((2 * rows + 16, HEAD), BF16),
        V(w_out.shape, BF16),
        V((beams, slots, HEAD), BF16),
        V((beams, slots, HEAD), BF16),
        V((rows, 128), jnp.int32),
        V((STEPS, rows, 128), jnp.int32),
        V((KN, CHUNKS, half, wide), F32),
        V((CHUNKS, half, wide), BF16),
        V((CHUNKS, half, wide), BF16),
        V((CHUNKS, YN, grp, wide), F32),
        V((CHUNKS, YN, 2 * grp, wide // 2), BF16),
        V((CHUNKS, YN, 2 * grp, wide // 2), BF16),
        V((CHUNKS, 16, wide // 4), BF16),
        V((CHUNKS, 16, wide // 4), BF16),
        D((4,)), D((4,)), D((XN,)), D((XN,)), D((PN,)), D((PN,)), D((2, XN, 2)), D((2, XN, 2)),
        D((XN,)), D((XN,)), D((XN, 4)), D((XN, 4)), D((4,)), D((4,)), D((4, XN)), D((4, XN)),
        D((XN, 4)), D((XN, 4)), D((XN,)), D((XN,)), D((XN,)), D((XN,)), D((PN,)), D((PN,)),
        D((PN,)), D((PN,)), D, D, D((CHUNKS,)), D((CHUNKS,)), D((CHUNKS, 4)), D((CHUNKS, 4)),
        D((CHUNKS,)), D((CHUNKS,)), D((8,)),
    ]
    keys_in = suffix_key_cache.reshape(beams, slots, HEAD)
    values_in = suffix_value_cache.reshape(beams, slots, HEAD)
    hidden, fresh = pl.pallas_call(
        functools.partial(kernel, dims, prompt_total),
        out_shape=(
            jax.ShapeDtypeStruct((STEPS, width), F32),
            jax.ShapeDtypeStruct((2, rows, HEAD), BF16),
        ),
        in_specs=[vmem] * 5 + [hbm] * 8 + [smem] * 2,
        out_specs=(vmem, vmem),
        scratch_shapes=scratch,
        compiler_params=pltpu.CompilerParams(
            collective_id=0, has_side_effects=True, vmem_limit_bytes=63 * 1024 * 1024
        ),
    )(
        hidden_in.reshape(STEPS, width),
        pre_gain,
        post_gain,
        freq,
        perm,
        w_query,
        key_projection_weight,
        value_projection_weight,
        w_out,
        prompt_rotated_keys,
        prompt_value_rows,
        keys_in,
        values_in,
        parents,
        lengths,
    )
    hidden_out, keys_out, values_out = pl.pallas_call(
        cache_kernel,
        out_shape=(
            jax.ShapeDtypeStruct((STEPS, 1, 1, width), F32),
            jax.ShapeDtypeStruct((beams, slots, HEAD), BF16),
            jax.ShapeDtypeStruct((beams, slots, HEAD), BF16),
        ),
        in_specs=[vmem] * 2 + [hbm] * 2 + [smem] * 2,
        out_specs=(vmem, hbm, hbm),
        scratch_shapes=[
            V((2, beams, slots, HEAD), BF16),
            V((2, beams, slots, HEAD), BF16),
            V((rows, HEAD), F32),
            D((2,)),
            D((2, 4)),
        ],
        compiler_params=pltpu.CompilerParams(vmem_limit_bytes=63 * 1024 * 1024),
    )(hidden, fresh, keys_in, values_in, parents, lengths)
    return (
        hidden_out,
        keys_out.reshape(1, beams, slots, HEAD),
        values_out.reshape(1, beams, slots, HEAD),
    )


def solution(mesh, dims=(2, 4, 2, 8)):
    placed = (
        P(None, "context", "sample", None),
        P(),
        P(),
        P("context", "sample"),
        P("context", "sample"),
        P("context", "sample"),
        P("sample", None),
        P("context", "sample"),
        P("context", "sample"),
        P("context", None, None, "sample"),
        P("context", None, None, "sample"),
        P(None, "context", None),
        P(),
    )
    return jax.shard_map(
        functools.partial(body, dims),
        mesh=mesh,
        in_specs=placed,
        out_specs=(
            P(None, "context", "sample", None),
            P("context", None, None, "sample"),
            P("context", None, None, "sample"),
        ),
        check_vma=False,
    )
```

```python
import functools

import jax
import jax.numpy as jnp
import numpy as np
from jax import lax
from jax.experimental import pallas as pl
from jax.experimental.pallas import tpu as pltpu
from jax.sharding import PartitionSpec as P

HEAD = 128
STEPS = 3
XN = 4
BLOCK = 16
CHUNKS = 3

epsilon = 1e-06
query_scale = 144.0 ** (-0.5)
rope_base = 10000.0
logit_cap = 50.0
TURN = 2 * np.pi
TURN_A = 6.28125
TURN_B = float(np.float32(np.round((TURN - TURN_A) * 2.0**20) / 2.0**20))
TURN_C = float(TURN - TURN_A - TURN_B)
MESH = pl.DeviceIdType.MESH
F32 = jnp.float32
BF16 = jnp.bfloat16
AROUND = (1, 3, 2)


def weights_of(scores):
    return jnp.exp(logit_cap * jnp.tanh(scores * (1.0 / logit_cap)))


def dot_t(a, b):
    return lax.dot_general(a, b, (((1,), (1,)), ((), ())), preferred_element_type=F32)


def dot(a, b):
    return jnp.dot(a, b, preferred_element_type=F32)


def iota(shape, axis):
    return lax.broadcasted_iota(jnp.int32, shape, axis)


def kernel(
    dims, prompt_total,
    hid_in, pre_in, post_in, freq_in, perm_in, wq, wk, wv, wout, pk, pv, kc, vc, par_in, lens_in,
    out_h, out_f,
    hid, pre_gain, post_gain, freq, perm, par, lens,
    tiles, tilesf, cos_rows, sin_rows, a1, a1f, xb, wz, yf, sred, rred, g, gf, qa, kall, vall, acc,
    psend, precv, both, osend, orecv, woutv, kcv, vcv, ancv, freshv, br, csend, crecv, s1, ysend,
    yrecv, zsend, zrecv,
    as_, ar, ws, wr, wzs, wzr, ks, kr, pxs, pxr, pys, pyr, rys, ryr, rxs, rxr, cs, cr, rs, rr, gs,
    gr, qs, qr, ps, pr, os_, or_, bcs, bcr, bys, byr, bzs, bzr, ls,
):
    ZH, YN, KN, ZL = dims
    ZN = ZH * ZL
    PN = ZL // 2
    GN = 2 * ZH
    YK = YN * KN
    BEAMS = ZH * YK
    ROWS = STEPS * BEAMS
    s = lax.axis_index("sample")
    c = lax.axis_index("context")
    zh = lax.div(s, YK)
    y = lax.div(lax.rem(s, YK), KN)
    k = lax.rem(s, KN)
    zl = lax.div(c, XN)
    x = lax.rem(c, XN)
    z = zh * ZL + zl
    q = lax.div(zl, PN)
    p = lax.rem(zl, PN)
    width = hid_in.shape[1]

    def at(zh_=None, y_=None, k_=None, zl_=None, x_=None):
        zh_ = zh if zh_ is None else zh_
        y_ = y if y_ is None else y_
        k_ = k if k_ is None else k_
        zl_ = zl if zl_ is None else zl_
        x_ = x if x_ is None else x_
        return {"sample": zh_ * YK + y_ * KN + k_, "context": zl_ * XN + x_}

    def rc(src, dst, ssem, rsem, where):
        return pltpu.make_async_remote_copy(
            src_ref=src, dst_ref=dst, send_sem=ssem, recv_sem=rsem,
            device_id=where, device_id_type=MESH,
        )

    sends = []

    def push(cp):
        cp.start()
        sends.append(cp)
        return cp

    def x_of(o):
        return lax.rem(x + o + XN, XN)

    def y_of(o):
        return lax.rem(y + o + YN, YN)

    def p_of(o):
        return lax.rem(p + o + PN, PN)

    def half_at(m):
        zz = lax.rem(z + PN * m, ZN)
        zl_ = lax.rem(zz, ZL)
        return at(zh_=lax.div(zz, ZL), zl_=zl_), lax.div(zl_, PN)

    across = at(zl_=(1 - q) * PN + p)

    peers = [half_at(m)[0] for m in range(1, GN)]
    peers += [at(zl_=q * PN + p_of(o)) for o in range(1, PN)]
    peers += [at(x_=x_of(o)) for o in range(1, XN)]
    peers += [at(y_=y_of(o)) for o in range(1, YN)]
    if KN > 1:
        peers += [at(k_=1 - k)]
    if ZH == 1:
        assert GN == 2
    barrier = pltpu.get_barrier_semaphore()
    for peer in peers:
        pl.semaphore_signal(barrier, inc=1, device_id=peer, device_id_type=MESH)

    early = [pltpu.make_async_copy(hid_in, hid, ls.at[6]), pltpu.make_async_copy(pre_in, pre_gain, ls.at[7])]
    late = [
        pltpu.make_async_copy(src, dst, ls.at[8 + i])
        for i, (src, dst) in enumerate(
            ((post_in, post_gain), (freq_in, freq), (perm_in, perm), (par_in, par), (lens_in, lens))
        )
    ]
    for cp in early + late:
        cp.start()
    loc = [
        pltpu.make_async_copy(wout, woutv, ls.at[1]),
        pltpu.make_async_copy(kc, kcv, ls.at[2]),
        pltpu.make_async_copy(vc, vcv, ls.at[3]),
        pltpu.make_async_copy(pk, kall.at[x], ls.at[4]),
        pltpu.make_async_copy(pv, vall.at[x], ls.at[5]),
    ]
    for cp in loc:
        cp.start()

    J = width // 256
    TJ = a1.shape[1]
    for cp in early:
        cp.wait()
    hid_f = hid[...].astype(F32)
    mean_square = jnp.mean(hid_f * hid_f, axis=-1, keepdims=True)
    normed = hid_f * lax.rsqrt(mean_square + epsilon) * pre_gain[...].reshape(1, width).astype(F32)
    for part in range(2):
        for j in range(J):
            start = (part * J + j) * 128
            tilesf[part, pl.ds(j * STEPS, STEPS), :] = normed[:, start : start + 128]
        if TJ > J * STEPS:
            tilesf[part, pl.ds(J * STEPS, TJ - J * STEPS), :] = jnp.zeros((TJ - J * STEPS, 128), F32)
    tiles[...] = tilesf[...].astype(BF16)
    pl.semaphore_wait(barrier, len(peers))

    mine = lax.div(z, PN)
    a_copies = []
    for m in (2, 1, 3):
        if m < GN:
            where, q_to = half_at(m)
            a_copies.append(push(rc(tiles.at[q_to], a1.at[mine], as_.at[m], ar.at[m], where)))

    half = wq.shape[1] // 2
    w_src = [wq.at[:, pl.ds(0, half)], wq.at[:, pl.ds(half, half)], wk, wv]

    def w_copy(to):
        return rc(w_src[to], wz.at[p, x], ws.at[to], wr.at[x], at(x_=to))

    def w_local(to):
        return pltpu.make_async_copy(w_src[to], wz.at[p, x], ls.at[0])

    for to in range(XN):
        @pl.when(x != to)
        def _():
            w_copy(to).start()

        @pl.when(x == to)
        def _():
            w_local(to).start()

    kv_copies = {}
    positions = kall.shape[1]

    def send_prompt(which, o, part):
        src, dst = ((pk, kall), (pv, vall))[which]
        span = pl.ds(part * (positions // 2), positions // 2)
        cp = rc(
            src.at[span], dst.at[x, span], ks.at[which, o, part], kr.at[which, o, part], at(x_=x_of(o))
        )
        kv_copies[which, o, part] = push(cp)

    def pass_prompt(which, o):
        part = 0 if o == 1 else 1
        kv_copies.pop((which, o, part)).wait_recv()
        block = (kall, vall)[which].at[x_of(-o), pl.ds(part * (positions // 2), positions // 2)]
        cp = rc(block, block, ks.at[which, 2, part], kr.at[which, 2, part], at(x_=x_of(o)))
        kv_copies[which, 2, part] = push(cp)

    send_prompt(0, 1, 0)
    send_prompt(0, 3, 1)
    send_prompt(1, 1, 0)
    send_prompt(1, 3, 1)
    send_prompt(0, 1, 1)
    send_prompt(0, 3, 0)

    a1[mine] = tiles[q]
    for to in range(XN):
        @pl.when(x != to)
        def _():
            rc(w_src[to], wz.at[p, to], ws.at[to], wr.at[to], at(x_=to)).wait_recv()

        @pl.when(x == to)
        def _():
            w_local(to).wait()
    wz_copies = []
    for o in range(1, PN):
        wz_copies.append(
            push(rc(wz.at[p], wz.at[p], wzs.at[o], wzr.at[o], at(zl_=q * PN + p_of(o))))
        )
    for cp in a_copies:
        cp.wait_recv()

    for i in range(GN):
        a1f[pl.ds(i * TJ, TJ), :] = a1[i].astype(F32)
    own = (x * YN + y) * KN + k
    rest = jnp.zeros((BLOCK - STEPS * GN, 128), F32)
    for j in range(J):
        lines = [a1f[pl.ds(j * STEPS + t, GN, stride=TJ), :] for t in range(STEPS)]
        xb[own, :, pl.ds(j * 128, 128)] = jnp.concatenate(lines + [rest], axis=0).astype(BF16)

    cols = xb.shape[2] // 2

    def blk(ox, oy):
        return (x_of(-ox) * YN + y_of(-oy)) * KN + k

    def first(b):
        return xb.at[b, :, pl.ds(0, cols)]

    def second(b):
        return xb.at[b, :, pl.ds(cols, cols)]

    px, py, ry, rx, cc = {}, {}, {}, {}, {}

    def forward_y(ox):
        b = blk(ox, 0)
        for o in AROUND[: YN - 1]:
            py[ox, o] = push(rc(first(b), first(b), pys.at[ox, o], pyr.at[ox, o], at(y_=y_of(o))))

    def forward_x(oy):
        b = blk(0, oy)
        for o in AROUND:
            rx[oy, o] = push(rc(second(b), second(b), rxs.at[oy, o], rxr.at[oy, o], at(x_=x_of(o))))

    def to_core(ox, oy):
        if KN > 1:
            b = xb.at[blk(ox, oy)]
            cc[ox, oy] = push(rc(b, b, cs.at[ox, oy], cr.at[ox, oy], at(k_=1 - k)))

    y_around = [o for o in AROUND if o < YN]
    for o in AROUND:
        b = blk(0, 0)
        px[o] = push(rc(first(b), first(b), pxs.at[o], pxr.at[o], at(x_=x_of(o))))
        if o < YN:
            ry[o] = push(rc(second(b), second(b), rys.at[o], ryr.at[o], at(y_=y_of(o))))
    if YN > 1:
        for o in y_around:
            b = blk(0, 0)
            py[0, o] = push(rc(first(b), first(b), pys.at[0, o], pyr.at[0, o], at(y_=y_of(o))))
    forward_x(0)
    to_core(0, 0)
    for o in AROUND:
        px[o].wait_recv()
        for o2 in y_around:
            b = blk(o, 0)
            py[o, o2] = push(rc(first(b), first(b), pys.at[o, o2], pyr.at[o, o2], at(y_=y_of(o2))))
        if o < YN:
            ry[o].wait_recv()
            forward_x(o)

    def gather(ox):
        for oy in [0] + y_around:
            if oy > 0:
                py[ox, oy].wait_recv()
            if ox > 0:
                rx[oy, ox].wait_recv()
            if ox > 0 or oy > 0:
                to_core(ox, oy)

    r_copies = {}

    def project(ox):
        for oy in [0] + y_around:
            if KN > 1:
                cc[ox, oy].wait_recv()
        rows = xb[pl.ds(x_of(-ox) * YK, YK)].reshape(YK * BLOCK, xb.shape[2])
        yf[...] = dot(rows, wz[...].reshape(xb.shape[2], HEAD))
        for h in range(2):
            for t in range(STEPS):
                piece = [
                    yf[pl.ds(t * GN + i * 2 + h, YK, stride=BLOCK), :] for i in range(ZH)
                ]
                sred[ox, h, pl.ds(t * BEAMS, BEAMS), :] = jnp.concatenate(piece, axis=0).astype(BF16)
        r_copies[ox] = push(rc(sred.at[ox], rred.at[ox], rs.at[ox], rr.at[ox], across))

    for which in range(2):
        for o in (1, 3):
            pass_prompt(which, o)
    send_prompt(1, 1, 1)
    send_prompt(1, 3, 0)

    gather(0)
    for cp in wz_copies:
        cp.wait_recv()
    project(0)
    gather(1)
    gather(3)
    project(1)
    gather(2)
    project(3)
    project(2)

    for cp in late:
        cp.wait()
    NT = 2 * XN * STEPS
    at_row = iota((NT, 128), 0)
    place = jnp.zeros((NT, 128), jnp.int32)
    for h in range(2):
        for i in range(XN):
            for t in range(STEPS):
                here = lens[(h * PN + p) * XN + i] + (prompt_total + t)
                place = jnp.where(at_row == (h * XN + i) * STEPS + t, here, place)
    angles = place.astype(F32) * freq[...]
    turns = jnp.round(angles * (1.0 / TURN))
    angles = ((angles - turns * TURN_A) - turns * TURN_B) - turns * TURN_C
    lower = iota((NT, 128), 1) < HEAD // 2
    sines = jnp.sin(angles)
    plain = x == 3
    cos_rows[...] = jnp.where(plain, 1.0, jnp.cos(angles))
    sin_rows[...] = jnp.where(plain, 0.0, jnp.where(lower, -sines, sines))

    scale = jnp.where(x < 2, query_scale, 1.0).astype(F32)
    g_copies = {}
    for ox in (0,) + AROUND:
        xo = x_of(-ox)
        r_copies[ox].wait_recv()
        for h in range(2):
            total = sred[ox, h].astype(F32) + rred[ox, h].astype(F32)
            for t in range(STEPS):
                part = total[t * BEAMS : (t + 1) * BEAMS]
                row = pl.ds((h * XN + xo) * STEPS + t, 1)
                turned = part * cos_rows[row, :] + pltpu.roll(part, HEAD // 2, 1) * sin_rows[row, :]
                gf[ox, h, pl.ds(t * BEAMS, BEAMS), :] = (turned * scale).astype(BF16)
        if ox == 0:
            for h in range(2):
                g[h, x] = gf[0, h]
        else:
            g_copies[ox] = push(rc(gf.at[ox], g.at[:, x], gs.at[ox], gr.at[ox], at(x_=xo)))
    for ox in AROUND:
        g_copies[ox].wait_recv()

    q_copies = {}
    for o in range(1, PN):
        q_copies[o] = push(
            rc(g.at[:, pl.ds(0, 2)], qa.at[p], qs.at[o], qr.at[o], at(zl_=q * PN + p_of(o)))
        )
    for h in range(2):
        qa[p, h] = g[h, 0:2]

    for cp in loc[3:5]:
        cp.wait()
    QR = 2 * ROWS
    eye = iota((QR, 128), 0) == iota((QR, 128), 1)
    upper = iota((16, 128), 0) < 8

    def with_totals(line):
        coarse = line.astype(BF16).astype(F32)
        return jnp.where(upper, coarse, line - coarse).astype(BF16)

    p_copies = {}
    for o in [0] + [o for o in AROUND if o < PN]:
        if o > 0:
            q_copies[o].wait_recv()
        there = p_of(-o)
        queries = qa[there].reshape(2 * QR, HEAD)
        for ox in (0,) + AROUND:
            if o == 0 and ox > 0:
                for key, cp in kv_copies.items():
                    if key[1] == ox:
                        cp.wait_recv()
            xo = x_of(-ox)
            w = weights_of(dot_t(queries, kall[xo])).astype(BF16)
            part = dot(w, jnp.concatenate([vall[xo], jnp.ones((positions, HEAD), BF16)], axis=1))
            if ox == 0:
                acc[...] = part
            else:
                acc[...] += part
        for h in range(2):
            psend[o, h, pl.ds(0, QR), :] = acc[pl.ds(h * QR, QR), pl.ds(0, HEAD)].astype(BF16)
            totals = acc[pl.ds(h * QR, QR), pl.ds(HEAD, HEAD)]
            line = jnp.sum(jnp.where(eye, totals, 0.0), axis=0, keepdims=True)
            psend[o, h, pl.ds(QR, 16), :] = with_totals(line)
        if o > 0:
            p_copies[o] = push(
                rc(psend.at[o], precv.at[o], ps.at[o], pr.at[o], at(zl_=q * PN + there))
            )

    length = lens[c]
    for cp in loc[1:3]:
        cp.wait()
    never = jnp.int32(-1)
    for b in range(BEAMS):
        one = par[1, 0, b]
        two = par[2, 0, b]
        mid = par[1, 0, two]
        me = jnp.int32(b)
        chains = (
            (par[0, 0, b], me, never, never),
            (par[0, 0, one], one, me + BEAMS, never),
            (par[0, 0, mid], mid, two + BEAMS, me + 2 * BEAMS),
        )
        for t in range(STEPS):
            row = t * BEAMS + b
            ancv[pl.ds(row, 1), :] = jnp.full((1, 128), chains[t][0], jnp.int32)
            for u in range(STEPS):
                freshv[u, pl.ds(row, 1), :] = jnp.full((1, 128), chains[t][1 + u], jnp.int32)
    my_q = g[q, 0:2].reshape(QR, HEAD)
    SLOTS = kcv.shape[1]
    anc = ancv[:, :SLOTS]
    anc2 = jnp.concatenate([anc, anc], axis=0)
    in_use = iota((QR, SLOTS), 1) < length
    lane = iota((ROWS, ROWS), 1)
    seen = (lane == freshv[0, :, :ROWS]) | (lane == freshv[1, :, :ROWS]) | (lane == freshv[2, :, :ROWS])
    seen2 = jnp.concatenate([seen.astype(F32)] * 2, axis=0)
    fresh_w = weights_of(dot_t(my_q, g[q, 2])) * seen2
    suf_w = dot(fresh_w.astype(BF16), g[q, 3])
    suf_t = jnp.sum(fresh_w, axis=1, keepdims=True)
    for b in range(BEAMS):
        cached = weights_of(dot_t(my_q, kcv[b]))
        cached = jnp.where((anc2 == b) & in_use, cached, 0.0)
        suf_w = suf_w + dot(cached.astype(BF16), vcv[b])
        suf_t = suf_t + jnp.sum(cached, axis=1, keepdims=True)
    out_f[...] = g[q, 2:4]

    for h in range(2):
        both[h] = psend[0, h].astype(F32)
    for o in range(1, PN):
        p_copies[o].wait_recv()
        for h in range(2):
            both[h] += precv[o, h].astype(F32)
    theirs = both[1 - q]
    osend[pl.ds(0, QR), :] = theirs[:QR].astype(BF16)
    osend[pl.ds(QR, 16), :] = with_totals(theirs[QR : QR + 1] + theirs[QR + 8 : QR + 9])
    o_copy = push(rc(osend, orecv, os_, or_, across))
    ours = both[q]
    o_copy.wait_recv()
    ours = ours + orecv[...].astype(F32)
    line = ours[QR : QR + 1] + ours[QR + 8 : QR + 9]
    column = jnp.sum(jnp.where(eye, line, 0.0), axis=1, keepdims=True)
    attended = ((ours[:QR] + suf_w) / (column + suf_t)).astype(BF16)
    heads = jnp.concatenate([attended[:ROWS], attended[ROWS:]], axis=1)

    loc[0].wait()
    ordered = dot(perm[...], heads).astype(BF16)
    GRP = 4 * ZH
    HALF = YN * GRP
    wide = width // CHUNKS
    bc_copies = []
    by_copies = {}

    def project_out(i):
        for n in range(3):
            part = wide // 3
            at_col = pl.ds(i * wide + n * part, part)
            res = dot(ordered, woutv[:, at_col])
            for kk in range(KN):
                br[kk, i, :, pl.ds(n * part, part)] = res[kk * HALF : (kk + 1) * HALF]
        if KN > 1:
            csend[i] = br[1 - k, i].astype(BF16)
            bc_copies.append(push(rc(csend.at[i], crecv.at[i], bcs.at[i], bcr.at[i], at(k_=1 - k))))

    def over_y(i):
        total = br[k, i]
        if KN > 1:
            bc_copies[i].wait_recv()
            total = total + crecv[i].astype(F32)
        for yy in range(YN):
            s1[i, yy] = total[yy * GRP : (yy + 1) * GRP]
        for o in reversed(y_around):
            v = s1[i, y_of(o)]
            ysend[i, o] = jnp.concatenate([v[:, : wide // 2], v[:, wide // 2 :]], axis=0).astype(BF16)
            by_copies[i, o] = push(
                rc(ysend.at[i, o], yrecv.at[i, o], bys.at[i, o], byr.at[i, o], at(y_=y_of(o)))
            )

    project_out(0)
    for i in range(1, CHUNKS):
        project_out(i)
        over_y(i - 1)
    over_y(CHUNKS - 1)
    bz_copies = []
    kept = []
    is_first = zh == 0
    quarter = wide // 4
    for i in range(CHUNKS):
        total = s1[i, y]
        for o in y_around:
            by_copies[i, o].wait_recv()
            v = yrecv[i, o].astype(F32)
            total = total + jnp.concatenate([v[:GRP], v[GRP:]], axis=1)
        if ZH > 1:
            other = jnp.where(is_first, total[4:8], total[0:4])
            zsend[i] = jnp.concatenate(
                [other[:, n * quarter : (n + 1) * quarter] for n in range(4)], axis=0
            ).astype(BF16)
            bz_copies.append(push(rc(zsend.at[i], zrecv.at[i], bzs.at[i], bzr.at[i], at(zh_=1 - zh))))
            kept.append(jnp.where(is_first, total[0:4], total[4:8]))
        else:
            kept.append(total[0:4])
    if ZH > 1:
        for i in range(CHUNKS):
            bz_copies[i].wait_recv()
            v = zrecv[i].astype(F32)
            kept[i] = kept[i] + jnp.concatenate([v[n * 4 : (n + 1) * 4] for n in range(4)], axis=1)
    square = sum(jnp.sum(v * v, axis=-1, keepdims=True) for v in kept) * (1.0 / width)
    factor = lax.rsqrt(square + epsilon)
    branch = jnp.concatenate(kept, axis=1) * factor
    result = hid[...].astype(F32) + branch[:STEPS] * post_gain[...].reshape(1, width).astype(F32)
    for t in range(STEPS):
        out_h[t, 0] = result[t : t + 1]

    for cp in sends:
        cp.wait_send()
    for to in range(XN):
        @pl.when(x != to)
        def _():
            w_copy(to).wait_send()


def cache_kernel(
    hid, fresh, kc, vc, par, lens, out_h, out_k, out_v, hidv, freshv, old, new, rows, ins, outs, sem
):
    beams, slots = kc.shape[0], kc.shape[1]
    loads = [pltpu.make_async_copy(src, old.at[i], ins.at[i]) for i, src in enumerate((kc, vc))]
    loads.append(pltpu.make_async_copy(fresh, freshv, ins.at[2]))
    loads.append(pltpu.make_async_copy(hid, hidv, ins.at[3]))
    for i in (2, 0, 1, 3):
        loads[i].start()
    length = lens[lax.axis_index("context")]
    window = min(32, slots)
    start = pl.multiple_of(jnp.minimum(lax.div(length, 16) * 16, slots - window), 16)
    at_slot = iota((window, HEAD), 0) + start
    group = max(beams // 4, 1)
    stores = []
    loads[2].wait()
    for i, dst in enumerate((out_k, out_v)):
        rows[...] = freshv[i].astype(F32)
        loads[i].wait()
        for b in range(beams):
            two = par[2, 0, b]
            mid = par[1, 0, two]
            new[i, b] = old[i, par[0, 0, mid]]
            block = new[i, b, pl.ds(start, window), :].astype(F32)
            for u, row in enumerate((mid, two + beams, b + 2 * beams)):
                block = jnp.where(at_slot == length + u, rows[pl.ds(row, 1), :], block)
            new[i, b, pl.ds(start, window), :] = block.astype(BF16)
            if (b + 1) % group == 0:
                span = pl.ds(b + 1 - group, group)
                cp = pltpu.make_async_copy(new.at[i, span], dst.at[span], outs.at[i, b // group])
                cp.start()
                stores.append(cp)
        if i == 0:
            loads[3].wait()
            cp = pltpu.make_async_copy(hidv, out_h, sem)
            cp.start()
            stores.append(cp)
    for cp in stores:
        cp.wait()


def order_matrix(dims):
    ZH, YN, KN, ZL = dims
    beams = ZH * YN * KN
    m = np.zeros((KN * YN * ZH * 4, STEPS * beams), np.float32)
    for kk in range(KN):
        for yy in range(YN):
            for hh in range(ZH):
                for t in range(STEPS):
                    m[((kk * YN + yy) * ZH + hh) * 4 + t, t * beams + (hh * YN + yy) * KN + kk] = 1.0
    return m


def body(
    dims,
    hidden_in,
    pre_gain,
    post_gain,
    w_query,
    key_projection_weight,
    value_projection_weight,
    w_out,
    prompt_rotated_keys,
    prompt_value_rows,
    suffix_key_cache,
    suffix_value_cache,
    parents,
    lengths,
):
    ZH, YN, KN, ZL = dims
    PN = ZL // 2
    GN = 2 * ZH
    YK = YN * KN
    beams = ZH * YK
    rows = STEPS * beams
    width = hidden_in.shape[3]
    slots = suffix_key_cache.shape[2]
    positions = prompt_rotated_keys.shape[0]
    prompt_total = positions * ZL * XN
    J = width // 256
    TJ = -(-(STEPS * J) // 16) * 16
    frequency = 1.0 / rope_base ** (np.arange(HEAD // 2) * 2.0 / HEAD)
    freq = jnp.asarray(np.concatenate([frequency, frequency])[None], F32)
    perm = jnp.asarray(order_matrix(dims), BF16)
    hbm = pl.BlockSpec(memory_space=pltpu.HBM)
    vmem = pl.BlockSpec(memory_space=pltpu.VMEM)
    smem = pl.BlockSpec(memory_space=pltpu.SMEM)
    wrows = w_query.shape[0]
    grp = 4 * ZH
    half = YN * grp
    wide = width // CHUNKS
    V = pltpu.VMEM
    D = pltpu.SemaphoreType.DMA
    scratch = [
        V((STEPS, width), BF16),
        V((width,), BF16),
        V((width,), BF16),
        V((1, HEAD), F32),
        V(perm.shape, BF16),
        pltpu.SMEM(parents.shape, jnp.int32),
        pltpu.SMEM(lengths.shape, jnp.int32),
        V((2, TJ, 128), BF16),
        V((2, TJ, 128), F32),
        V((2 * XN * STEPS, 128), F32),
        V((2 * XN * STEPS, 128), F32),
        V((GN, TJ, 128), BF16),
        V((GN * TJ, 128), F32),
        V((XN * YK, BLOCK, width // 2), BF16),
        V((PN, XN, wrows, HEAD), BF16),
        V((YK * BLOCK, HEAD), F32),
        V((XN, 2, rows, HEAD), BF16),
        V((XN, 2, rows, HEAD), BF16),
        V((2, XN, rows, HEAD), BF16),
        V((XN, 2, rows, HEAD), BF16),
        V((PN, 2, 2, rows, HEAD), BF16),
        V((XN, positions, HEAD), BF16),
        V((XN, positions, HEAD), BF16),
        V((4 * rows, 2 * HEAD), F32),
        V((PN, 2, 2 * rows + 16, HEAD), BF16),
        V((PN, 2, 2 * rows + 16, HEAD), BF16),
        V((2, 2 * rows + 16, HEAD), F32),
        V((2 * rows + 16, HEAD), BF16),
        V((2 * rows + 16, HEAD), BF16),
        V(w_out.shape, BF16),
        V((beams, slots, HEAD), BF16),
        V((beams, slots, HEAD), BF16),
        V((rows, 128), jnp.int32),
        V((STEPS, rows, 128), jnp.int32),
        V((KN, CHUNKS, half, wide), F32),
        V((CHUNKS, half, wide), BF16),
        V((CHUNKS, half, wide), BF16),
        V((CHUNKS, YN, grp, wide), F32),
        V((CHUNKS, YN, 2 * grp, wide // 2), BF16),
        V((CHUNKS, YN, 2 * grp, wide // 2), BF16),
        V((CHUNKS, 16, wide // 4), BF16),
        V((CHUNKS, 16, wide // 4), BF16),
        D((4,)), D((4,)), D((XN,)), D((XN,)), D((PN,)), D((PN,)), D((2, XN, 2)), D((2, XN, 2)),
        D((XN,)), D((XN,)), D((XN, 4)), D((XN, 4)), D((4,)), D((4,)), D((4, XN)), D((4, XN)),
        D((XN, 4)), D((XN, 4)), D((XN,)), D((XN,)), D((XN,)), D((XN,)), D((PN,)), D((PN,)),
        D((PN,)), D((PN,)), D, D, D((CHUNKS,)), D((CHUNKS,)), D((CHUNKS, 4)), D((CHUNKS, 4)),
        D((CHUNKS,)), D((CHUNKS,)), D((16,)),
    ]
    keys_in = suffix_key_cache.reshape(beams, slots, HEAD)
    values_in = suffix_value_cache.reshape(beams, slots, HEAD)
    hidden, fresh = pl.pallas_call(
        functools.partial(kernel, dims, prompt_total),
        out_shape=(
            jax.ShapeDtypeStruct((STEPS, 1, 1, width), F32),
            jax.ShapeDtypeStruct((2, rows, HEAD), BF16),
        ),
        in_specs=[hbm] * 15,
        out_specs=(vmem, vmem),
        scratch_shapes=scratch,
        compiler_params=pltpu.CompilerParams(
            collective_id=0, has_side_effects=True, vmem_limit_bytes=63 * 1024 * 1024
        ),
    )(
        hidden_in.reshape(STEPS, width),
        pre_gain,
        post_gain,
        freq,
        perm,
        w_query,
        key_projection_weight,
        value_projection_weight,
        w_out,
        prompt_rotated_keys,
        prompt_value_rows,
        keys_in,
        values_in,
        parents,
        lengths,
    )
    hidden_out, keys_out, values_out = pl.pallas_call(
        cache_kernel,
        out_shape=(
            jax.ShapeDtypeStruct((STEPS, 1, 1, width), F32),
            jax.ShapeDtypeStruct((beams, slots, HEAD), BF16),
            jax.ShapeDtypeStruct((beams, slots, HEAD), BF16),
        ),
        in_specs=[hbm] * 4 + [smem] * 2,
        out_specs=(hbm, hbm, hbm),
        scratch_shapes=[
            V((STEPS, 1, 1, width), F32),
            V((2, rows, HEAD), BF16),
            V((2, beams, slots, HEAD), BF16),
            V((2, beams, slots, HEAD), BF16),
            V((rows, HEAD), F32),
            D((4,)),
            D((2, 4)),
            D,
        ],
        compiler_params=pltpu.CompilerParams(vmem_limit_bytes=63 * 1024 * 1024),
    )(hidden, fresh, keys_in, values_in, parents, lengths)
    return (
        hidden_out,
        keys_out.reshape(1, beams, slots, HEAD),
        values_out.reshape(1, beams, slots, HEAD),
    )


def solution(mesh, dims=(2, 4, 2, 8)):
    placed = (
        P(None, "context", "sample", None),
        P(),
        P(),
        P("context", "sample"),
        P("context", "sample"),
        P("context", "sample"),
        P("sample", None),
        P("context", "sample"),
        P("context", "sample"),
        P("context", None, None, "sample"),
        P("context", None, None, "sample"),
        P(None, "context", None),
        P(),
    )
    return jax.shard_map(
        functools.partial(body, dims),
        mesh=mesh,
        in_specs=placed,
        out_specs=(
            P(None, "context", "sample", None),
            P("context", None, None, "sample"),
            P("context", None, None, "sample"),
        ),
        check_vma=False,
    )
```

```python
import functools

import jax
import jax.numpy as jnp
import numpy as np
from jax import lax
from jax.experimental import pallas as pl
from jax.experimental.pallas import tpu as pltpu
from jax.sharding import PartitionSpec as P

HEAD = 128
STEPS = 3
XN = 4
BLOCK = 16
CHUNKS = 3

epsilon = 1e-06
query_scale = 144.0 ** (-0.5)
rope_base = 10000.0
logit_cap = 50.0
TURN = 2 * np.pi
TURN_A = 6.28125
TURN_B = float(np.float32(np.round((TURN - TURN_A) * 2.0**20) / 2.0**20))
TURN_C = float(TURN - TURN_A - TURN_B)
MESH = pl.DeviceIdType.MESH
F32 = jnp.float32
BF16 = jnp.bfloat16
AROUND = (1, 3, 2)


def weights_of(scores):
    return jnp.exp(logit_cap * jnp.tanh(scores * (1.0 / logit_cap)))


def dot_t(a, b):
    return lax.dot_general(a, b, (((1,), (1,)), ((), ())), preferred_element_type=F32)


def dot(a, b):
    return jnp.dot(a, b, preferred_element_type=F32)


def iota(shape, axis):
    return lax.broadcasted_iota(jnp.int32, shape, axis)


def kernel(
    dims, prompt_total,
    hid_in, pre_in, post_in, freq_in, perm_in, wq, wk, wv, wout, pk, pv, kc, vc, par_in, lens_in,
    out_h, out_f,
    hid, pre_gain, post_gain, freq, perm, par, lens,
    tiles, relay, tilesf, cos_rows, sin_rows, a1, a1f, xb, wz, yf, sred, rred, g, gf, qa, kall, vall, acc,
    psend, precv, both, osend, orecv, woutv, kcv, vcv, ancv, freshv, br, csend, crecv, s1, ysend,
    yrecv, zsend, zrecv,
    as_, ar, hs, hr, fs, fr, ws, wr, wzs, wzr, ks, kr, pxs, pxr, pys, pyr, rys, ryr, rxs, rxr, cs, cr, rs, rr, gs,
    gr, qs, qr, ps, pr, os_, or_, bcs, bcr, bys, byr, bzs, bzr, ls,
):
    ZH, YN, KN, ZL = dims
    ZN = ZH * ZL
    PN = ZL // 2
    GN = 2 * ZH
    YK = YN * KN
    BEAMS = ZH * YK
    ROWS = STEPS * BEAMS
    s = lax.axis_index("sample")
    c = lax.axis_index("context")
    zh = lax.div(s, YK)
    y = lax.div(lax.rem(s, YK), KN)
    k = lax.rem(s, KN)
    zl = lax.div(c, XN)
    x = lax.rem(c, XN)
    z = zh * ZL + zl
    q = lax.div(zl, PN)
    p = lax.rem(zl, PN)
    width = hid_in.shape[1]

    def at(zh_=None, y_=None, k_=None, zl_=None, x_=None):
        zh_ = zh if zh_ is None else zh_
        y_ = y if y_ is None else y_
        k_ = k if k_ is None else k_
        zl_ = zl if zl_ is None else zl_
        x_ = x if x_ is None else x_
        return {"sample": zh_ * YK + y_ * KN + k_, "context": zl_ * XN + x_}

    def rc(src, dst, ssem, rsem, where):
        return pltpu.make_async_remote_copy(
            src_ref=src, dst_ref=dst, send_sem=ssem, recv_sem=rsem,
            device_id=where, device_id_type=MESH,
        )

    sends = []

    def push(cp):
        cp.start()
        sends.append(cp)
        return cp

    def x_of(o):
        return lax.rem(x + o + XN, XN)

    def y_of(o):
        return lax.rem(y + o + YN, YN)

    def p_of(o):
        return lax.rem(p + o + PN, PN)

    def half_at(m):
        zz = lax.rem(z + PN * m, ZN)
        zl_ = lax.rem(zz, ZL)
        return at(zh_=lax.div(zz, ZL), zl_=zl_), lax.div(zl_, PN)

    across = at(zl_=(1 - q) * PN + p)

    peers = [half_at(m)[0] for m in range(1, GN, 2)]
    peers += [at(zl_=q * PN + p_of(o)) for o in range(1, PN)]
    peers += [at(x_=x_of(o)) for o in range(1, XN)]
    peers += [at(y_=y_of(o)) for o in range(1, YN)]
    if KN > 1:
        peers += [at(k_=1 - k)]
    barrier = pltpu.get_barrier_semaphore()
    for peer in peers:
        pl.semaphore_signal(barrier, inc=1, device_id=peer, device_id_type=MESH)

    early = [pltpu.make_async_copy(hid_in, hid, ls.at[6]), pltpu.make_async_copy(pre_in, pre_gain, ls.at[7])]
    late = [
        pltpu.make_async_copy(src, dst, ls.at[8 + i])
        for i, (src, dst) in enumerate(
            ((post_in, post_gain), (freq_in, freq), (perm_in, perm), (par_in, par), (lens_in, lens))
        )
    ]
    for cp in early + late:
        cp.start()
    loc = [
        pltpu.make_async_copy(wout, woutv, ls.at[1]),
        pltpu.make_async_copy(kc, kcv, ls.at[2]),
        pltpu.make_async_copy(vc, vcv, ls.at[3]),
        pltpu.make_async_copy(pk, kall.at[x], ls.at[4]),
        pltpu.make_async_copy(pv, vall.at[x], ls.at[5]),
    ]
    for cp in loc:
        cp.start()

    J = width // 256
    TJ = a1.shape[1]
    for cp in early:
        cp.wait()
    hid_f = hid[...].astype(F32)
    mean_square = jnp.mean(hid_f * hid_f, axis=-1, keepdims=True)
    normed = hid_f * lax.rsqrt(mean_square + epsilon) * pre_gain[...].reshape(1, width).astype(F32)
    for part in range(2):
        for j in range(J):
            start = (part * J + j) * 128
            tilesf[part, pl.ds(j * STEPS, STEPS), :] = normed[:, start : start + 128]
        if TJ > J * STEPS:
            tilesf[part, pl.ds(J * STEPS, TJ - J * STEPS), :] = jnp.zeros((TJ - J * STEPS, 128), F32)
    tiles[...] = tilesf[...].astype(BF16)
    pl.semaphore_wait(barrier, len(peers))

    mine = lax.div(z, PN)
    a_copies = []
    h_copies = []
    TH = TJ // 2
    if GN > 2:
        for i, m in enumerate((1, 3)):
            part = tiles.at[q, pl.ds(i * TH, TH)]
            h_copies.append(push(rc(part, relay.at[i], hs.at[i], hr.at[i], half_at(m)[0])))
    for m in range(1, GN, 2):
        where, q_to = half_at(m)
        a_copies.append(push(rc(tiles.at[q_to], a1.at[mine], as_.at[m], ar.at[m], where)))

    half = wq.shape[1] // 2
    w_src = [wq.at[:, pl.ds(0, half)], wq.at[:, pl.ds(half, half)], wk, wv]

    def w_copy(to):
        return rc(w_src[to], wz.at[p, x], ws.at[to], wr.at[x], at(x_=to))

    def w_local(to):
        return pltpu.make_async_copy(w_src[to], wz.at[p, x], ls.at[0])

    for to in range(XN):
        @pl.when(x != to)
        def _():
            w_copy(to).start()

        @pl.when(x == to)
        def _():
            w_local(to).start()

    kv_copies = {}
    positions = kall.shape[1]

    def send_prompt(which, o, part):
        src, dst = ((pk, kall), (pv, vall))[which]
        span = pl.ds(part * (positions // 2), positions // 2)
        cp = rc(
            src.at[span], dst.at[x, span], ks.at[which, o, part], kr.at[which, o, part], at(x_=x_of(o))
        )
        kv_copies[which, o, part] = push(cp)

    def pass_prompt(which, o):
        part = 0 if o == 1 else 1
        kv_copies.pop((which, o, part)).wait_recv()
        block = (kall, vall)[which].at[x_of(-o), pl.ds(part * (positions // 2), positions // 2)]
        cp = rc(block, block, ks.at[which, 2, part], kr.at[which, 2, part], at(x_=x_of(o)))
        kv_copies[which, 2, part] = push(cp)

    send_prompt(0, 1, 0)
    send_prompt(0, 3, 1)
    send_prompt(1, 1, 0)
    send_prompt(1, 3, 1)
    send_prompt(0, 1, 1)
    send_prompt(0, 3, 0)

    a1[mine] = tiles[q]
    for i, cp in enumerate(h_copies):
        cp.wait_recv()
        target = a1.at[lax.rem(mine + (GN - 1, 1)[i], GN), pl.ds(i * TH, TH)]
        a_copies.append(push(rc(relay.at[i], target, fs.at[i], fr.at[i], half_at((1, 3)[i])[0])))
    for to in range(XN):
        @pl.when(x != to)
        def _():
            rc(w_src[to], wz.at[p, to], ws.at[to], wr.at[to], at(x_=to)).wait_recv()

        @pl.when(x == to)
        def _():
            w_local(to).wait()
    wz_copies = []
    for o in range(1, PN):
        wz_copies.append(
            push(rc(wz.at[p], wz.at[p], wzs.at[o], wzr.at[o], at(zl_=q * PN + p_of(o))))
        )
    for cp in a_copies:
        cp.wait_recv()

    for i in range(GN):
        a1f[pl.ds(i * TJ, TJ), :] = a1[i].astype(F32)
    own = (x * YN + y) * KN + k
    rest = jnp.zeros((BLOCK - STEPS * GN, 128), F32)
    for j in range(J):
        lines = [a1f[pl.ds(j * STEPS + t, GN, stride=TJ), :] for t in range(STEPS)]
        xb[own, :, pl.ds(j * 128, 128)] = jnp.concatenate(lines + [rest], axis=0).astype(BF16)

    cols = xb.shape[2] // 2

    def blk(ox, oy):
        return (x_of(-ox) * YN + y_of(-oy)) * KN + k

    def first(b):
        return xb.at[b, :, pl.ds(0, cols)]

    def second(b):
        return xb.at[b, :, pl.ds(cols, cols)]

    px, py, ry, rx, cc = {}, {}, {}, {}, {}

    def forward_y(ox):
        b = blk(ox, 0)
        for o in AROUND[: YN - 1]:
            py[ox, o] = push(rc(first(b), first(b), pys.at[ox, o], pyr.at[ox, o], at(y_=y_of(o))))

    def forward_x(oy):
        b = blk(0, oy)
        for o in AROUND:
            rx[oy, o] = push(rc(second(b), second(b), rxs.at[oy, o], rxr.at[oy, o], at(x_=x_of(o))))

    def to_core(ox, oy):
        if KN > 1:
            b = xb.at[blk(ox, oy)]
            cc[ox, oy] = push(rc(b, b, cs.at[ox, oy], cr.at[ox, oy], at(k_=1 - k)))

    y_around = [o for o in AROUND if o < YN]
    for o in AROUND:
        b = blk(0, 0)
        px[o] = push(rc(first(b), first(b), pxs.at[o], pxr.at[o], at(x_=x_of(o))))
        if o < YN:
            ry[o] = push(rc(second(b), second(b), rys.at[o], ryr.at[o], at(y_=y_of(o))))
    if YN > 1:
        for o in y_around:
            b = blk(0, 0)
            py[0, o] = push(rc(first(b), first(b), pys.at[0, o], pyr.at[0, o], at(y_=y_of(o))))
    forward_x(0)
    to_core(0, 0)
    for o in AROUND:
        px[o].wait_recv()
        for o2 in y_around:
            b = blk(o, 0)
            py[o, o2] = push(rc(first(b), first(b), pys.at[o, o2], pyr.at[o, o2], at(y_=y_of(o2))))
        if o < YN:
            ry[o].wait_recv()
            forward_x(o)

    def gather(ox):
        for oy in [0] + y_around:
            if oy > 0:
                py[ox, oy].wait_recv()
            if ox > 0:
                rx[oy, ox].wait_recv()
            if ox > 0 or oy > 0:
                to_core(ox, oy)

    r_copies = {}

    def project(ox):
        for oy in [0] + y_around:
            if KN > 1:
                cc[ox, oy].wait_recv()
        rows = xb[pl.ds(x_of(-ox) * YK, YK)].reshape(YK * BLOCK, xb.shape[2])
        yf[...] = dot(rows, wz[...].reshape(xb.shape[2], HEAD))
        for h in range(2):
            for t in range(STEPS):
                piece = [
                    yf[pl.ds(t * GN + i * 2 + h, YK, stride=BLOCK), :] for i in range(ZH)
                ]
                sred[ox, h, pl.ds(t * BEAMS, BEAMS), :] = jnp.concatenate(piece, axis=0).astype(BF16)
        r_copies[ox] = push(rc(sred.at[ox], rred.at[ox], rs.at[ox], rr.at[ox], across))

    for which in range(2):
        for o in (1, 3):
            pass_prompt(which, o)
    send_prompt(1, 1, 1)
    send_prompt(1, 3, 0)

    gather(0)
    for cp in wz_copies:
        cp.wait_recv()
    project(0)
    gather(1)
    gather(3)
    project(1)
    gather(2)
    project(3)
    project(2)

    for cp in late:
        cp.wait()
    NT = 2 * XN * STEPS
    at_row = iota((NT, 128), 0)
    place = jnp.zeros((NT, 128), jnp.int32)
    for h in range(2):
        for i in range(XN):
            for t in range(STEPS):
                here = lens[(h * PN + p) * XN + i] + (prompt_total + t)
                place = jnp.where(at_row == (h * XN + i) * STEPS + t, here, place)
    angles = place.astype(F32) * freq[...]
    turns = jnp.round(angles * (1.0 / TURN))
    angles = ((angles - turns * TURN_A) - turns * TURN_B) - turns * TURN_C
    lower = iota((NT, 128), 1) < HEAD // 2
    sines = jnp.sin(angles)
    plain = x == 3
    cos_rows[...] = jnp.where(plain, 1.0, jnp.cos(angles))
    sin_rows[...] = jnp.where(plain, 0.0, jnp.where(lower, -sines, sines))

    scale = jnp.where(x < 2, query_scale, 1.0).astype(F32)
    g_copies = {}
    for ox in (0,) + AROUND:
        xo = x_of(-ox)
        r_copies[ox].wait_recv()
        for h in range(2):
            total = sred[ox, h].astype(F32) + rred[ox, h].astype(F32)
            for t in range(STEPS):
                part = total[t * BEAMS : (t + 1) * BEAMS]
                row = pl.ds((h * XN + xo) * STEPS + t, 1)
                turned = part * cos_rows[row, :] + pltpu.roll(part, HEAD // 2, 1) * sin_rows[row, :]
                gf[ox, h, pl.ds(t * BEAMS, BEAMS), :] = (turned * scale).astype(BF16)
        if ox == 0:
            for h in range(2):
                g[h, x] = gf[0, h]
        else:
            g_copies[ox] = push(rc(gf.at[ox], g.at[:, x], gs.at[ox], gr.at[ox], at(x_=xo)))
    for ox in AROUND:
        g_copies[ox].wait_recv()

    q_copies = {}
    for o in range(1, PN):
        q_copies[o] = push(
            rc(g.at[:, pl.ds(0, 2)], qa.at[p], qs.at[o], qr.at[o], at(zl_=q * PN + p_of(o)))
        )
    for h in range(2):
        qa[p, h] = g[h, 0:2]

    for cp in loc[3:5]:
        cp.wait()
    QR = 2 * ROWS
    eye = iota((QR, 128), 0) == iota((QR, 128), 1)
    upper = iota((16, 128), 0) < 8

    def with_totals(line):
        coarse = line.astype(BF16).astype(F32)
        return jnp.where(upper, coarse, line - coarse).astype(BF16)

    p_copies = {}
    for o in [0] + [o for o in AROUND if o < PN]:
        if o > 0:
            q_copies[o].wait_recv()
        there = p_of(-o)
        queries = qa[there].reshape(2 * QR, HEAD)
        for ox in (0,) + AROUND:
            if o == 0 and ox > 0:
                for key, cp in kv_copies.items():
                    if key[1] == ox:
                        cp.wait_recv()
            xo = x_of(-ox)
            w = weights_of(dot_t(queries, kall[xo])).astype(BF16)
            part = dot(w, jnp.concatenate([vall[xo], jnp.ones((positions, HEAD), BF16)], axis=1))
            if ox == 0:
                acc[...] = part
            else:
                acc[...] += part
        for h in range(2):
            psend[o, h, pl.ds(0, QR), :] = acc[pl.ds(h * QR, QR), pl.ds(0, HEAD)].astype(BF16)
            totals = acc[pl.ds(h * QR, QR), pl.ds(HEAD, HEAD)]
            line = jnp.sum(jnp.where(eye, totals, 0.0), axis=0, keepdims=True)
            psend[o, h, pl.ds(QR, 16), :] = with_totals(line)
        if o > 0:
            p_copies[o] = push(
                rc(psend.at[o], precv.at[o], ps.at[o], pr.at[o], at(zl_=q * PN + there))
            )

    length = lens[c]
    for cp in loc[1:3]:
        cp.wait()
    never = jnp.int32(-1)
    for b in range(BEAMS):
        one = par[1, 0, b]
        two = par[2, 0, b]
        mid = par[1, 0, two]
        me = jnp.int32(b)
        chains = (
            (par[0, 0, b], me, never, never),
            (par[0, 0, one], one, me + BEAMS, never),
            (par[0, 0, mid], mid, two + BEAMS, me + 2 * BEAMS),
        )
        for t in range(STEPS):
            row = t * BEAMS + b
            ancv[pl.ds(row, 1), :] = jnp.full((1, 128), chains[t][0], jnp.int32)
            for u in range(STEPS):
                freshv[u, pl.ds(row, 1), :] = jnp.full((1, 128), chains[t][1 + u], jnp.int32)
    my_q = g[q, 0:2].reshape(QR, HEAD)
    SLOTS = kcv.shape[1]
    anc = ancv[:, :SLOTS]
    anc2 = jnp.concatenate([anc, anc], axis=0)
    in_use = iota((QR, SLOTS), 1) < length
    lane = iota((ROWS, ROWS), 1)
    seen = (lane == freshv[0, :, :ROWS]) | (lane == freshv[1, :, :ROWS]) | (lane == freshv[2, :, :ROWS])
    seen2 = jnp.concatenate([seen.astype(F32)] * 2, axis=0)
    fresh_w = weights_of(dot_t(my_q, g[q, 2])) * seen2
    suf_w = dot(fresh_w.astype(BF16), g[q, 3])
    suf_t = jnp.sum(fresh_w, axis=1, keepdims=True)
    for b in range(BEAMS):
        cached = weights_of(dot_t(my_q, kcv[b]))
        cached = jnp.where((anc2 == b) & in_use, cached, 0.0)
        suf_w = suf_w + dot(cached.astype(BF16), vcv[b])
        suf_t = suf_t + jnp.sum(cached, axis=1, keepdims=True)
    out_f[...] = g[q, 2:4]

    for h in range(2):
        both[h] = psend[0, h].astype(F32)
    for o in range(1, PN):
        p_copies[o].wait_recv()
        for h in range(2):
            both[h] += precv[o, h].astype(F32)
    theirs = both[1 - q]
    osend[pl.ds(0, QR), :] = theirs[:QR].astype(BF16)
    osend[pl.ds(QR, 16), :] = with_totals(theirs[QR : QR + 1] + theirs[QR + 8 : QR + 9])
    o_copy = push(rc(osend, orecv, os_, or_, across))
    ours = both[q]
    o_copy.wait_recv()
    ours = ours + orecv[...].astype(F32)
    line = ours[QR : QR + 1] + ours[QR + 8 : QR + 9]
    column = jnp.sum(jnp.where(eye, line, 0.0), axis=1, keepdims=True)
    attended = ((ours[:QR] + suf_w) / (column + suf_t)).astype(BF16)
    heads = jnp.concatenate([attended[:ROWS], attended[ROWS:]], axis=1)

    loc[0].wait()
    ordered = dot(perm[...], heads).astype(BF16)
    GRP = 4 * ZH
    HALF = YN * GRP
    wide = width // CHUNKS
    bc_copies = []
    by_copies = {}

    def project_out(i):
        for n in range(3):
            part = wide // 3
            at_col = pl.ds(i * wide + n * part, part)
            res = dot(ordered, woutv[:, at_col])
            for kk in range(KN):
                br[kk, i, :, pl.ds(n * part, part)] = res[kk * HALF : (kk + 1) * HALF]
        if KN > 1:
            csend[i] = br[1 - k, i].astype(BF16)
            bc_copies.append(push(rc(csend.at[i], crecv.at[i], bcs.at[i], bcr.at[i], at(k_=1 - k))))

    def over_y(i):
        total = br[k, i]
        if KN > 1:
            bc_copies[i].wait_recv()
            total = total + crecv[i].astype(F32)
        for yy in range(YN):
            s1[i, yy] = total[yy * GRP : (yy + 1) * GRP]
        for o in reversed(y_around):
            v = s1[i, y_of(o)]
            ysend[i, o] = jnp.concatenate([v[:, : wide // 2], v[:, wide // 2 :]], axis=0).astype(BF16)
            by_copies[i, o] = push(
                rc(ysend.at[i, o], yrecv.at[i, o], bys.at[i, o], byr.at[i, o], at(y_=y_of(o)))
            )

    project_out(0)
    for i in range(1, CHUNKS):
        project_out(i)
        over_y(i - 1)
    over_y(CHUNKS - 1)
    bz_copies = []
    kept = []
    is_first = zh == 0
    quarter = wide // 4
    for i in range(CHUNKS):
        total = s1[i, y]
        for o in y_around:
            by_copies[i, o].wait_recv()
            v = yrecv[i, o].astype(F32)
            total = total + jnp.concatenate([v[:GRP], v[GRP:]], axis=1)
        if ZH > 1:
            other = jnp.where(is_first, total[4:8], total[0:4])
            zsend[i] = jnp.concatenate(
                [other[:, n * quarter : (n + 1) * quarter] for n in range(4)], axis=0
            ).astype(BF16)
            bz_copies.append(push(rc(zsend.at[i], zrecv.at[i], bzs.at[i], bzr.at[i], at(zh_=1 - zh))))
            kept.append(jnp.where(is_first, total[0:4], total[4:8]))
        else:
            kept.append(total[0:4])
    if ZH > 1:
        for i in range(CHUNKS):
            bz_copies[i].wait_recv()
            v = zrecv[i].astype(F32)
            kept[i] = kept[i] + jnp.concatenate([v[n * 4 : (n + 1) * 4] for n in range(4)], axis=1)
    square = sum(jnp.sum(v * v, axis=-1, keepdims=True) for v in kept) * (1.0 / width)
    factor = lax.rsqrt(square + epsilon)
    branch = jnp.concatenate(kept, axis=1) * factor
    result = hid[...].astype(F32) + branch[:STEPS] * post_gain[...].reshape(1, width).astype(F32)
    for t in range(STEPS):
        out_h[t, 0] = result[t : t + 1]

    for cp in sends:
        cp.wait_send()
    for to in range(XN):
        @pl.when(x != to)
        def _():
            w_copy(to).wait_send()


def cache_kernel(
    hid, fresh, kc, vc, par, lens, out_h, out_k, out_v, hidv, freshv, old, new, rows, ins, outs, sem
):
    beams, slots = kc.shape[0], kc.shape[1]
    loads = [pltpu.make_async_copy(src, old.at[i], ins.at[i]) for i, src in enumerate((kc, vc))]
    loads.append(pltpu.make_async_copy(fresh, freshv, ins.at[2]))
    loads.append(pltpu.make_async_copy(hid, hidv, ins.at[3]))
    for i in (2, 0, 1, 3):
        loads[i].start()
    length = lens[lax.axis_index("context")]
    window = min(32, slots)
    start = pl.multiple_of(jnp.minimum(lax.div(length, 16) * 16, slots - window), 16)
    at_slot = iota((window, HEAD), 0) + start
    group = max(beams // 4, 1)
    stores = []
    loads[2].wait()
    for i, dst in enumerate((out_k, out_v)):
        rows[...] = freshv[i].astype(F32)
        loads[i].wait()
        for b in range(beams):
            two = par[2, 0, b]
            mid = par[1, 0, two]
            new[i, b] = old[i, par[0, 0, mid]]
            block = new[i, b, pl.ds(start, window), :].astype(F32)
            for u, row in enumerate((mid, two + beams, b + 2 * beams)):
                block = jnp.where(at_slot == length + u, rows[pl.ds(row, 1), :], block)
            new[i, b, pl.ds(start, window), :] = block.astype(BF16)
            if (b + 1) % group == 0:
                span = pl.ds(b + 1 - group, group)
                cp = pltpu.make_async_copy(new.at[i, span], dst.at[span], outs.at[i, b // group])
                cp.start()
                stores.append(cp)
        if i == 0:
            loads[3].wait()
            cp = pltpu.make_async_copy(hidv, out_h, sem)
            cp.start()
            stores.append(cp)
    for cp in stores:
        cp.wait()


def order_matrix(dims):
    ZH, YN, KN, ZL = dims
    beams = ZH * YN * KN
    m = np.zeros((KN * YN * ZH * 4, STEPS * beams), np.float32)
    for kk in range(KN):
        for yy in range(YN):
            for hh in range(ZH):
                for t in range(STEPS):
                    m[((kk * YN + yy) * ZH + hh) * 4 + t, t * beams + (hh * YN + yy) * KN + kk] = 1.0
    return m


def body(
    dims,
    hidden_in,
    pre_gain,
    post_gain,
    w_query,
    key_projection_weight,
    value_projection_weight,
    w_out,
    prompt_rotated_keys,
    prompt_value_rows,
    suffix_key_cache,
    suffix_value_cache,
    parents,
    lengths,
):
    ZH, YN, KN, ZL = dims
    PN = ZL // 2
    GN = 2 * ZH
    YK = YN * KN
    beams = ZH * YK
    rows = STEPS * beams
    width = hidden_in.shape[3]
    slots = suffix_key_cache.shape[2]
    positions = prompt_rotated_keys.shape[0]
    prompt_total = positions * ZL * XN
    J = width // 256
    TJ = -(-(STEPS * J) // 16) * 16
    frequency = 1.0 / rope_base ** (np.arange(HEAD // 2) * 2.0 / HEAD)
    freq = jnp.asarray(np.concatenate([frequency, frequency])[None], F32)
    perm = jnp.asarray(order_matrix(dims), BF16)
    hbm = pl.BlockSpec(memory_space=pltpu.HBM)
    vmem = pl.BlockSpec(memory_space=pltpu.VMEM)
    smem = pl.BlockSpec(memory_space=pltpu.SMEM)
    wrows = w_query.shape[0]
    grp = 4 * ZH
    half = YN * grp
    wide = width // CHUNKS
    V = pltpu.VMEM
    D = pltpu.SemaphoreType.DMA
    scratch = [
        V((STEPS, width), BF16),
        V((width,), BF16),
        V((width,), BF16),
        V((1, HEAD), F32),
        V(perm.shape, BF16),
        pltpu.SMEM(parents.shape, jnp.int32),
        pltpu.SMEM(lengths.shape, jnp.int32),
        V((2, TJ, 128), BF16),
        V((2, TJ // 2, 128), BF16),
        V((2, TJ, 128), F32),
        V((2 * XN * STEPS, 128), F32),
        V((2 * XN * STEPS, 128), F32),
        V((GN, TJ, 128), BF16),
        V((GN * TJ, 128), F32),
        V((XN * YK, BLOCK, width // 2), BF16),
        V((PN, XN, wrows, HEAD), BF16),
        V((YK * BLOCK, HEAD), F32),
        V((XN, 2, rows, HEAD), BF16),
        V((XN, 2, rows, HEAD), BF16),
        V((2, XN, rows, HEAD), BF16),
        V((XN, 2, rows, HEAD), BF16),
        V((PN, 2, 2, rows, HEAD), BF16),
        V((XN, positions, HEAD), BF16),
        V((XN, positions, HEAD), BF16),
        V((4 * rows, 2 * HEAD), F32),
        V((PN, 2, 2 * rows + 16, HEAD), BF16),
        V((PN, 2, 2 * rows + 16, HEAD), BF16),
        V((2, 2 * rows + 16, HEAD), F32),
        V((2 * rows + 16, HEAD), BF16),
        V((2 * rows + 16, HEAD), BF16),
        V(w_out.shape, BF16),
        V((beams, slots, HEAD), BF16),
        V((beams, slots, HEAD), BF16),
        V((rows, 128), jnp.int32),
        V((STEPS, rows, 128), jnp.int32),
        V((KN, CHUNKS, half, wide), F32),
        V((CHUNKS, half, wide), BF16),
        V((CHUNKS, half, wide), BF16),
        V((CHUNKS, YN, grp, wide), F32),
        V((CHUNKS, YN, 2 * grp, wide // 2), BF16),
        V((CHUNKS, YN, 2 * grp, wide // 2), BF16),
        V((CHUNKS, 16, wide // 4), BF16),
        V((CHUNKS, 16, wide // 4), BF16),
        D((4,)), D((4,)), D((2,)), D((2,)), D((2,)), D((2,)), D((XN,)), D((XN,)), D((PN,)), D((PN,)), D((2, XN, 2)), D((2, XN, 2)),
        D((XN,)), D((XN,)), D((XN, 4)), D((XN, 4)), D((4,)), D((4,)), D((4, XN)), D((4, XN)),
        D((XN, 4)), D((XN, 4)), D((XN,)), D((XN,)), D((XN,)), D((XN,)), D((PN,)), D((PN,)),
        D((PN,)), D((PN,)), D, D, D((CHUNKS,)), D((CHUNKS,)), D((CHUNKS, 4)), D((CHUNKS, 4)),
        D((CHUNKS,)), D((CHUNKS,)), D((16,)),
    ]
    keys_in = suffix_key_cache.reshape(beams, slots, HEAD)
    values_in = suffix_value_cache.reshape(beams, slots, HEAD)
    hidden, fresh = pl.pallas_call(
        functools.partial(kernel, dims, prompt_total),
        out_shape=(
            jax.ShapeDtypeStruct((STEPS, 1, 1, width), F32),
            jax.ShapeDtypeStruct((2, rows, HEAD), BF16),
        ),
        in_specs=[hbm] * 15,
        out_specs=(vmem, vmem),
        scratch_shapes=scratch,
        compiler_params=pltpu.CompilerParams(
            collective_id=0, has_side_effects=True, vmem_limit_bytes=63 * 1024 * 1024
        ),
    )(
        hidden_in.reshape(STEPS, width),
        pre_gain,
        post_gain,
        freq,
        perm,
        w_query,
        key_projection_weight,
        value_projection_weight,
        w_out,
        prompt_rotated_keys,
        prompt_value_rows,
        keys_in,
        values_in,
        parents,
        lengths,
    )
    hidden_out, keys_out, values_out = pl.pallas_call(
        cache_kernel,
        out_shape=(
            jax.ShapeDtypeStruct((STEPS, 1, 1, width), F32),
            jax.ShapeDtypeStruct((beams, slots, HEAD), BF16),
            jax.ShapeDtypeStruct((beams, slots, HEAD), BF16),
        ),
        in_specs=[hbm] * 4 + [smem] * 2,
        out_specs=(hbm, hbm, hbm),
        scratch_shapes=[
            V((STEPS, 1, 1, width), F32),
            V((2, rows, HEAD), BF16),
            V((2, beams, slots, HEAD), BF16),
            V((2, beams, slots, HEAD), BF16),
            V((rows, HEAD), F32),
            D((4,)),
            D((2, 4)),
            D,
        ],
        compiler_params=pltpu.CompilerParams(vmem_limit_bytes=63 * 1024 * 1024),
    )(hidden, fresh, keys_in, values_in, parents, lengths)
    return (
        hidden_out,
        keys_out.reshape(1, beams, slots, HEAD),
        values_out.reshape(1, beams, slots, HEAD),
    )


def solution(mesh, dims=(2, 4, 2, 8)):
    placed = (
        P(None, "context", "sample", None),
        P(),
        P(),
        P("context", "sample"),
        P("context", "sample"),
        P("context", "sample"),
        P("sample", None),
        P("context", "sample"),
        P("context", "sample"),
        P("context", None, None, "sample"),
        P("context", None, None, "sample"),
        P(None, "context", None),
        P(),
    )
    return jax.shard_map(
        functools.partial(body, dims),
        mesh=mesh,
        in_specs=placed,
        out_specs=(
            P(None, "context", "sample", None),
            P("context", None, None, "sample"),
            P("context", None, None, "sample"),
        ),
        check_vma=False,
    )
```

```python
import functools

import jax
import jax.numpy as jnp
import numpy as np
from jax import lax
from jax.experimental import pallas as pl
from jax.experimental.pallas import tpu as pltpu
from jax.sharding import PartitionSpec as P

HEAD = 128
STEPS = 3
XN = 4
BLOCK = 16
CHUNKS = 3

epsilon = 1e-06
query_scale = 144.0 ** (-0.5)
rope_base = 10000.0
logit_cap = 50.0
TURN = 2 * np.pi
TURN_A = 6.28125
TURN_B = float(np.float32(np.round((TURN - TURN_A) * 2.0**20) / 2.0**20))
TURN_C = float(TURN - TURN_A - TURN_B)
MESH = pl.DeviceIdType.MESH
F32 = jnp.float32
BF16 = jnp.bfloat16
AROUND = (1, 3, 2)


def weights_of(scores):
    return jnp.exp(logit_cap * jnp.tanh(scores * (1.0 / logit_cap)))


def dot_t(a, b):
    return lax.dot_general(a, b, (((1,), (1,)), ((), ())), preferred_element_type=F32)


def dot(a, b):
    return jnp.dot(a, b, preferred_element_type=F32)


def iota(shape, axis):
    return lax.broadcasted_iota(jnp.int32, shape, axis)


def kernel(
    dims, prompt_total,
    hid_in, pre_in, post_in, freq_in, perm_in, wq, wk, wv, wout, pk, pv, kc, vc, par_in, lens_in,
    out_h, out_f,
    hid, pre_gain, post_gain, freq, perm, par, lens,
    tiles, relay, tilesf, cos_rows, sin_rows, a1, a1f, xb, wz, yk, ysnd, ystd, sred, rred, g, gf, qa, kall, vall, acc,
    psend, precv, both, osend, orecv, woutv, kcv, vcv, ancv, freshv, br, csend, crecv, s1, ysend,
    yrecv, zsend, zrecv,
    as_, ar, hs, hr, fs, fr, ws, wr, wzs, wzr, wcs, wcr, ks, kr, pxs, pxr, pys, pyr, rys, ryr, rxs, rxr, cs, cr, rs, rr, gs,
    gr, qs, qr, ps, pr, os_, or_, bcs, bcr, bys, byr, bzs, bzr, ls,
):
    ZH, YN, KN, ZL = dims
    ZN = ZH * ZL
    PN = ZL // 2
    GN = 2 * ZH
    YK = YN * KN
    BEAMS = ZH * YK
    ROWS = STEPS * BEAMS
    s = lax.axis_index("sample")
    c = lax.axis_index("context")
    zh = lax.div(s, YK)
    y = lax.div(lax.rem(s, YK), KN)
    k = lax.rem(s, KN)
    zl = lax.div(c, XN)
    x = lax.rem(c, XN)
    z = zh * ZL + zl
    q = lax.div(zl, PN)
    p = lax.rem(zl, PN)
    width = hid_in.shape[1]

    def at(zh_=None, y_=None, k_=None, zl_=None, x_=None):
        zh_ = zh if zh_ is None else zh_
        y_ = y if y_ is None else y_
        k_ = k if k_ is None else k_
        zl_ = zl if zl_ is None else zl_
        x_ = x if x_ is None else x_
        return {"sample": zh_ * YK + y_ * KN + k_, "context": zl_ * XN + x_}

    def rc(src, dst, ssem, rsem, where):
        return pltpu.make_async_remote_copy(
            src_ref=src, dst_ref=dst, send_sem=ssem, recv_sem=rsem,
            device_id=where, device_id_type=MESH,
        )

    sends = []

    def push(cp):
        cp.start()
        sends.append(cp)
        return cp

    def x_of(o):
        return lax.rem(x + o + XN, XN)

    def y_of(o):
        return lax.rem(y + o + YN, YN)

    def p_of(o):
        return lax.rem(p + o + PN, PN)

    def half_at(m):
        zz = lax.rem(z + PN * m, ZN)
        zl_ = lax.rem(zz, ZL)
        return at(zh_=lax.div(zz, ZL), zl_=zl_), lax.div(zl_, PN)

    across = at(zl_=(1 - q) * PN + p)

    early = [pltpu.make_async_copy(hid_in, hid, ls.at[6]), pltpu.make_async_copy(pre_in, pre_gain, ls.at[7])]
    late = [
        pltpu.make_async_copy(src, dst, ls.at[8 + i])
        for i, (src, dst) in enumerate(
            ((post_in, post_gain), (freq_in, freq), (perm_in, perm), (par_in, par), (lens_in, lens))
        )
    ]
    for cp in early:
        cp.start()

    peers = [half_at(m)[0] for m in range(1, GN, 2)]
    peers += [at(zl_=q * PN + p_of(o)) for o in range(1, PN)]
    peers += [at(x_=x_of(o)) for o in range(1, XN)]
    peers += [at(y_=y_of(o)) for o in range(1, YN)]
    if KN > 1:
        peers += [at(k_=1 - k)]
    barrier = pltpu.get_barrier_semaphore()
    for peer in peers:
        pl.semaphore_signal(barrier, inc=1, device_id=peer, device_id_type=MESH)

    loc = [
        pltpu.make_async_copy(wout, woutv, ls.at[1]),
        pltpu.make_async_copy(kc, kcv, ls.at[2]),
        pltpu.make_async_copy(vc, vcv, ls.at[3]),
        pltpu.make_async_copy(pk, kall.at[x], ls.at[4]),
        pltpu.make_async_copy(pv, vall.at[x], ls.at[5]),
    ]
    for cp in late + loc:
        cp.start()

    J = width // 256
    TJ = a1.shape[1]
    for cp in early:
        cp.wait()
    hid_f = hid[...].astype(F32)
    mean_square = jnp.mean(hid_f * hid_f, axis=-1, keepdims=True)
    normed = hid_f * lax.rsqrt(mean_square + epsilon) * pre_gain[...].reshape(1, width).astype(F32)
    for part in range(2):
        for j in range(J):
            start = (part * J + j) * 128
            tilesf[part, pl.ds(j * STEPS, STEPS), :] = normed[:, start : start + 128]
        if TJ > J * STEPS:
            tilesf[part, pl.ds(J * STEPS, TJ - J * STEPS), :] = jnp.zeros((TJ - J * STEPS, 128), F32)
    tiles[...] = tilesf[...].astype(BF16)
    pl.semaphore_wait(barrier, len(peers))

    mine = lax.div(z, PN)
    a_copies = []
    h_copies = []
    TH = TJ // 2
    if GN > 2:
        for i, m in enumerate((1, 3)):
            part = tiles.at[q, pl.ds(i * TH, TH)]
            h_copies.append(push(rc(part, relay.at[i], hs.at[i], hr.at[i], half_at(m)[0])))
    for m in range(1, GN, 2):
        where, q_to = half_at(m)
        a_copies.append(push(rc(tiles.at[q_to], a1.at[mine], as_.at[m], ar.at[m], where)))

    half = wq.shape[1] // 2
    w_src = [wq.at[:, pl.ds(0, half)], wq.at[:, pl.ds(half, half)], wk, wv]

    def own_part(x_):
        return wz.at[p, x_, :, pl.ds(0, HEAD)]

    def w_copy(to):
        return rc(w_src[to], own_part(x), ws.at[to], wr.at[x], at(x_=to))

    def w_local(to):
        return pltpu.make_async_copy(w_src[to], own_part(x), ls.at[0])

    for to in range(XN):
        @pl.when(x != to)
        def _():
            w_copy(to).start()

        @pl.when(x == to)
        def _():
            w_local(to).start()

    kv_copies = {}
    positions = kall.shape[1]

    def send_prompt(which, o, part):
        src, dst = ((pk, kall), (pv, vall))[which]
        span = pl.ds(part * (positions // 2), positions // 2)
        cp = rc(
            src.at[span], dst.at[x, span], ks.at[which, o, part], kr.at[which, o, part], at(x_=x_of(o))
        )
        kv_copies[which, o, part] = push(cp)

    def pass_prompt(which, o):
        part = 0 if o == 1 else 1
        kv_copies.pop((which, o, part)).wait_recv()
        block = (kall, vall)[which].at[x_of(-o), pl.ds(part * (positions // 2), positions // 2)]
        cp = rc(block, block, ks.at[which, 2, part], kr.at[which, 2, part], at(x_=x_of(o)))
        kv_copies[which, 2, part] = push(cp)

    send_prompt(0, 1, 0)
    send_prompt(0, 3, 1)
    send_prompt(1, 1, 0)
    send_prompt(1, 3, 1)
    send_prompt(0, 1, 1)
    send_prompt(0, 3, 0)

    a1[mine] = tiles[q]
    for i, cp in enumerate(h_copies):
        cp.wait_recv()
        target = a1.at[lax.rem(mine + (GN - 1, 1)[i], GN), pl.ds(i * TH, TH)]
        a_copies.append(push(rc(relay.at[i], target, fs.at[i], fr.at[i], half_at((1, 3)[i])[0])))
    for to in range(XN):
        @pl.when(x != to)
        def _():
            rc(w_src[to], own_part(to), ws.at[to], wr.at[to], at(x_=to)).wait_recv()

        @pl.when(x == to)
        def _():
            w_local(to).wait()
    wz_copies = {}
    wc_copies = []
    for o in range(1, PN):
        part = wz.at[p, :, :, pl.ds(0, HEAD)]
        wz_copies[o] = push(rc(part, part, wzs.at[o], wzr.at[o], at(zl_=q * PN + p_of(o))))

    def weights_to_core(o):
        if o > 0:
            wz_copies[o].wait_recv()
        if KN > 1:
            from_ = wz.at[p_of(-o), :, :, pl.ds(0, HEAD)]
            into = wz.at[p_of(-o), :, :, pl.ds(HEAD, HEAD)]
            wc_copies.append(push(rc(from_, into, wcs.at[o], wcr.at[o], at(k_=1 - k))))

    weights_to_core(0)
    for cp in a_copies:
        cp.wait_recv()

    for i in range(GN):
        a1f[pl.ds(i * TJ, TJ), :] = a1[i].astype(F32)
    own = x * YN + y
    rest = jnp.zeros((BLOCK - STEPS * GN, 128), F32)
    for j in range(J):
        lines = [a1f[pl.ds(j * STEPS + t, GN, stride=TJ), :] for t in range(STEPS)]
        xb[own, :, pl.ds(j * 128, 128)] = jnp.concatenate(lines + [rest], axis=0).astype(BF16)

    cols = xb.shape[2] // 2

    def blk(ox, oy):
        return x_of(-ox) * YN + y_of(-oy)

    def first(b):
        return xb.at[b, :, pl.ds(0, cols)]

    def second(b):
        return xb.at[b, :, pl.ds(cols, cols)]

    px, py, ry, rx, cc = {}, {}, {}, {}, {}

    def forward_y(ox):
        b = blk(ox, 0)
        for o in AROUND[: YN - 1]:
            py[ox, o] = push(rc(first(b), first(b), pys.at[ox, o], pyr.at[ox, o], at(y_=y_of(o))))

    def forward_x(oy):
        b = blk(0, oy)
        for o in AROUND:
            rx[oy, o] = push(rc(second(b), second(b), rxs.at[oy, o], rxr.at[oy, o], at(x_=x_of(o))))

    y_around = [o for o in AROUND if o < YN]
    for o in AROUND:
        b = blk(0, 0)
        px[o] = push(rc(first(b), first(b), pxs.at[o], pxr.at[o], at(x_=x_of(o))))
        if o < YN:
            ry[o] = push(rc(second(b), second(b), rys.at[o], ryr.at[o], at(y_=y_of(o))))
    if YN > 1:
        for o in y_around:
            b = blk(0, 0)
            py[0, o] = push(rc(first(b), first(b), pys.at[0, o], pyr.at[0, o], at(y_=y_of(o))))
    forward_x(0)
    for o in AROUND:
        px[o].wait_recv()
        for o2 in y_around:
            b = blk(o, 0)
            py[o, o2] = push(rc(first(b), first(b), pys.at[o, o2], pyr.at[o, o2], at(y_=y_of(o2))))
        if o < YN:
            ry[o].wait_recv()
            forward_x(o)

    def gather(ox):
        for oy in [0] + y_around:
            if oy > 0:
                py[ox, oy].wait_recv()
            if ox > 0:
                rx[oy, ox].wait_recv()

    r_copies = {}

    def project(ox):
        rows = xb[pl.ds(x_of(-ox) * YN, YN)].reshape(YN * BLOCK, xb.shape[2])
        res = dot(rows, wz[...].reshape(xb.shape[2], KN * HEAD))
        yk[ox, k] = res[:, :HEAD]
        if KN > 1:
            ysnd[ox] = res[:, HEAD:]
            cc[ox] = push(rc(ysnd.at[ox], yk.at[ox, k], cs.at[ox], cr.at[ox], at(k_=1 - k)))

    def finish(ox):
        if KN > 1:
            cc[ox].wait_recv()
        for kk in range(KN):
            for h in range(2):
                for t in range(STEPS):
                    for i in range(ZH):
                        lines = yk[ox, kk, pl.ds(t * GN + i * 2 + h, YN, stride=BLOCK), :]
                        start = h * ROWS + t * BEAMS + i * YK + kk
                        ystd[pl.ds(start, YN, stride=KN), :] = lines
        sred[ox] = ystd[...].reshape(2, ROWS, HEAD).astype(BF16)
        r_copies[ox] = push(rc(sred.at[ox], rred.at[ox], rs.at[ox], rr.at[ox], across))

    for which in range(2):
        for o in (1, 3):
            pass_prompt(which, o)
    send_prompt(1, 1, 1)
    send_prompt(1, 3, 0)

    for o in [o for o in AROUND if o < PN]:
        weights_to_core(o)
    gather(0)
    for cp in wc_copies:
        cp.wait_recv()
    project(0)
    gather(1)
    project(1)
    finish(0)
    gather(3)
    project(3)
    finish(1)
    gather(2)
    project(2)
    finish(3)
    finish(2)

    for cp in late:
        cp.wait()
    NT = 2 * XN * STEPS
    at_row = iota((NT, 128), 0)
    place = jnp.zeros((NT, 128), jnp.int32)
    for h in range(2):
        for i in range(XN):
            for t in range(STEPS):
                here = lens[(h * PN + p) * XN + i] + (prompt_total + t)
                place = jnp.where(at_row == (h * XN + i) * STEPS + t, here, place)
    angles = place.astype(F32) * freq[...]
    turns = jnp.round(angles * (1.0 / TURN))
    angles = ((angles - turns * TURN_A) - turns * TURN_B) - turns * TURN_C
    lower = iota((NT, 128), 1) < HEAD // 2
    sines = jnp.sin(angles)
    plain = x == 3
    cos_rows[...] = jnp.where(plain, 1.0, jnp.cos(angles))
    sin_rows[...] = jnp.where(plain, 0.0, jnp.where(lower, -sines, sines))

    scale = jnp.where(x < 2, query_scale, 1.0).astype(F32)
    g_copies = {}
    for ox in (0,) + AROUND:
        xo = x_of(-ox)
        r_copies[ox].wait_recv()
        for h in range(2):
            total = sred[ox, h].astype(F32) + rred[ox, h].astype(F32)
            for t in range(STEPS):
                part = total[t * BEAMS : (t + 1) * BEAMS]
                row = pl.ds((h * XN + xo) * STEPS + t, 1)
                turned = part * cos_rows[row, :] + pltpu.roll(part, HEAD // 2, 1) * sin_rows[row, :]
                gf[ox, h, pl.ds(t * BEAMS, BEAMS), :] = (turned * scale).astype(BF16)
        if ox == 0:
            for h in range(2):
                g[h, x] = gf[0, h]
        else:
            g_copies[ox] = push(rc(gf.at[ox], g.at[:, x], gs.at[ox], gr.at[ox], at(x_=xo)))
    for ox in AROUND:
        g_copies[ox].wait_recv()

    q_copies = {}
    for o in range(1, PN):
        q_copies[o] = push(
            rc(g.at[:, pl.ds(0, 2)], qa.at[p], qs.at[o], qr.at[o], at(zl_=q * PN + p_of(o)))
        )
    for h in range(2):
        qa[p, h] = g[h, 0:2]

    for cp in loc[3:5]:
        cp.wait()
    QR = 2 * ROWS
    eye = iota((QR, 128), 0) == iota((QR, 128), 1)
    upper = iota((16, 128), 0) < 8

    def with_totals(line):
        coarse = line.astype(BF16).astype(F32)
        return jnp.where(upper, coarse, line - coarse).astype(BF16)

    p_copies = {}
    for o in [0] + [o for o in AROUND if o < PN]:
        if o > 0:
            q_copies[o].wait_recv()
        there = p_of(-o)
        queries = qa[there].reshape(2 * QR, HEAD)
        for ox in (0,) + AROUND:
            if o == 0 and ox > 0:
                for key, cp in kv_copies.items():
                    if key[1] == ox:
                        cp.wait_recv()
            xo = x_of(-ox)
            w = weights_of(dot_t(queries, kall[xo])).astype(BF16)
            part = dot(w, jnp.concatenate([vall[xo], jnp.ones((positions, HEAD), BF16)], axis=1))
            if ox == 0:
                acc[...] = part
            else:
                acc[...] += part
        for h in range(2):
            psend[o, h, pl.ds(0, QR), :] = acc[pl.ds(h * QR, QR), pl.ds(0, HEAD)].astype(BF16)
            totals = acc[pl.ds(h * QR, QR), pl.ds(HEAD, HEAD)]
            line = jnp.sum(jnp.where(eye, totals, 0.0), axis=0, keepdims=True)
            psend[o, h, pl.ds(QR, 16), :] = with_totals(line)
        if o > 0:
            p_copies[o] = push(
                rc(psend.at[o], precv.at[o], ps.at[o], pr.at[o], at(zl_=q * PN + there))
            )

    length = lens[c]
    for cp in loc[1:3]:
        cp.wait()
    never = jnp.int32(-1)
    for b in range(BEAMS):
        one = par[1, 0, b]
        two = par[2, 0, b]
        mid = par[1, 0, two]
        me = jnp.int32(b)
        chains = (
            (par[0, 0, b], me, never, never),
            (par[0, 0, one], one, me + BEAMS, never),
            (par[0, 0, mid], mid, two + BEAMS, me + 2 * BEAMS),
        )
        for t in range(STEPS):
            row = t * BEAMS + b
            ancv[pl.ds(row, 1), :] = jnp.full((1, 128), chains[t][0], jnp.int32)
            for u in range(STEPS):
                freshv[u, pl.ds(row, 1), :] = jnp.full((1, 128), chains[t][1 + u], jnp.int32)
    my_q = g[q, 0:2].reshape(QR, HEAD)
    SLOTS = kcv.shape[1]
    anc = ancv[:, :SLOTS]
    anc2 = jnp.concatenate([anc, anc], axis=0)
    in_use = iota((QR, SLOTS), 1) < length
    lane = iota((ROWS, ROWS), 1)
    seen = (lane == freshv[0, :, :ROWS]) | (lane == freshv[1, :, :ROWS]) | (lane == freshv[2, :, :ROWS])
    seen2 = jnp.concatenate([seen.astype(F32)] * 2, axis=0)
    fresh_w = weights_of(dot_t(my_q, g[q, 2])) * seen2
    suf_w = dot(fresh_w.astype(BF16), g[q, 3])
    suf_t = jnp.sum(fresh_w, axis=1, keepdims=True)
    for b in range(BEAMS):
        cached = weights_of(dot_t(my_q, kcv[b]))
        cached = jnp.where((anc2 == b) & in_use, cached, 0.0)
        suf_w = suf_w + dot(cached.astype(BF16), vcv[b])
        suf_t = suf_t + jnp.sum(cached, axis=1, keepdims=True)
    out_f[...] = g[q, 2:4]

    for h in range(2):
        both[h] = psend[0, h].astype(F32)
    for o in range(1, PN):
        p_copies[o].wait_recv()
        for h in range(2):
            both[h] += precv[o, h].astype(F32)
    theirs = both[1 - q]
    osend[pl.ds(0, QR), :] = theirs[:QR].astype(BF16)
    osend[pl.ds(QR, 16), :] = with_totals(theirs[QR : QR + 1] + theirs[QR + 8 : QR + 9])
    o_copy = push(rc(osend, orecv, os_, or_, across))
    ours = both[q]
    o_copy.wait_recv()
    ours = ours + orecv[...].astype(F32)
    line = ours[QR : QR + 1] + ours[QR + 8 : QR + 9]
    column = jnp.sum(jnp.where(eye, line, 0.0), axis=1, keepdims=True)
    attended = ((ours[:QR] + suf_w) / (column + suf_t)).astype(BF16)
    heads = jnp.concatenate([attended[:ROWS], attended[ROWS:]], axis=1)

    loc[0].wait()
    ordered = dot(perm[...], heads).astype(BF16)
    GRP = 4 * ZH
    HALF = YN * GRP
    wide = width // CHUNKS
    bc_copies = []
    by_copies = {}

    def project_out(i):
        for n in range(3):
            part = wide // 3
            at_col = pl.ds(i * wide + n * part, part)
            res = dot(ordered, woutv[:, at_col])
            for kk in range(KN):
                br[kk, i, :, pl.ds(n * part, part)] = res[kk * HALF : (kk + 1) * HALF]
        if KN > 1:
            csend[i] = br[1 - k, i].astype(BF16)
            bc_copies.append(push(rc(csend.at[i], crecv.at[i], bcs.at[i], bcr.at[i], at(k_=1 - k))))

    def over_y(i):
        total = br[k, i]
        if KN > 1:
            bc_copies[i].wait_recv()
            total = total + crecv[i].astype(F32)
        for yy in range(YN):
            s1[i, yy] = total[yy * GRP : (yy + 1) * GRP]
        for o in reversed(y_around):
            v = s1[i, y_of(o)]
            ysend[i, o] = jnp.concatenate([v[:, : wide // 2], v[:, wide // 2 :]], axis=0).astype(BF16)
            by_copies[i, o] = push(
                rc(ysend.at[i, o], yrecv.at[i, o], bys.at[i, o], byr.at[i, o], at(y_=y_of(o)))
            )

    project_out(0)
    for i in range(1, CHUNKS):
        project_out(i)
        over_y(i - 1)
    over_y(CHUNKS - 1)
    bz_copies = []
    kept = []
    is_first = zh == 0
    quarter = wide // 4
    for i in range(CHUNKS):
        total = s1[i, y]
        for o in y_around:
            by_copies[i, o].wait_recv()
            v = yrecv[i, o].astype(F32)
            total = total + jnp.concatenate([v[:GRP], v[GRP:]], axis=1)
        if ZH > 1:
            other = jnp.where(is_first, total[4:8], total[0:4])
            zsend[i] = jnp.concatenate(
                [other[:, n * quarter : (n + 1) * quarter] for n in range(4)], axis=0
            ).astype(BF16)
            bz_copies.append(push(rc(zsend.at[i], zrecv.at[i], bzs.at[i], bzr.at[i], at(zh_=1 - zh))))
            kept.append(jnp.where(is_first, total[0:4], total[4:8]))
        else:
            kept.append(total[0:4])
    if ZH > 1:
        for i in range(CHUNKS):
            bz_copies[i].wait_recv()
            v = zrecv[i].astype(F32)
            kept[i] = kept[i] + jnp.concatenate([v[n * 4 : (n + 1) * 4] for n in range(4)], axis=1)
    square = sum(jnp.sum(v * v, axis=-1, keepdims=True) for v in kept) * (1.0 / width)
    factor = lax.rsqrt(square + epsilon)
    branch = jnp.concatenate(kept, axis=1) * factor
    result = hid[...].astype(F32) + branch[:STEPS] * post_gain[...].reshape(1, width).astype(F32)
    for t in range(STEPS):
        out_h[t, 0] = result[t : t + 1]

    for cp in sends:
        cp.wait_send()
    for to in range(XN):
        @pl.when(x != to)
        def _():
            w_copy(to).wait_send()


def cache_kernel(
    hid, fresh, kc, vc, par, lens, out_h, out_k, out_v, hidv, freshv, old, new, rows, ins, outs, sem
):
    beams, slots = kc.shape[0], kc.shape[1]
    loads = [pltpu.make_async_copy(src, old.at[i], ins.at[i]) for i, src in enumerate((kc, vc))]
    loads.append(pltpu.make_async_copy(fresh, freshv, ins.at[2]))
    loads.append(pltpu.make_async_copy(hid, hidv, ins.at[3]))
    for i in (2, 0, 1, 3):
        loads[i].start()
    length = lens[lax.axis_index("context")]
    window = min(32, slots)
    start = pl.multiple_of(jnp.minimum(lax.div(length, 16) * 16, slots - window), 16)
    at_slot = iota((window, HEAD), 0) + start
    group = max(beams // 4, 1)
    stores = []
    loads[2].wait()
    for i, dst in enumerate((out_k, out_v)):
        rows[...] = freshv[i].astype(F32)
        loads[i].wait()
        for b in range(beams):
            two = par[2, 0, b]
            mid = par[1, 0, two]
            new[i, b] = old[i, par[0, 0, mid]]
            block = new[i, b, pl.ds(start, window), :].astype(F32)
            for u, row in enumerate((mid, two + beams, b + 2 * beams)):
                block = jnp.where(at_slot == length + u, rows[pl.ds(row, 1), :], block)
            new[i, b, pl.ds(start, window), :] = block.astype(BF16)
            if (b + 1) % group == 0:
                span = pl.ds(b + 1 - group, group)
                cp = pltpu.make_async_copy(new.at[i, span], dst.at[span], outs.at[i, b // group])
                cp.start()
                stores.append(cp)
        if i == 0:
            loads[3].wait()
            cp = pltpu.make_async_copy(hidv, out_h, sem)
            cp.start()
            stores.append(cp)
    for cp in stores:
        cp.wait()


def order_matrix(dims):
    ZH, YN, KN, ZL = dims
    beams = ZH * YN * KN
    m = np.zeros((KN * YN * ZH * 4, STEPS * beams), np.float32)
    for kk in range(KN):
        for yy in range(YN):
            for hh in range(ZH):
                for t in range(STEPS):
                    m[((kk * YN + yy) * ZH + hh) * 4 + t, t * beams + (hh * YN + yy) * KN + kk] = 1.0
    return m


def body(
    dims,
    hidden_in,
    pre_gain,
    post_gain,
    w_query,
    key_projection_weight,
    value_projection_weight,
    w_out,
    prompt_rotated_keys,
    prompt_value_rows,
    suffix_key_cache,
    suffix_value_cache,
    parents,
    lengths,
):
    ZH, YN, KN, ZL = dims
    PN = ZL // 2
    GN = 2 * ZH
    YK = YN * KN
    beams = ZH * YK
    rows = STEPS * beams
    width = hidden_in.shape[3]
    slots = suffix_key_cache.shape[2]
    positions = prompt_rotated_keys.shape[0]
    prompt_total = positions * ZL * XN
    J = width // 256
    TJ = -(-(STEPS * J) // 16) * 16
    frequency = 1.0 / rope_base ** (np.arange(HEAD // 2) * 2.0 / HEAD)
    freq = jnp.asarray(np.concatenate([frequency, frequency])[None], F32)
    perm = jnp.asarray(order_matrix(dims), BF16)
    hbm = pl.BlockSpec(memory_space=pltpu.HBM)
    vmem = pl.BlockSpec(memory_space=pltpu.VMEM)
    smem = pl.BlockSpec(memory_space=pltpu.SMEM)
    wrows = w_query.shape[0]
    grp = 4 * ZH
    half = YN * grp
    wide = width // CHUNKS
    V = pltpu.VMEM
    D = pltpu.SemaphoreType.DMA
    scratch = [
        V((STEPS, width), BF16),
        V((width,), BF16),
        V((width,), BF16),
        V((1, HEAD), F32),
        V(perm.shape, BF16),
        pltpu.SMEM(parents.shape, jnp.int32),
        pltpu.SMEM(lengths.shape, jnp.int32),
        V((2, TJ, 128), BF16),
        V((2, TJ // 2, 128), BF16),
        V((2, TJ, 128), F32),
        V((2 * XN * STEPS, 128), F32),
        V((2 * XN * STEPS, 128), F32),
        V((GN, TJ, 128), BF16),
        V((GN * TJ, 128), F32),
        V((XN * YN, BLOCK, width // 2), BF16),
        V((PN, XN, wrows, KN * HEAD), BF16),
        V((XN, KN, YN * BLOCK, HEAD), F32),
        V((XN, YN * BLOCK, HEAD), F32),
        V((2 * rows, HEAD), F32),
        V((XN, 2, rows, HEAD), BF16),
        V((XN, 2, rows, HEAD), BF16),
        V((2, XN, rows, HEAD), BF16),
        V((XN, 2, rows, HEAD), BF16),
        V((PN, 2, 2, rows, HEAD), BF16),
        V((XN, positions, HEAD), BF16),
        V((XN, positions, HEAD), BF16),
        V((4 * rows, 2 * HEAD), F32),
        V((PN, 2, 2 * rows + 16, HEAD), BF16),
        V((PN, 2, 2 * rows + 16, HEAD), BF16),
        V((2, 2 * rows + 16, HEAD), F32),
        V((2 * rows + 16, HEAD), BF16),
        V((2 * rows + 16, HEAD), BF16),
        V(w_out.shape, BF16),
        V((beams, slots, HEAD), BF16),
        V((beams, slots, HEAD), BF16),
        V((rows, 128), jnp.int32),
        V((STEPS, rows, 128), jnp.int32),
        V((KN, CHUNKS, half, wide), F32),
        V((CHUNKS, half, wide), BF16),
        V((CHUNKS, half, wide), BF16),
        V((CHUNKS, YN, grp, wide), F32),
        V((CHUNKS, YN, 2 * grp, wide // 2), BF16),
        V((CHUNKS, YN, 2 * grp, wide // 2), BF16),
        V((CHUNKS, 16, wide // 4), BF16),
        V((CHUNKS, 16, wide // 4), BF16),
        D((4,)), D((4,)), D((2,)), D((2,)), D((2,)), D((2,)), D((XN,)), D((XN,)), D((PN,)), D((PN,)), D((PN,)), D((PN,)), D((2, XN, 2)), D((2, XN, 2)),
        D((XN,)), D((XN,)), D((XN, 4)), D((XN, 4)), D((4,)), D((4,)), D((4, XN)), D((4, XN)),
        D((XN,)), D((XN,)), D((XN,)), D((XN,)), D((XN,)), D((XN,)), D((PN,)), D((PN,)),
        D((PN,)), D((PN,)), D, D, D((CHUNKS,)), D((CHUNKS,)), D((CHUNKS, 4)), D((CHUNKS, 4)),
        D((CHUNKS,)), D((CHUNKS,)), D((16,)),
    ]
    keys_in = suffix_key_cache.reshape(beams, slots, HEAD)
    values_in = suffix_value_cache.reshape(beams, slots, HEAD)
    hidden, fresh = pl.pallas_call(
        functools.partial(kernel, dims, prompt_total),
        out_shape=(
            jax.ShapeDtypeStruct((STEPS, 1, 1, width), F32),
            jax.ShapeDtypeStruct((2, rows, HEAD), BF16),
        ),
        in_specs=[hbm] * 15,
        out_specs=(vmem, vmem),
        scratch_shapes=scratch,
        compiler_params=pltpu.CompilerParams(
            collective_id=0, has_side_effects=True, vmem_limit_bytes=63 * 1024 * 1024
        ),
    )(
        hidden_in.reshape(STEPS, width),
        pre_gain,
        post_gain,
        freq,
        perm,
        w_query,
        key_projection_weight,
        value_projection_weight,
        w_out,
        prompt_rotated_keys,
        prompt_value_rows,
        keys_in,
        values_in,
        parents,
        lengths,
    )
    hidden_out, keys_out, values_out = pl.pallas_call(
        cache_kernel,
        out_shape=(
            jax.ShapeDtypeStruct((STEPS, 1, 1, width), F32),
            jax.ShapeDtypeStruct((beams, slots, HEAD), BF16),
            jax.ShapeDtypeStruct((beams, slots, HEAD), BF16),
        ),
        in_specs=[hbm] * 4 + [smem] * 2,
        out_specs=(hbm, hbm, hbm),
        scratch_shapes=[
            V((STEPS, 1, 1, width), F32),
            V((2, rows, HEAD), BF16),
            V((2, beams, slots, HEAD), BF16),
            V((2, beams, slots, HEAD), BF16),
            V((rows, HEAD), F32),
            D((4,)),
            D((2, 4)),
            D,
        ],
        compiler_params=pltpu.CompilerParams(vmem_limit_bytes=63 * 1024 * 1024),
    )(hidden, fresh, keys_in, values_in, parents, lengths)
    return (
        hidden_out,
        keys_out.reshape(1, beams, slots, HEAD),
        values_out.reshape(1, beams, slots, HEAD),
    )


def solution(mesh, dims=(2, 4, 2, 8)):
    placed = (
        P(None, "context", "sample", None),
        P(),
        P(),
        P("context", "sample"),
        P("context", "sample"),
        P("context", "sample"),
        P("sample", None),
        P("context", "sample"),
        P("context", "sample"),
        P("context", None, None, "sample"),
        P("context", None, None, "sample"),
        P(None, "context", None),
        P(),
    )
    return jax.shard_map(
        functools.partial(body, dims),
        mesh=mesh,
        in_specs=placed,
        out_specs=(
            P(None, "context", "sample", None),
            P("context", None, None, "sample"),
            P("context", None, None, "sample"),
        ),
        check_vma=False,
    )
```

```python
import functools

import jax
import jax.numpy as jnp
import numpy as np
from jax import lax
from jax.experimental import pallas as pl
from jax.experimental.pallas import tpu as pltpu
from jax.sharding import PartitionSpec as P

HEAD = 128
STEPS = 3
XN = 4
BLOCK = 16
CHUNKS = 3

epsilon = 1e-06
query_scale = 144.0 ** (-0.5)
rope_base = 10000.0
logit_cap = 50.0
TURN = 2 * np.pi
TURN_A = 6.28125
TURN_B = float(np.float32(np.round((TURN - TURN_A) * 2.0**20) / 2.0**20))
TURN_C = float(TURN - TURN_A - TURN_B)
MESH = pl.DeviceIdType.MESH
F32 = jnp.float32
BF16 = jnp.bfloat16
AROUND = (1, 3, 2)


def weights_of(scores):
    return jnp.exp(logit_cap * jnp.tanh(scores * (1.0 / logit_cap)))


def dot_t(a, b):
    return lax.dot_general(a, b, (((1,), (1,)), ((), ())), preferred_element_type=F32)


def dot(a, b):
    return jnp.dot(a, b, preferred_element_type=F32)


def iota(shape, axis):
    return lax.broadcasted_iota(jnp.int32, shape, axis)


def kernel(
    dims, prompt_total,
    hid_in, pre_in, post_in, freq_in, perm_in, wq, wk, wv, wout, pk, pv, kc, vc, par_in, lens_in,
    out_h, out_k, out_v,
    hid, pre_gain, post_gain, freq, perm, par, lens,
    tiles, relay, tilesf, cos_rows, sin_rows, a1, a1f, xb, wz, yf, sred, rred, g, gf, qa, kall, vall, acc,
    psend, precv, both, osend, orecv, woutv, kcv, vcv, ancv, freshv, br, csend, crecv, s1, ysend,
    yrecv, zsend, zrecv, freshk, new,
    as_, ar, hs, hr, fs, fr, ws, wr, wzs, wzr, ks, kr, pxs, pxr, pys, pyr, rys, ryr, rxs, rxr, cs, cr, rs, rr, gs,
    gr, qs, qr, ps, pr, os_, or_, bcs, bcr, bys, byr, bzs, bzr, ls,
):
    ZH, YN, KN, ZL = dims
    ZN = ZH * ZL
    PN = ZL // 2
    GN = 2 * ZH
    YK = YN * KN
    BEAMS = ZH * YK
    ROWS = STEPS * BEAMS
    s = lax.axis_index("sample")
    c = lax.axis_index("context")
    zh = lax.div(s, YK)
    y = lax.div(lax.rem(s, YK), KN)
    k = lax.rem(s, KN)
    zl = lax.div(c, XN)
    x = lax.rem(c, XN)
    z = zh * ZL + zl
    q = lax.div(zl, PN)
    p = lax.rem(zl, PN)
    width = hid_in.shape[1]

    def at(zh_=None, y_=None, k_=None, zl_=None, x_=None):
        zh_ = zh if zh_ is None else zh_
        y_ = y if y_ is None else y_
        k_ = k if k_ is None else k_
        zl_ = zl if zl_ is None else zl_
        x_ = x if x_ is None else x_
        return {"sample": zh_ * YK + y_ * KN + k_, "context": zl_ * XN + x_}

    def rc(src, dst, ssem, rsem, where):
        return pltpu.make_async_remote_copy(
            src_ref=src, dst_ref=dst, send_sem=ssem, recv_sem=rsem,
            device_id=where, device_id_type=MESH,
        )

    sends = []

    def push(cp):
        cp.start()
        sends.append(cp)
        return cp

    def x_of(o):
        return lax.rem(x + o + XN, XN)

    def y_of(o):
        return lax.rem(y + o + YN, YN)

    def p_of(o):
        return lax.rem(p + o + PN, PN)

    def half_at(m):
        zz = lax.rem(z + PN * m, ZN)
        zl_ = lax.rem(zz, ZL)
        return at(zh_=lax.div(zz, ZL), zl_=zl_), lax.div(zl_, PN)

    across = at(zl_=(1 - q) * PN + p)

    early = [pltpu.make_async_copy(hid_in, hid, ls.at[6]), pltpu.make_async_copy(pre_in, pre_gain, ls.at[7])]
    late = [
        pltpu.make_async_copy(src, dst, ls.at[8 + i])
        for i, (src, dst) in enumerate(
            ((post_in, post_gain), (freq_in, freq), (perm_in, perm), (par_in, par), (lens_in, lens))
        )
    ]
    for cp in early:
        cp.start()

    peers = [half_at(m)[0] for m in range(1, GN, 2)]
    peers += [at(zl_=q * PN + p_of(o)) for o in range(1, PN)]
    peers += [at(x_=x_of(o)) for o in range(1, XN)]
    peers += [at(y_=y_of(o)) for o in range(1, YN)]
    if KN > 1:
        peers += [at(k_=1 - k)]
    barrier = pltpu.get_barrier_semaphore()
    for peer in peers:
        pl.semaphore_signal(barrier, inc=1, device_id=peer, device_id_type=MESH)

    loc = [
        pltpu.make_async_copy(wout, woutv, ls.at[1]),
        pltpu.make_async_copy(kc, kcv, ls.at[2]),
        pltpu.make_async_copy(vc, vcv, ls.at[3]),
        pltpu.make_async_copy(pk, kall.at[x], ls.at[4]),
        pltpu.make_async_copy(pv, vall.at[x], ls.at[5]),
    ]
    for cp in late + loc:
        cp.start()

    J = width // 256
    TJ = a1.shape[1]
    for cp in early:
        cp.wait()
    hid_f = hid[...].astype(F32)
    mean_square = jnp.mean(hid_f * hid_f, axis=-1, keepdims=True)
    normed = hid_f * lax.rsqrt(mean_square + epsilon) * pre_gain[...].reshape(1, width).astype(F32)
    for part in range(2):
        for j in range(J):
            start = (part * J + j) * 128
            tilesf[part, pl.ds(j * STEPS, STEPS), :] = normed[:, start : start + 128]
        if TJ > J * STEPS:
            tilesf[part, pl.ds(J * STEPS, TJ - J * STEPS), :] = jnp.zeros((TJ - J * STEPS, 128), F32)
    tiles[...] = tilesf[...].astype(BF16)
    pl.semaphore_wait(barrier, len(peers))

    mine = lax.div(z, PN)
    a_copies = []
    h_copies = []
    TH = TJ // 2
    if GN > 2:
        for i, m in enumerate((1, 3)):
            part = tiles.at[q, pl.ds(i * TH, TH)]
            h_copies.append(push(rc(part, relay.at[i], hs.at[i], hr.at[i], half_at(m)[0])))
    for m in range(1, GN, 2):
        where, q_to = half_at(m)
        a_copies.append(push(rc(tiles.at[q_to], a1.at[mine], as_.at[m], ar.at[m], where)))

    half = wq.shape[1] // 2
    w_src = [wq.at[:, pl.ds(0, half)], wq.at[:, pl.ds(half, half)], wk, wv]

    def w_copy(to):
        return rc(w_src[to], wz.at[p, x], ws.at[to], wr.at[x], at(x_=to))

    def w_local(to):
        return pltpu.make_async_copy(w_src[to], wz.at[p, x], ls.at[0])

    for to in range(XN):
        @pl.when(x != to)
        def _():
            w_copy(to).start()

        @pl.when(x == to)
        def _():
            w_local(to).start()

    kv_copies = {}
    positions = kall.shape[1]

    def send_prompt(which, o, part):
        src, dst = ((pk, kall), (pv, vall))[which]
        span = pl.ds(part * (positions // 2), positions // 2)
        cp = rc(
            src.at[span], dst.at[x, span], ks.at[which, o, part], kr.at[which, o, part], at(x_=x_of(o))
        )
        kv_copies[which, o, part] = push(cp)

    def pass_prompt(which, o):
        part = 0 if o == 1 else 1
        kv_copies.pop((which, o, part)).wait_recv()
        block = (kall, vall)[which].at[x_of(-o), pl.ds(part * (positions // 2), positions // 2)]
        cp = rc(block, block, ks.at[which, 2, part], kr.at[which, 2, part], at(x_=x_of(o)))
        kv_copies[which, 2, part] = push(cp)

    send_prompt(0, 1, 0)
    send_prompt(0, 3, 1)
    send_prompt(1, 1, 0)
    send_prompt(1, 3, 1)
    send_prompt(0, 1, 1)
    send_prompt(0, 3, 0)

    a1[mine] = tiles[q]
    for i, cp in enumerate(h_copies):
        cp.wait_recv()
        target = a1.at[lax.rem(mine + (GN - 1, 1)[i], GN), pl.ds(i * TH, TH)]
        a_copies.append(push(rc(relay.at[i], target, fs.at[i], fr.at[i], half_at((1, 3)[i])[0])))
    for to in range(XN):
        @pl.when(x != to)
        def _():
            rc(w_src[to], wz.at[p, to], ws.at[to], wr.at[to], at(x_=to)).wait_recv()

        @pl.when(x == to)
        def _():
            w_local(to).wait()
    wz_copies = []
    for o in range(1, PN):
        wz_copies.append(
            push(rc(wz.at[p], wz.at[p], wzs.at[o], wzr.at[o], at(zl_=q * PN + p_of(o))))
        )
    for cp in a_copies:
        cp.wait_recv()

    for i in range(GN):
        a1f[pl.ds(i * TJ, TJ), :] = a1[i].astype(F32)
    own = (x * YN + y) * KN + k
    rest = jnp.zeros((BLOCK - STEPS * GN, 128), F32)
    for j in range(J):
        lines = [a1f[pl.ds(j * STEPS + t, GN, stride=TJ), :] for t in range(STEPS)]
        xb[own, :, pl.ds(j * 128, 128)] = jnp.concatenate(lines + [rest], axis=0).astype(BF16)

    cols = xb.shape[2] // 2

    def blk(ox, oy):
        return (x_of(-ox) * YN + y_of(-oy)) * KN + k

    def first(b):
        return xb.at[b, :, pl.ds(0, cols)]

    def second(b):
        return xb.at[b, :, pl.ds(cols, cols)]

    px, py, ry, rx, cc = {}, {}, {}, {}, {}

    def forward_y(ox):
        b = blk(ox, 0)
        for o in AROUND[: YN - 1]:
            py[ox, o] = push(rc(first(b), first(b), pys.at[ox, o], pyr.at[ox, o], at(y_=y_of(o))))

    def forward_x(oy):
        b = blk(0, oy)
        for o in AROUND:
            rx[oy, o] = push(rc(second(b), second(b), rxs.at[oy, o], rxr.at[oy, o], at(x_=x_of(o))))

    def to_core(ox, oy):
        if KN > 1:
            b = xb.at[blk(ox, oy)]
            cc[ox, oy] = push(rc(b, b, cs.at[ox, oy], cr.at[ox, oy], at(k_=1 - k)))

    y_around = [o for o in AROUND if o < YN]
    for o in AROUND:
        b = blk(0, 0)
        px[o] = push(rc(first(b), first(b), pxs.at[o], pxr.at[o], at(x_=x_of(o))))
        if o < YN:
            ry[o] = push(rc(second(b), second(b), rys.at[o], ryr.at[o], at(y_=y_of(o))))
    if YN > 1:
        for o in y_around:
            b = blk(0, 0)
            py[0, o] = push(rc(first(b), first(b), pys.at[0, o], pyr.at[0, o], at(y_=y_of(o))))
    forward_x(0)
    to_core(0, 0)
    for o in AROUND:
        px[o].wait_recv()
        for o2 in y_around:
            b = blk(o, 0)
            py[o, o2] = push(rc(first(b), first(b), pys.at[o, o2], pyr.at[o, o2], at(y_=y_of(o2))))
        if o < YN:
            ry[o].wait_recv()
            forward_x(o)

    def gather(ox):
        for oy in [0] + y_around:
            if oy > 0:
                py[ox, oy].wait_recv()
            if ox > 0:
                rx[oy, ox].wait_recv()
            if ox > 0 or oy > 0:
                to_core(ox, oy)

    r_copies = {}

    def project(ox):
        for oy in [0] + y_around:
            if KN > 1:
                cc[ox, oy].wait_recv()
        rows = xb[pl.ds(x_of(-ox) * YK, YK)].reshape(YK * BLOCK, xb.shape[2])
        yf[...] = dot(rows, wz[...].reshape(xb.shape[2], HEAD))
        for h in range(2):
            for t in range(STEPS):
                piece = [
                    yf[pl.ds(t * GN + i * 2 + h, YK, stride=BLOCK), :] for i in range(ZH)
                ]
                sred[ox, h, pl.ds(t * BEAMS, BEAMS), :] = jnp.concatenate(piece, axis=0).astype(BF16)
        r_copies[ox] = push(rc(sred.at[ox], rred.at[ox], rs.at[ox], rr.at[ox], across))

    for which in range(2):
        for o in (1, 3):
            pass_prompt(which, o)
    send_prompt(1, 1, 1)
    send_prompt(1, 3, 0)

    gather(0)
    for cp in wz_copies:
        cp.wait_recv()
    project(0)
    gather(1)
    gather(3)
    project(1)
    gather(2)
    project(3)
    project(2)

    for cp in late:
        cp.wait()
    NT = 2 * XN * STEPS
    at_row = iota((NT, 128), 0)
    place = jnp.zeros((NT, 128), jnp.int32)
    for h in range(2):
        for i in range(XN):
            for t in range(STEPS):
                here = lens[(h * PN + p) * XN + i] + (prompt_total + t)
                place = jnp.where(at_row == (h * XN + i) * STEPS + t, here, place)
    angles = place.astype(F32) * freq[...]
    turns = jnp.round(angles * (1.0 / TURN))
    angles = ((angles - turns * TURN_A) - turns * TURN_B) - turns * TURN_C
    lower = iota((NT, 128), 1) < HEAD // 2
    sines = jnp.sin(angles)
    plain = x == 3
    cos_rows[...] = jnp.where(plain, 1.0, jnp.cos(angles))
    sin_rows[...] = jnp.where(plain, 0.0, jnp.where(lower, -sines, sines))

    scale = jnp.where(x < 2, query_scale, 1.0).astype(F32)
    g_copies = {}
    for ox in (0,) + AROUND:
        xo = x_of(-ox)
        r_copies[ox].wait_recv()
        for h in range(2):
            total = sred[ox, h].astype(F32) + rred[ox, h].astype(F32)
            for t in range(STEPS):
                part = total[t * BEAMS : (t + 1) * BEAMS]
                row = pl.ds((h * XN + xo) * STEPS + t, 1)
                turned = part * cos_rows[row, :] + pltpu.roll(part, HEAD // 2, 1) * sin_rows[row, :]
                gf[ox, h, pl.ds(t * BEAMS, BEAMS), :] = (turned * scale).astype(BF16)
        if ox == 0:
            for h in range(2):
                g[h, x] = gf[0, h]
        else:
            g_copies[ox] = push(rc(gf.at[ox], g.at[:, x], gs.at[ox], gr.at[ox], at(x_=xo)))
    for ox in AROUND:
        g_copies[ox].wait_recv()

    q_copies = {}
    for o in range(1, PN):
        q_copies[o] = push(
            rc(g.at[:, pl.ds(0, 2)], qa.at[p], qs.at[o], qr.at[o], at(zl_=q * PN + p_of(o)))
        )
    for h in range(2):
        qa[p, h] = g[h, 0:2]

    for cp in loc[3:5]:
        cp.wait()
    QR = 2 * ROWS
    eye = iota((QR, 128), 0) == iota((QR, 128), 1)
    upper = iota((16, 128), 0) < 8

    def with_totals(line):
        coarse = line.astype(BF16).astype(F32)
        return jnp.where(upper, coarse, line - coarse).astype(BF16)

    p_copies = {}
    for o in [0] + [o for o in AROUND if o < PN]:
        if o > 0:
            q_copies[o].wait_recv()
        there = p_of(-o)
        queries = qa[there].reshape(2 * QR, HEAD)
        for ox in (0,) + AROUND:
            if o == 0 and ox > 0:
                for key, cp in kv_copies.items():
                    if key[1] == ox:
                        cp.wait_recv()
            xo = x_of(-ox)
            w = weights_of(dot_t(queries, kall[xo])).astype(BF16)
            part = dot(w, jnp.concatenate([vall[xo], jnp.ones((positions, HEAD), BF16)], axis=1))
            if ox == 0:
                acc[...] = part
            else:
                acc[...] += part
        for h in range(2):
            psend[o, h, pl.ds(0, QR), :] = acc[pl.ds(h * QR, QR), pl.ds(0, HEAD)].astype(BF16)
            totals = acc[pl.ds(h * QR, QR), pl.ds(HEAD, HEAD)]
            line = jnp.sum(jnp.where(eye, totals, 0.0), axis=0, keepdims=True)
            psend[o, h, pl.ds(QR, 16), :] = with_totals(line)
        if o > 0:
            p_copies[o] = push(
                rc(psend.at[o], precv.at[o], ps.at[o], pr.at[o], at(zl_=q * PN + there))
            )

    length = lens[c]
    for cp in loc[1:3]:
        cp.wait()
    never = jnp.int32(-1)
    for b in range(BEAMS):
        one = par[1, 0, b]
        two = par[2, 0, b]
        mid = par[1, 0, two]
        me = jnp.int32(b)
        chains = (
            (par[0, 0, b], me, never, never),
            (par[0, 0, one], one, me + BEAMS, never),
            (par[0, 0, mid], mid, two + BEAMS, me + 2 * BEAMS),
        )
        for t in range(STEPS):
            row = t * BEAMS + b
            ancv[pl.ds(row, 1), :] = jnp.full((1, 128), chains[t][0], jnp.int32)
            for u in range(STEPS):
                freshv[u, pl.ds(row, 1), :] = jnp.full((1, 128), chains[t][1 + u], jnp.int32)
    my_q = g[q, 0:2].reshape(QR, HEAD)
    SLOTS = kcv.shape[1]
    anc = ancv[:, :SLOTS]
    anc2 = jnp.concatenate([anc, anc], axis=0)
    in_use = iota((QR, SLOTS), 1) < length
    lane = iota((ROWS, ROWS), 1)
    seen = (lane == freshv[0, :, :ROWS]) | (lane == freshv[1, :, :ROWS]) | (lane == freshv[2, :, :ROWS])
    seen2 = jnp.concatenate([seen.astype(F32)] * 2, axis=0)
    fresh_w = weights_of(dot_t(my_q, g[q, 2])) * seen2
    suf_w = dot(fresh_w.astype(BF16), g[q, 3])
    suf_t = jnp.sum(fresh_w, axis=1, keepdims=True)
    for b in range(BEAMS):
        cached = weights_of(dot_t(my_q, kcv[b]))
        cached = jnp.where((anc2 == b) & in_use, cached, 0.0)
        suf_w = suf_w + dot(cached.astype(BF16), vcv[b])
        suf_t = suf_t + jnp.sum(cached, axis=1, keepdims=True)

    for h in range(2):
        both[h] = psend[0, h].astype(F32)
    for o in range(1, PN):
        p_copies[o].wait_recv()
        for h in range(2):
            both[h] += precv[o, h].astype(F32)
    theirs = both[1 - q]
    osend[pl.ds(0, QR), :] = theirs[:QR].astype(BF16)
    osend[pl.ds(QR, 16), :] = with_totals(theirs[QR : QR + 1] + theirs[QR + 8 : QR + 9])
    o_copy = push(rc(osend, orecv, os_, or_, across))
    ours = both[q]
    o_copy.wait_recv()
    ours = ours + orecv[...].astype(F32)
    line = ours[QR : QR + 1] + ours[QR + 8 : QR + 9]
    column = jnp.sum(jnp.where(eye, line, 0.0), axis=1, keepdims=True)
    attended = ((ours[:QR] + suf_w) / (column + suf_t)).astype(BF16)
    heads = jnp.concatenate([attended[:ROWS], attended[ROWS:]], axis=1)

    loc[0].wait()
    ordered = dot(perm[...], heads).astype(BF16)
    GRP = 4 * ZH
    HALF = YN * GRP
    wide = width // CHUNKS
    bc_copies = []
    by_copies = {}

    def project_out(i):
        for n in range(3):
            part = wide // 3
            at_col = pl.ds(i * wide + n * part, part)
            res = dot(ordered, woutv[:, at_col])
            for kk in range(KN):
                br[kk, i, :, pl.ds(n * part, part)] = res[kk * HALF : (kk + 1) * HALF]
        if KN > 1:
            csend[i] = br[1 - k, i].astype(BF16)
            bc_copies.append(push(rc(csend.at[i], crecv.at[i], bcs.at[i], bcr.at[i], at(k_=1 - k))))

    def over_y(i):
        total = br[k, i]
        if KN > 1:
            bc_copies[i].wait_recv()
            total = total + crecv[i].astype(F32)
        for yy in range(YN):
            s1[i, yy] = total[yy * GRP : (yy + 1) * GRP]
        for o in reversed(y_around):
            v = s1[i, y_of(o)]
            ysend[i, o] = jnp.concatenate([v[:, : wide // 2], v[:, wide // 2 :]], axis=0).astype(BF16)
            by_copies[i, o] = push(
                rc(ysend.at[i, o], yrecv.at[i, o], bys.at[i, o], byr.at[i, o], at(y_=y_of(o)))
            )

    project_out(0)
    for i in range(1, CHUNKS):
        project_out(i)
        over_y(i - 1)
    over_y(CHUNKS - 1)
    bz_copies = []
    kept = []
    is_first = zh == 0
    quarter = wide // 4
    for i in range(CHUNKS):
        total = s1[i, y]
        for o in y_around:
            by_copies[i, o].wait_recv()
            v = yrecv[i, o].astype(F32)
            total = total + jnp.concatenate([v[:GRP], v[GRP:]], axis=1)
        if ZH > 1:
            other = jnp.where(is_first, total[4:8], total[0:4])
            zsend[i] = jnp.concatenate(
                [other[:, n * quarter : (n + 1) * quarter] for n in range(4)], axis=0
            ).astype(BF16)
            bz_copies.append(push(rc(zsend.at[i], zrecv.at[i], bzs.at[i], bzr.at[i], at(zh_=1 - zh))))
            kept.append(jnp.where(is_first, total[0:4], total[4:8]))
        else:
            kept.append(total[0:4])
    at_slot = iota((SLOTS, HEAD), 0)
    stores = []
    for i, (cache, dst) in enumerate(((kcv, out_k), (vcv, out_v))):
        freshk[...] = g[q, 2 + i].astype(F32)
        for b in range(BEAMS):
            two = par[2, 0, b]
            mid = par[1, 0, two]
            block = cache[par[0, 0, mid]].astype(F32)
            for u, row in enumerate((mid, two + BEAMS, b + 2 * BEAMS)):
                block = jnp.where(at_slot == length + u, freshk[pl.ds(row, 1), :], block)
            new[i, b] = block.astype(BF16)
        cp = pltpu.make_async_copy(new.at[i], dst, ls.at[13 + i])
        cp.start()
        stores.append(cp)
    if ZH > 1:
        for i in range(CHUNKS):
            bz_copies[i].wait_recv()
            v = zrecv[i].astype(F32)
            kept[i] = kept[i] + jnp.concatenate([v[n * 4 : (n + 1) * 4] for n in range(4)], axis=1)
    square = sum(jnp.sum(v * v, axis=-1, keepdims=True) for v in kept) * (1.0 / width)
    factor = lax.rsqrt(square + epsilon)
    branch = jnp.concatenate(kept, axis=1) * factor
    result = hid[...].astype(F32) + branch[:STEPS] * post_gain[...].reshape(1, width).astype(F32)
    for t in range(STEPS):
        out_h[t, 0] = result[t : t + 1]

    for cp in sends:
        cp.wait_send()
    for cp in stores:
        cp.wait()
    for to in range(XN):
        @pl.when(x != to)
        def _():
            w_copy(to).wait_send()


def place_kernel(hid, keys, values, out_h, out_k, out_v, hidv, keysv, valuesv, ins, outs):
    loads, stores = [], []
    for i, (src, held, dst) in enumerate(
        ((keys, keysv, out_k), (values, valuesv, out_v), (hid, hidv, out_h))
    ):
        loads.append(pltpu.make_async_copy(src, held, ins.at[i]))
        stores.append(pltpu.make_async_copy(held, dst, outs.at[i]))
    for cp in loads:
        cp.start()
    for load, store in zip(loads, stores):
        load.wait()
        store.start()
    for cp in stores:
        cp.wait()


def order_matrix(dims):
    ZH, YN, KN, ZL = dims
    beams = ZH * YN * KN
    m = np.zeros((KN * YN * ZH * 4, STEPS * beams), np.float32)
    for kk in range(KN):
        for yy in range(YN):
            for hh in range(ZH):
                for t in range(STEPS):
                    m[((kk * YN + yy) * ZH + hh) * 4 + t, t * beams + (hh * YN + yy) * KN + kk] = 1.0
    return m


def body(
    dims,
    hidden_in,
    pre_gain,
    post_gain,
    w_query,
    key_projection_weight,
    value_projection_weight,
    w_out,
    prompt_rotated_keys,
    prompt_value_rows,
    suffix_key_cache,
    suffix_value_cache,
    parents,
    lengths,
):
    ZH, YN, KN, ZL = dims
    PN = ZL // 2
    GN = 2 * ZH
    YK = YN * KN
    beams = ZH * YK
    rows = STEPS * beams
    width = hidden_in.shape[3]
    slots = suffix_key_cache.shape[2]
    positions = prompt_rotated_keys.shape[0]
    prompt_total = positions * ZL * XN
    J = width // 256
    TJ = -(-(STEPS * J) // 16) * 16
    frequency = 1.0 / rope_base ** (np.arange(HEAD // 2) * 2.0 / HEAD)
    freq = jnp.asarray(np.concatenate([frequency, frequency])[None], F32)
    perm = jnp.asarray(order_matrix(dims), BF16)
    hbm = pl.BlockSpec(memory_space=pltpu.HBM)
    vmem = pl.BlockSpec(memory_space=pltpu.VMEM)
    wrows = w_query.shape[0]
    grp = 4 * ZH
    half = YN * grp
    wide = width // CHUNKS
    V = pltpu.VMEM
    D = pltpu.SemaphoreType.DMA
    scratch = [
        V((STEPS, width), BF16),
        V((width,), BF16),
        V((width,), BF16),
        V((1, HEAD), F32),
        V(perm.shape, BF16),
        pltpu.SMEM(parents.shape, jnp.int32),
        pltpu.SMEM(lengths.shape, jnp.int32),
        V((2, TJ, 128), BF16),
        V((2, TJ // 2, 128), BF16),
        V((2, TJ, 128), F32),
        V((2 * XN * STEPS, 128), F32),
        V((2 * XN * STEPS, 128), F32),
        V((GN, TJ, 128), BF16),
        V((GN * TJ, 128), F32),
        V((XN * YK, BLOCK, width // 2), BF16),
        V((PN, XN, wrows, HEAD), BF16),
        V((YK * BLOCK, HEAD), F32),
        V((XN, 2, rows, HEAD), BF16),
        V((XN, 2, rows, HEAD), BF16),
        V((2, XN, rows, HEAD), BF16),
        V((XN, 2, rows, HEAD), BF16),
        V((PN, 2, 2, rows, HEAD), BF16),
        V((XN, positions, HEAD), BF16),
        V((XN, positions, HEAD), BF16),
        V((4 * rows, 2 * HEAD), F32),
        V((PN, 2, 2 * rows + 16, HEAD), BF16),
        V((PN, 2, 2 * rows + 16, HEAD), BF16),
        V((2, 2 * rows + 16, HEAD), F32),
        V((2 * rows + 16, HEAD), BF16),
        V((2 * rows + 16, HEAD), BF16),
        V(w_out.shape, BF16),
        V((beams, slots, HEAD), BF16),
        V((beams, slots, HEAD), BF16),
        V((rows, 128), jnp.int32),
        V((STEPS, rows, 128), jnp.int32),
        V((KN, CHUNKS, half, wide), F32),
        V((CHUNKS, half, wide), BF16),
        V((CHUNKS, half, wide), BF16),
        V((CHUNKS, YN, grp, wide), F32),
        V((CHUNKS, YN, 2 * grp, wide // 2), BF16),
        V((CHUNKS, YN, 2 * grp, wide // 2), BF16),
        V((CHUNKS, 16, wide // 4), BF16),
        V((CHUNKS, 16, wide // 4), BF16),
        V((rows, HEAD), F32),
        V((2, beams, slots, HEAD), BF16),
        D((4,)), D((4,)), D((2,)), D((2,)), D((2,)), D((2,)), D((XN,)), D((XN,)), D((PN,)), D((PN,)), D((2, XN, 2)), D((2, XN, 2)),
        D((XN,)), D((XN,)), D((XN, 4)), D((XN, 4)), D((4,)), D((4,)), D((4, XN)), D((4, XN)),
        D((XN, 4)), D((XN, 4)), D((XN,)), D((XN,)), D((XN,)), D((XN,)), D((PN,)), D((PN,)),
        D((PN,)), D((PN,)), D, D, D((CHUNKS,)), D((CHUNKS,)), D((CHUNKS, 4)), D((CHUNKS, 4)),
        D((CHUNKS,)), D((CHUNKS,)), D((16,)),
    ]
    keys_in = suffix_key_cache.reshape(beams, slots, HEAD)
    values_in = suffix_value_cache.reshape(beams, slots, HEAD)
    hidden, keys_new, values_new = pl.pallas_call(
        functools.partial(kernel, dims, prompt_total),
        out_shape=(
            jax.ShapeDtypeStruct((STEPS, 1, 1, width), F32),
            jax.ShapeDtypeStruct((beams, slots, HEAD), BF16),
            jax.ShapeDtypeStruct((beams, slots, HEAD), BF16),
        ),
        in_specs=[hbm] * 15,
        out_specs=(vmem, hbm, hbm),
        scratch_shapes=scratch,
        compiler_params=pltpu.CompilerParams(
            collective_id=0, has_side_effects=True, vmem_limit_bytes=63 * 1024 * 1024
        ),
    )(
        hidden_in.reshape(STEPS, width),
        pre_gain,
        post_gain,
        freq,
        perm,
        w_query,
        key_projection_weight,
        value_projection_weight,
        w_out,
        prompt_rotated_keys,
        prompt_value_rows,
        keys_in,
        values_in,
        parents,
        lengths,
    )
    hidden_out, keys_out, values_out = pl.pallas_call(
        place_kernel,
        out_shape=(
            jax.ShapeDtypeStruct((STEPS, 1, 1, width), F32),
            jax.ShapeDtypeStruct((beams, slots, HEAD), BF16),
            jax.ShapeDtypeStruct((beams, slots, HEAD), BF16),
        ),
        in_specs=[hbm] * 3,
        out_specs=(hbm, hbm, hbm),
        scratch_shapes=[
            V((STEPS, 1, 1, width), F32),
            V((beams, slots, HEAD), BF16),
            V((beams, slots, HEAD), BF16),
            D((3,)),
            D((3,)),
        ],
        compiler_params=pltpu.CompilerParams(vmem_limit_bytes=63 * 1024 * 1024),
    )(hidden, keys_new, values_new)
    return (
        hidden_out,
        keys_out.reshape(1, beams, slots, HEAD),
        values_out.reshape(1, beams, slots, HEAD),
    )


def solution(mesh, dims=(2, 4, 2, 8)):
    placed = (
        P(None, "context", "sample", None),
        P(),
        P(),
        P("context", "sample"),
        P("context", "sample"),
        P("context", "sample"),
        P("sample", None),
        P("context", "sample"),
        P("context", "sample"),
        P("context", None, None, "sample"),
        P("context", None, None, "sample"),
        P(None, "context", None),
        P(),
    )
    return jax.shard_map(
        functools.partial(body, dims),
        mesh=mesh,
        in_specs=placed,
        out_specs=(
            P(None, "context", "sample", None),
            P("context", None, None, "sample"),
            P("context", None, None, "sample"),
        ),
        check_vma=False,
    )
```

```python
import functools

import jax
import jax.numpy as jnp
import numpy as np
from jax import lax
from jax.experimental import pallas as pl
from jax.experimental.pallas import tpu as pltpu
from jax.sharding import PartitionSpec as P

HEAD = 128
STEPS = 3
XN = 4
BLOCK = 16
CHUNKS = 3

epsilon = 1e-06
query_scale = 144.0 ** (-0.5)
rope_base = 10000.0
logit_cap = 50.0
TURN = 2 * np.pi
TURN_A = 6.28125
TURN_B = float(np.float32(np.round((TURN - TURN_A) * 2.0**20) / 2.0**20))
TURN_C = float(TURN - TURN_A - TURN_B)
MESH = pl.DeviceIdType.MESH
F32 = jnp.float32
BF16 = jnp.bfloat16
AROUND = (1, 3, 2)


def weights_of(scores):
    return jnp.exp(logit_cap * jnp.tanh(scores * (1.0 / logit_cap)))


def dot_t(a, b):
    return lax.dot_general(a, b, (((1,), (1,)), ((), ())), preferred_element_type=F32)


def dot(a, b):
    return jnp.dot(a, b, preferred_element_type=F32)


def iota(shape, axis):
    return lax.broadcasted_iota(jnp.int32, shape, axis)


def kernel(
    dims, prompt_total,
    hid_in, pre_in, post_in, freq_in, perm_in, wq, wk, wv, wout, pk, pv, kc, vc, par_in, lens_in,
    out_h, out_k, out_v,
    hid, pre_gain, post_gain, freq, perm, par, lens,
    tiles, relay, tilesf, cos_rows, sin_rows, a1, a1f, xb, wz, yf, sred, rred, g, gf, qa, kall, vall, acc,
    psend, precv, both, osend, orecv, woutv, kcv, vcv, ancv, freshv, br, csend, crecv, s1, ysend,
    yrecv, zsend, zrecv, freshk, new,
    as_, ar, hs, hr, fs, fr, ws, wr, wzs, wzr, ks, kr, pxs, pxr, pys, pyr, rys, ryr, rxs, rxr, cs, cr, rs, rr, gs,
    gr, qs, qr, ps, pr, os_, or_, bcs, bcr, bys, byr, bzs, bzr, ls,
):
    ZH, YN, KN, ZL = dims
    ZN = ZH * ZL
    PN = ZL // 2
    GN = 2 * ZH
    YK = YN * KN
    BEAMS = ZH * YK
    ROWS = STEPS * BEAMS
    s = lax.axis_index("sample")
    c = lax.axis_index("context")
    zh = lax.div(s, YK)
    y = lax.div(lax.rem(s, YK), KN)
    k = lax.rem(s, KN)
    zl = lax.div(c, XN)
    x = lax.rem(c, XN)
    z = zh * ZL + zl
    q = lax.div(zl, PN)
    p = lax.rem(zl, PN)
    width = hid_in.shape[1]

    def at(zh_=None, y_=None, k_=None, zl_=None, x_=None):
        zh_ = zh if zh_ is None else zh_
        y_ = y if y_ is None else y_
        k_ = k if k_ is None else k_
        zl_ = zl if zl_ is None else zl_
        x_ = x if x_ is None else x_
        return {"sample": zh_ * YK + y_ * KN + k_, "context": zl_ * XN + x_}

    def rc(src, dst, ssem, rsem, where):
        return pltpu.make_async_remote_copy(
            src_ref=src, dst_ref=dst, send_sem=ssem, recv_sem=rsem,
            device_id=where, device_id_type=MESH,
        )

    sends = []

    def push(cp):
        cp.start()
        sends.append(cp)
        return cp

    def x_of(o):
        return lax.rem(x + o + XN, XN)

    def y_of(o):
        return lax.rem(y + o + YN, YN)

    def p_of(o):
        return lax.rem(p + o + PN, PN)

    def half_at(m):
        zz = lax.rem(z + PN * m, ZN)
        zl_ = lax.rem(zz, ZL)
        return at(zh_=lax.div(zz, ZL), zl_=zl_), lax.div(zl_, PN)

    across = at(zl_=(1 - q) * PN + p)

    early = [pltpu.make_async_copy(hid_in, hid, ls.at[6]), pltpu.make_async_copy(pre_in, pre_gain, ls.at[7])]
    late = [
        pltpu.make_async_copy(src, dst, ls.at[8 + i])
        for i, (src, dst) in enumerate(
            ((post_in, post_gain), (freq_in, freq), (perm_in, perm), (par_in, par), (lens_in, lens))
        )
    ]
    for cp in early:
        cp.start()

    peers = [half_at(m)[0] for m in range(1, GN, 2)]
    peers += [at(zl_=q * PN + p_of(o)) for o in range(1, PN)]
    peers += [at(x_=x_of(o)) for o in range(1, XN)]
    peers += [at(y_=y_of(o)) for o in range(1, YN)]
    if KN > 1:
        peers += [at(k_=1 - k)]
    barrier = pltpu.get_barrier_semaphore()
    for peer in peers:
        pl.semaphore_signal(barrier, inc=1, device_id=peer, device_id_type=MESH)

    loc = [
        pltpu.make_async_copy(wout, woutv, ls.at[1]),
        pltpu.make_async_copy(kc, kcv, ls.at[2]),
        pltpu.make_async_copy(vc, vcv, ls.at[3]),
        pltpu.make_async_copy(pk, kall.at[x], ls.at[4]),
        pltpu.make_async_copy(pv, vall.at[x], ls.at[5]),
    ]
    for cp in late + loc:
        cp.start()

    J = width // 256
    TJ = a1.shape[1]
    for cp in early:
        cp.wait()
    hid_f = hid[...].astype(F32)
    mean_square = jnp.mean(hid_f * hid_f, axis=-1, keepdims=True)
    normed = hid_f * lax.rsqrt(mean_square + epsilon) * pre_gain[...].reshape(1, width).astype(F32)
    for part in range(2):
        for j in range(J):
            start = (part * J + j) * 128
            tilesf[part, pl.ds(j * STEPS, STEPS), :] = normed[:, start : start + 128]
        if TJ > J * STEPS:
            tilesf[part, pl.ds(J * STEPS, TJ - J * STEPS), :] = jnp.zeros((TJ - J * STEPS, 128), F32)
    tiles[...] = tilesf[...].astype(BF16)
    pl.semaphore_wait(barrier, len(peers))

    mine = lax.div(z, PN)
    a_copies = []
    h_copies = []
    TH = TJ // 2
    if GN > 2:
        for i, m in enumerate((1, 3)):
            part = tiles.at[q, pl.ds(i * TH, TH)]
            h_copies.append(push(rc(part, relay.at[i], hs.at[i], hr.at[i], half_at(m)[0])))
    for m in range(1, GN, 2):
        where, q_to = half_at(m)
        a_copies.append(push(rc(tiles.at[q_to], a1.at[mine], as_.at[m], ar.at[m], where)))

    half = wq.shape[1] // 2
    w_src = [wq.at[:, pl.ds(0, half)], wq.at[:, pl.ds(half, half)], wk, wv]

    def w_copy(to):
        return rc(w_src[to], wz.at[p, x], ws.at[to], wr.at[x], at(x_=to))

    def w_local(to):
        return pltpu.make_async_copy(w_src[to], wz.at[p, x], ls.at[0])

    for to in range(XN):
        @pl.when(x != to)
        def _():
            w_copy(to).start()

        @pl.when(x == to)
        def _():
            w_local(to).start()

    kv_copies = {}
    positions = kall.shape[1]

    def send_prompt(which, o, part):
        src, dst = ((pk, kall), (pv, vall))[which]
        span = pl.ds(part * (positions // 2), positions // 2)
        cp = rc(
            src.at[span], dst.at[x, span], ks.at[which, o, part], kr.at[which, o, part], at(x_=x_of(o))
        )
        kv_copies[which, o, part] = push(cp)

    def pass_prompt(which, o):
        part = 0 if o == 1 else 1
        kv_copies.pop((which, o, part)).wait_recv()
        block = (kall, vall)[which].at[x_of(-o), pl.ds(part * (positions // 2), positions // 2)]
        cp = rc(block, block, ks.at[which, 2, part], kr.at[which, 2, part], at(x_=x_of(o)))
        kv_copies[which, 2, part] = push(cp)

    send_prompt(0, 1, 0)
    send_prompt(0, 3, 1)
    send_prompt(1, 1, 0)
    send_prompt(1, 3, 1)
    send_prompt(0, 1, 1)
    send_prompt(0, 3, 0)

    a1[mine] = tiles[q]
    for i, cp in enumerate(h_copies):
        cp.wait_recv()
        target = a1.at[lax.rem(mine + (GN - 1, 1)[i], GN), pl.ds(i * TH, TH)]
        a_copies.append(push(rc(relay.at[i], target, fs.at[i], fr.at[i], half_at((1, 3)[i])[0])))
    for to in range(XN):
        @pl.when(x != to)
        def _():
            rc(w_src[to], wz.at[p, to], ws.at[to], wr.at[to], at(x_=to)).wait_recv()

        @pl.when(x == to)
        def _():
            w_local(to).wait()
    wz_copies = []
    for o in range(1, PN):
        wz_copies.append(
            push(rc(wz.at[p], wz.at[p], wzs.at[o], wzr.at[o], at(zl_=q * PN + p_of(o))))
        )
    for cp in a_copies:
        cp.wait_recv()

    for i in range(GN):
        a1f[pl.ds(i * TJ, TJ), :] = a1[i].astype(F32)
    own = (x * YN + y) * KN + k
    rest = jnp.zeros((BLOCK - STEPS * GN, 128), F32)
    for j in range(J):
        lines = [a1f[pl.ds(j * STEPS + t, GN, stride=TJ), :] for t in range(STEPS)]
        xb[own, :, pl.ds(j * 128, 128)] = jnp.concatenate(lines + [rest], axis=0).astype(BF16)

    cols = xb.shape[2] // 2

    def blk(ox, oy):
        return (x_of(-ox) * YN + y_of(-oy)) * KN + k

    def first(b):
        return xb.at[b, :, pl.ds(0, cols)]

    def second(b):
        return xb.at[b, :, pl.ds(cols, cols)]

    px, py, ry, rx, cc = {}, {}, {}, {}, {}

    def forward_y(ox):
        b = blk(ox, 0)
        for o in AROUND[: YN - 1]:
            py[ox, o] = push(rc(first(b), first(b), pys.at[ox, o], pyr.at[ox, o], at(y_=y_of(o))))

    def forward_x(oy):
        b = blk(0, oy)
        for o in AROUND:
            rx[oy, o] = push(rc(second(b), second(b), rxs.at[oy, o], rxr.at[oy, o], at(x_=x_of(o))))

    def to_core(ox, oy):
        if KN > 1:
            b = xb.at[blk(ox, oy)]
            cc[ox, oy] = push(rc(b, b, cs.at[ox, oy], cr.at[ox, oy], at(k_=1 - k)))

    y_around = [o for o in AROUND if o < YN]
    for o in AROUND:
        b = blk(0, 0)
        px[o] = push(rc(first(b), first(b), pxs.at[o], pxr.at[o], at(x_=x_of(o))))
        if o < YN:
            ry[o] = push(rc(second(b), second(b), rys.at[o], ryr.at[o], at(y_=y_of(o))))
    if YN > 1:
        for o in y_around:
            b = blk(0, 0)
            py[0, o] = push(rc(first(b), first(b), pys.at[0, o], pyr.at[0, o], at(y_=y_of(o))))
    forward_x(0)
    to_core(0, 0)
    for o in AROUND:
        px[o].wait_recv()
        for o2 in y_around:
            b = blk(o, 0)
            py[o, o2] = push(rc(first(b), first(b), pys.at[o, o2], pyr.at[o, o2], at(y_=y_of(o2))))
        if o < YN:
            ry[o].wait_recv()
            forward_x(o)

    def gather(ox):
        for oy in [0] + y_around:
            if oy > 0:
                py[ox, oy].wait_recv()
            if ox > 0:
                rx[oy, ox].wait_recv()
            if ox > 0 or oy > 0:
                to_core(ox, oy)

    r_copies = {}

    def project(ox):
        for oy in [0] + y_around:
            if KN > 1:
                cc[ox, oy].wait_recv()
        rows = xb[pl.ds(x_of(-ox) * YK, YK)].reshape(YK * BLOCK, xb.shape[2])
        yf[...] = dot(rows, wz[...].reshape(xb.shape[2], HEAD))
        for h in range(2):
            for t in range(STEPS):
                piece = [
                    yf[pl.ds(t * GN + i * 2 + h, YK, stride=BLOCK), :] for i in range(ZH)
                ]
                sred[ox, h, pl.ds(t * BEAMS, BEAMS), :] = jnp.concatenate(piece, axis=0).astype(BF16)
        r_copies[ox] = push(rc(sred.at[ox], rred.at[ox], rs.at[ox], rr.at[ox], across))

    for which in range(2):
        for o in (1, 3):
            pass_prompt(which, o)
    send_prompt(1, 1, 1)
    send_prompt(1, 3, 0)

    gather(0)
    for cp in wz_copies:
        cp.wait_recv()
    project(0)
    gather(1)
    gather(3)
    project(1)
    gather(2)
    project(3)
    project(2)

    for cp in late:
        cp.wait()
    NT = 2 * XN * STEPS
    at_row = iota((NT, 128), 0)
    place = jnp.zeros((NT, 128), jnp.int32)
    for h in range(2):
        for i in range(XN):
            for t in range(STEPS):
                here = lens[(h * PN + p) * XN + i] + (prompt_total + t)
                place = jnp.where(at_row == (h * XN + i) * STEPS + t, here, place)
    angles = place.astype(F32) * freq[...]
    turns = jnp.round(angles * (1.0 / TURN))
    angles = ((angles - turns * TURN_A) - turns * TURN_B) - turns * TURN_C
    lower = iota((NT, 128), 1) < HEAD // 2
    sines = jnp.sin(angles)
    plain = x == 3
    cos_rows[...] = jnp.where(plain, 1.0, jnp.cos(angles))
    sin_rows[...] = jnp.where(plain, 0.0, jnp.where(lower, -sines, sines))

    scale = jnp.where(x < 2, query_scale, 1.0).astype(F32)
    g_copies = {}
    for ox in (0,) + AROUND:
        xo = x_of(-ox)
        r_copies[ox].wait_recv()
        for h in range(2):
            total = sred[ox, h].astype(F32) + rred[ox, h].astype(F32)
            for t in range(STEPS):
                part = total[t * BEAMS : (t + 1) * BEAMS]
                row = pl.ds((h * XN + xo) * STEPS + t, 1)
                turned = part * cos_rows[row, :] + pltpu.roll(part, HEAD // 2, 1) * sin_rows[row, :]
                gf[ox, h, pl.ds(t * BEAMS, BEAMS), :] = (turned * scale).astype(BF16)
        if ox == 0:
            for h in range(2):
                g[h, x] = gf[0, h]
        else:
            g_copies[ox] = push(rc(gf.at[ox], g.at[:, x], gs.at[ox], gr.at[ox], at(x_=xo)))
    for ox in AROUND:
        g_copies[ox].wait_recv()

    q_copies = {}
    for o in range(1, PN):
        q_copies[o] = push(
            rc(g.at[:, pl.ds(0, 2)], qa.at[p], qs.at[o], qr.at[o], at(zl_=q * PN + p_of(o)))
        )
    for h in range(2):
        qa[p, h] = g[h, 0:2]

    for cp in loc[3:5]:
        cp.wait()
    QR = 2 * ROWS
    eye = iota((QR, 128), 0) == iota((QR, 128), 1)
    upper = iota((16, 128), 0) < 8

    def with_totals(line):
        coarse = line.astype(BF16).astype(F32)
        return jnp.where(upper, coarse, line - coarse).astype(BF16)

    p_copies = {}
    for o in [0] + [o for o in AROUND if o < PN]:
        if o > 0:
            q_copies[o].wait_recv()
        there = p_of(-o)
        queries = qa[there].reshape(2 * QR, HEAD)
        for ox in (0,) + AROUND:
            if o == 0 and ox > 0:
                for key, cp in kv_copies.items():
                    if key[1] == ox:
                        cp.wait_recv()
            xo = x_of(-ox)
            w = weights_of(dot_t(queries, kall[xo])).astype(BF16)
            part = dot(w, jnp.concatenate([vall[xo], jnp.ones((positions, HEAD), BF16)], axis=1))
            if ox == 0:
                acc[...] = part
            else:
                acc[...] += part
        for h in range(2):
            psend[o, h, pl.ds(0, QR), :] = acc[pl.ds(h * QR, QR), pl.ds(0, HEAD)].astype(BF16)
            totals = acc[pl.ds(h * QR, QR), pl.ds(HEAD, HEAD)]
            line = jnp.sum(jnp.where(eye, totals, 0.0), axis=0, keepdims=True)
            psend[o, h, pl.ds(QR, 16), :] = with_totals(line)
        if o > 0:
            p_copies[o] = push(
                rc(psend.at[o], precv.at[o], ps.at[o], pr.at[o], at(zl_=q * PN + there))
            )

    length = lens[c]
    for cp in loc[1:3]:
        cp.wait()
    never = jnp.int32(-1)
    for b in range(BEAMS):
        one = par[1, 0, b]
        two = par[2, 0, b]
        mid = par[1, 0, two]
        me = jnp.int32(b)
        chains = (
            (par[0, 0, b], me, never, never),
            (par[0, 0, one], one, me + BEAMS, never),
            (par[0, 0, mid], mid, two + BEAMS, me + 2 * BEAMS),
        )
        for t in range(STEPS):
            row = t * BEAMS + b
            ancv[pl.ds(row, 1), :] = jnp.full((1, 128), chains[t][0], jnp.int32)
            for u in range(STEPS):
                freshv[u, pl.ds(row, 1), :] = jnp.full((1, 128), chains[t][1 + u], jnp.int32)
    my_q = g[q, 0:2].reshape(QR, HEAD)
    SLOTS = kcv.shape[1]
    anc = ancv[:, :SLOTS]
    anc2 = jnp.concatenate([anc, anc], axis=0)
    in_use = iota((QR, SLOTS), 1) < length
    lane = iota((ROWS, ROWS), 1)
    seen = (lane == freshv[0, :, :ROWS]) | (lane == freshv[1, :, :ROWS]) | (lane == freshv[2, :, :ROWS])
    seen2 = jnp.concatenate([seen.astype(F32)] * 2, axis=0)
    fresh_w = weights_of(dot_t(my_q, g[q, 2])) * seen2
    suf_w = dot(fresh_w.astype(BF16), g[q, 3])
    suf_t = jnp.sum(fresh_w, axis=1, keepdims=True)
    for b in range(BEAMS):
        cached = weights_of(dot_t(my_q, kcv[b]))
        cached = jnp.where((anc2 == b) & in_use, cached, 0.0)
        suf_w = suf_w + dot(cached.astype(BF16), vcv[b])
        suf_t = suf_t + jnp.sum(cached, axis=1, keepdims=True)

    for h in range(2):
        both[h] = psend[0, h].astype(F32)
    for o in range(1, PN):
        p_copies[o].wait_recv()
        for h in range(2):
            both[h] += precv[o, h].astype(F32)
    theirs = both[1 - q]
    osend[pl.ds(0, QR), :] = theirs[:QR].astype(BF16)
    osend[pl.ds(QR, 16), :] = with_totals(theirs[QR : QR + 1] + theirs[QR + 8 : QR + 9])
    o_copy = push(rc(osend, orecv, os_, or_, across))
    ours = both[q]
    o_copy.wait_recv()
    ours = ours + orecv[...].astype(F32)
    line = ours[QR : QR + 1] + ours[QR + 8 : QR + 9]
    column = jnp.sum(jnp.where(eye, line, 0.0), axis=1, keepdims=True)
    attended = ((ours[:QR] + suf_w) / (column + suf_t)).astype(BF16)
    heads = jnp.concatenate([attended[:ROWS], attended[ROWS:]], axis=1)

    loc[0].wait()
    ordered = dot(perm[...], heads).astype(BF16)
    GRP = 4 * ZH
    HALF = YN * GRP
    wide = width // CHUNKS
    bc_copies = []
    by_copies = {}

    def project_out(i):
        for n in range(3):
            part = wide // 3
            at_col = pl.ds(i * wide + n * part, part)
            res = dot(ordered, woutv[:, at_col])
            for kk in range(KN):
                br[kk, i, :, pl.ds(n * part, part)] = res[kk * HALF : (kk + 1) * HALF]
        if KN > 1:
            csend[i] = br[1 - k, i].astype(BF16)
            bc_copies.append(push(rc(csend.at[i], crecv.at[i], bcs.at[i], bcr.at[i], at(k_=1 - k))))

    def over_y(i):
        total = br[k, i]
        if KN > 1:
            bc_copies[i].wait_recv()
            total = total + crecv[i].astype(F32)
        for yy in range(YN):
            s1[i, yy] = total[yy * GRP : (yy + 1) * GRP]
        for o in reversed(y_around):
            v = s1[i, y_of(o)]
            ysend[i, o] = jnp.concatenate([v[:, : wide // 2], v[:, wide // 2 :]], axis=0).astype(BF16)
            by_copies[i, o] = push(
                rc(ysend.at[i, o], yrecv.at[i, o], bys.at[i, o], byr.at[i, o], at(y_=y_of(o)))
            )

    project_out(0)
    for i in range(1, CHUNKS):
        project_out(i)
        over_y(i - 1)
    over_y(CHUNKS - 1)
    bz_copies = []
    before = len(sends)
    kept = []
    is_first = zh == 0
    quarter = wide // 4
    for i in range(CHUNKS):
        total = s1[i, y]
        for o in y_around:
            by_copies[i, o].wait_recv()
            v = yrecv[i, o].astype(F32)
            total = total + jnp.concatenate([v[:GRP], v[GRP:]], axis=1)
        if ZH > 1:
            other = jnp.where(is_first, total[4:8], total[0:4])
            zsend[i] = jnp.concatenate(
                [other[:, n * quarter : (n + 1) * quarter] for n in range(4)], axis=0
            ).astype(BF16)
            bz_copies.append(push(rc(zsend.at[i], zrecv.at[i], bzs.at[i], bzr.at[i], at(zh_=1 - zh))))
            kept.append(jnp.where(is_first, total[0:4], total[4:8]))
        else:
            kept.append(total[0:4])
    at_slot = iota((SLOTS, HEAD), 0)
    stores = []
    for i, (cache, dst) in enumerate(((kcv, out_k), (vcv, out_v))):
        freshk[...] = g[q, 2 + i].astype(F32)
        for b in range(BEAMS):
            two = par[2, 0, b]
            mid = par[1, 0, two]
            block = cache[par[0, 0, mid]].astype(F32)
            for u, row in enumerate((mid, two + BEAMS, b + 2 * BEAMS)):
                block = jnp.where(at_slot == length + u, freshk[pl.ds(row, 1), :], block)
            new[i, b] = block.astype(BF16)
        cp = pltpu.make_async_copy(new.at[i], dst, ls.at[13 + i])
        cp.start()
        stores.append(cp)
    for cp in sends[:before]:
        cp.wait_send()
    for to in range(XN):
        @pl.when(x != to)
        def _():
            w_copy(to).wait_send()
    if ZH > 1:
        for i in range(CHUNKS):
            bz_copies[i].wait_recv()
            v = zrecv[i].astype(F32)
            kept[i] = kept[i] + jnp.concatenate([v[n * 4 : (n + 1) * 4] for n in range(4)], axis=1)
    square = sum(jnp.sum(v * v, axis=-1, keepdims=True) for v in kept) * (1.0 / width)
    factor = lax.rsqrt(square + epsilon)
    branch = jnp.concatenate(kept, axis=1) * factor
    result = hid[...].astype(F32) + branch[:STEPS] * post_gain[...].reshape(1, width).astype(F32)
    for t in range(STEPS):
        out_h[t, 0] = result[t : t + 1]

    for cp in sends[before:]:
        cp.wait_send()
    for cp in stores:
        cp.wait()


def place_kernel(hid, keys, values, out_h, out_k, out_v, hidv, keysv, valuesv, ins, outs):
    loads, stores = [], []
    for i, (src, held, dst) in enumerate(
        ((keys, keysv, out_k), (values, valuesv, out_v), (hid, hidv, out_h))
    ):
        loads.append(pltpu.make_async_copy(src, held, ins.at[i]))
        stores.append(pltpu.make_async_copy(held, dst, outs.at[i]))
    for cp in loads:
        cp.start()
    for load, store in zip(loads, stores):
        load.wait()
        store.start()
    for cp in stores:
        cp.wait()


def order_matrix(dims):
    ZH, YN, KN, ZL = dims
    beams = ZH * YN * KN
    m = np.zeros((KN * YN * ZH * 4, STEPS * beams), np.float32)
    for kk in range(KN):
        for yy in range(YN):
            for hh in range(ZH):
                for t in range(STEPS):
                    m[((kk * YN + yy) * ZH + hh) * 4 + t, t * beams + (hh * YN + yy) * KN + kk] = 1.0
    return m


def body(
    dims,
    hidden_in,
    pre_gain,
    post_gain,
    w_query,
    key_projection_weight,
    value_projection_weight,
    w_out,
    prompt_rotated_keys,
    prompt_value_rows,
    suffix_key_cache,
    suffix_value_cache,
    parents,
    lengths,
):
    ZH, YN, KN, ZL = dims
    PN = ZL // 2
    GN = 2 * ZH
    YK = YN * KN
    beams = ZH * YK
    rows = STEPS * beams
    width = hidden_in.shape[3]
    slots = suffix_key_cache.shape[2]
    positions = prompt_rotated_keys.shape[0]
    prompt_total = positions * ZL * XN
    J = width // 256
    TJ = -(-(STEPS * J) // 16) * 16
    frequency = 1.0 / rope_base ** (np.arange(HEAD // 2) * 2.0 / HEAD)
    freq = jnp.asarray(np.concatenate([frequency, frequency])[None], F32)
    perm = jnp.asarray(order_matrix(dims), BF16)
    hbm = pl.BlockSpec(memory_space=pltpu.HBM)
    vmem = pl.BlockSpec(memory_space=pltpu.VMEM)
    wrows = w_query.shape[0]
    grp = 4 * ZH
    half = YN * grp
    wide = width // CHUNKS
    V = pltpu.VMEM
    D = pltpu.SemaphoreType.DMA
    scratch = [
        V((STEPS, width), BF16),
        V((width,), BF16),
        V((width,), BF16),
        V((1, HEAD), F32),
        V(perm.shape, BF16),
        pltpu.SMEM(parents.shape, jnp.int32),
        pltpu.SMEM(lengths.shape, jnp.int32),
        V((2, TJ, 128), BF16),
        V((2, TJ // 2, 128), BF16),
        V((2, TJ, 128), F32),
        V((2 * XN * STEPS, 128), F32),
        V((2 * XN * STEPS, 128), F32),
        V((GN, TJ, 128), BF16),
        V((GN * TJ, 128), F32),
        V((XN * YK, BLOCK, width // 2), BF16),
        V((PN, XN, wrows, HEAD), BF16),
        V((YK * BLOCK, HEAD), F32),
        V((XN, 2, rows, HEAD), BF16),
        V((XN, 2, rows, HEAD), BF16),
        V((2, XN, rows, HEAD), BF16),
        V((XN, 2, rows, HEAD), BF16),
        V((PN, 2, 2, rows, HEAD), BF16),
        V((XN, positions, HEAD), BF16),
        V((XN, positions, HEAD), BF16),
        V((4 * rows, 2 * HEAD), F32),
        V((PN, 2, 2 * rows + 16, HEAD), BF16),
        V((PN, 2, 2 * rows + 16, HEAD), BF16),
        V((2, 2 * rows + 16, HEAD), F32),
        V((2 * rows + 16, HEAD), BF16),
        V((2 * rows + 16, HEAD), BF16),
        V(w_out.shape, BF16),
        V((beams, slots, HEAD), BF16),
        V((beams, slots, HEAD), BF16),
        V((rows, 128), jnp.int32),
        V((STEPS, rows, 128), jnp.int32),
        V((KN, CHUNKS, half, wide), F32),
        V((CHUNKS, half, wide), BF16),
        V((CHUNKS, half, wide), BF16),
        V((CHUNKS, YN, grp, wide), F32),
        V((CHUNKS, YN, 2 * grp, wide // 2), BF16),
        V((CHUNKS, YN, 2 * grp, wide // 2), BF16),
        V((CHUNKS, 16, wide // 4), BF16),
        V((CHUNKS, 16, wide // 4), BF16),
        V((rows, HEAD), F32),
        V((2, beams, slots, HEAD), BF16),
        D((4,)), D((4,)), D((2,)), D((2,)), D((2,)), D((2,)), D((XN,)), D((XN,)), D((PN,)), D((PN,)), D((2, XN, 2)), D((2, XN, 2)),
        D((XN,)), D((XN,)), D((XN, 4)), D((XN, 4)), D((4,)), D((4,)), D((4, XN)), D((4, XN)),
        D((XN, 4)), D((XN, 4)), D((XN,)), D((XN,)), D((XN,)), D((XN,)), D((PN,)), D((PN,)),
        D((PN,)), D((PN,)), D, D, D((CHUNKS,)), D((CHUNKS,)), D((CHUNKS, 4)), D((CHUNKS, 4)),
        D((CHUNKS,)), D((CHUNKS,)), D((16,)),
    ]
    keys_in = suffix_key_cache.reshape(beams, slots, HEAD)
    values_in = suffix_value_cache.reshape(beams, slots, HEAD)
    hidden, keys_new, values_new = pl.pallas_call(
        functools.partial(kernel, dims, prompt_total),
        out_shape=(
            jax.ShapeDtypeStruct((STEPS, 1, 1, width), F32),
            jax.ShapeDtypeStruct((beams, slots, HEAD), BF16),
            jax.ShapeDtypeStruct((beams, slots, HEAD), BF16),
        ),
        in_specs=[hbm] * 15,
        out_specs=(vmem, hbm, hbm),
        scratch_shapes=scratch,
        compiler_params=pltpu.CompilerParams(
            collective_id=0, has_side_effects=True, vmem_limit_bytes=63 * 1024 * 1024
        ),
    )(
        hidden_in.reshape(STEPS, width),
        pre_gain,
        post_gain,
        freq,
        perm,
        w_query,
        key_projection_weight,
        value_projection_weight,
        w_out,
        prompt_rotated_keys,
        prompt_value_rows,
        keys_in,
        values_in,
        parents,
        lengths,
    )
    hidden_out, keys_out, values_out = pl.pallas_call(
        place_kernel,
        out_shape=(
            jax.ShapeDtypeStruct((STEPS, 1, 1, width), F32),
            jax.ShapeDtypeStruct((beams, slots, HEAD), BF16),
            jax.ShapeDtypeStruct((beams, slots, HEAD), BF16),
        ),
        in_specs=[hbm] * 3,
        out_specs=(hbm, hbm, hbm),
        scratch_shapes=[
            V((STEPS, 1, 1, width), F32),
            V((beams, slots, HEAD), BF16),
            V((beams, slots, HEAD), BF16),
            D((3,)),
            D((3,)),
        ],
        compiler_params=pltpu.CompilerParams(vmem_limit_bytes=63 * 1024 * 1024),
    )(hidden, keys_new, values_new)
    return (
        hidden_out,
        keys_out.reshape(1, beams, slots, HEAD),
        values_out.reshape(1, beams, slots, HEAD),
    )


def solution(mesh, dims=(2, 4, 2, 8)):
    placed = (
        P(None, "context", "sample", None),
        P(),
        P(),
        P("context", "sample"),
        P("context", "sample"),
        P("context", "sample"),
        P("sample", None),
        P("context", "sample"),
        P("context", "sample"),
        P("context", None, None, "sample"),
        P("context", None, None, "sample"),
        P(None, "context", None),
        P(),
    )
    return jax.shard_map(
        functools.partial(body, dims),
        mesh=mesh,
        in_specs=placed,
        out_specs=(
            P(None, "context", "sample", None),
            P("context", None, None, "sample"),
            P("context", None, None, "sample"),
        ),
        check_vma=False,
    )
```
